32 devices in a mesh: gy: 8 (over y, x, core), gz: 4 (over z).
Axes of the slice: x: 2, y: 2, z: 4, core: 2. Of those that a mesh axis runs over, the one named last changes fastest.
Arguments:
- carbon_input_volume: bfloat16 [32, 32, 16, 256], P(None, 'gy', 'gz'), may hold values from -6 to 6
- cotangent: bfloat16 [32, 32, 16, 256], P(None, 'gy', 'gz'), may hold values from -6 to 6
- spec_weight: float32 [2, 32, 32, 8, 32, 32], P(None, 'gy', 'gz'), may hold values from -12 to 12
- lin_weight: bfloat16 [32, 32], replicated, may hold values from -1 to 1
- conv_fine: bfloat16 [27, 32, 32], replicated, may hold values from -0.21875 to 0.21875
- bias_fine: float32 [32], replicated, may hold values from -3 to 3
- conv_coarse: bfloat16 [27, 32, 32], replicated, may hold values from -0.21875 to 0.21875
- bias_coarse: float32 [32], replicated, may hold values from -3 to 3
Outputs:
- predicted_plume_output: bfloat16 [32, 32, 16, 256], P(None, 'gy', 'gz')
- input_sensitivity: bfloat16 [32, 32, 16, 256], P(None, 'gy', 'gz')
- fourier_kernel_sensitivity: float32 [2, 32, 32, 8, 32, 32], P(None, 'gy', 'gz')
The draws below stay inside these ranges and needn't reach their ends.
All inputs are finite; a program needn't handle non-finite values.
Results may differ from the reference program's by a relative error of at most 0.015.
Values may be sent and summed in bfloat16 or wider, within the bound.
No kernel may reach another device: no remote copies, remote signals or barrier semaphores. Data moves between devices by JAX's collectives and lax.ppermute only.
A program may use at most 128 MiB of HBM per device.

```python
import math
import jax
import jax.numpy as jnp
from jax import lax

C = 32
NX = 256
MX = 32
MY = 32
MZ = 8
NY = 32
NZ = 16


def block_scale(rng, shape, pieces, least, largest):
    def one(dim, blocks):
        draws = jax.random.uniform(jax.random.fold_in(jax.random.fold_in(rng, 6), dim), (blocks,), jnp.float32, least / len(pieces), largest / len(pieces))
        return jnp.repeat(jnp.exp(draws), shape[dim] // blocks).reshape((-1,) + (1,) * (len(shape) - dim - 1))

    loudness = one(*pieces[0])
    for cut in pieces[1:]:
        loudness = loudness * one(*cut)
    return loudness


def noise(key, shape, scale, limit, split=(), held_as=jnp.bfloat16):
    values = jax.random.normal(key, shape, jnp.float32) * scale
    if len(split) > 0:
        values = block_scale(key, shape, split, -0.22, 0.18) * values
    return jnp.clip(values, min=-limit, max=limit).astype(held_as)


def setup_inputs(seed: int = 0) -> dict:
    arg_keys = jax.random.split(jax.random.key(seed), 9)
    carbon_input_volume = noise(arg_keys[0], (C, NY, NZ, NX), 1.0, 6.0, ((1, 8), (2, 4)))
    cotangent = noise(arg_keys[1], (C, NY, NZ, NX), 1.0, 6.0, ((1, 8), (2, 4)))
    spec_weight = noise(arg_keys[2], (2, MX, MY, MZ, C, C), 2.0, 12.0, ((1, 8), (2, 4)), jnp.float32)
    lin_weight = noise(arg_keys[3], (C, C), C ** -0.5, 1.0)
    conv_fine = noise(arg_keys[4], (27, C, C), (27 * C) ** -0.5, 0.21875)
    bias_fine = noise(arg_keys[5], (C,), 0.5, 3.0, (), jnp.float32)
    conv_coarse = noise(arg_keys[6], (27, C, C), (27 * C) ** -0.5, 0.21875)
    bias_coarse = noise(arg_keys[7], (C,), 0.5, 3.0, (), jnp.float32)
    return {"carbon_input_volume": carbon_input_volume, "cotangent": cotangent, "spec_weight": spec_weight, "lin_weight": lin_weight, "conv_fine": conv_fine, "bias_fine": bias_fine, "conv_coarse": conv_coarse, "bias_coarse": bias_coarse}


highest = lax.Precision.HIGHEST
root_coef = math.sqrt(2.0 / math.pi)

def kept_freq(retained_mode_number, domain_length):
    position = jnp.arange(retained_mode_number, dtype=jnp.int32)
    return jnp.where(position < retained_mode_number // 2, position, domain_length - retained_mode_number + position).astype(jnp.int32)

def gelu_pair(pre_act):
    cube_term = pre_act * pre_act * pre_act
    tanh_result = jnp.tanh(root_coef * (pre_act + 0.044715 * cube_term))
    activated_output = 0.5 * pre_act * (1.0 + tanh_result)
    gelu_slope = 0.5 * (1.0 + tanh_result) + 0.5 * pre_act * (1.0 - tanh_result * tanh_result) * root_coef * (1.0 + 3.0 * 0.044715 * pre_act * pre_act)
    return (activated_output, gelu_slope)

def averaging_voxels(source):
    channels, span_y, span_z, span_x = source.shape
    blocks = source.reshape(channels, span_y // 2, 2, span_z // 2, 2, span_x // 2, 2)
    return lax.optimization_barrier(jnp.mean(blocks, axis=(2, 4, 6)))

def block_total(source):
    channels, span_y, span_z, span_x = source.shape
    blocks = source.reshape(channels, span_y // 2, 2, span_z // 2, 2, span_x // 2, 2)
    return lax.optimization_barrier(jnp.sum(blocks, axis=(2, 4, 6)))

def upsample(source):
    channels, span_y, span_z, span_x = source.shape
    spread = jnp.broadcast_to(source[:, :, None, :, None, :, None], (channels, span_y, 2, span_z, 2, span_x, 2))
    return spread.reshape(channels, 2 * span_y, 2 * span_z, 2 * span_x)

def kernel_full(kernel):
    return jnp.transpose(kernel.reshape(3, 3, 3, kernel.shape[1], kernel.shape[2]), (3, 4, 0, 1, 2))

def convolve(source, kernel):
    result = lax.conv_general_dilated(source[None].astype(jnp.float32), kernel_full(kernel).astype(jnp.float32), (1, 1, 1), [(1, 1), (1, 1), (1, 1)], dimension_numbers=('NCDHW', 'OIDHW', 'NCDHW'), precision=highest)
    return result[0]

def convolve_adjoint(source, kernel):
    flipped = jnp.transpose(kernel_full(kernel), (1, 0, 2, 3, 4))[:, :, ::-1, ::-1, ::-1]
    result = lax.conv_general_dilated(source[None].astype(jnp.float32), flipped.astype(jnp.float32), (1, 1, 1), [(1, 1), (1, 1), (1, 1)], dimension_numbers=('NCDHW', 'OIDHW', 'NCDHW'), precision=highest)
    return result[0]

def spectral(source, weights):
    freq_x = kept_freq(MX, NX)
    freq_y = kept_freq(MY, NY)
    freqs_z = jnp.arange(MZ, dtype=jnp.int32)

    def single_sample_apply(channel):
        whole_grid = jnp.fft.rfftn(jnp.transpose(channel, (0, 2, 1)), norm='ortho')
        return whole_grid[freq_y][:, freq_x][:, :, :MZ]
    spectrum = lax.map(single_sample_apply, source)
    complex_weight = weights[0] + 1j * weights[1]
    mixed_modes = jnp.einsum('xykoi,iyxk->oyxk', complex_weight, spectrum, precision=highest)

    def inverse_one(mode_vals):
        whole_grid = jnp.zeros((NY, NX, NZ // 2 + 1), mode_vals.dtype)
        whole_grid = whole_grid.at[freq_y[:, None, None], freq_x[None, :, None], freqs_z[None, None, :]].set(mode_vals)
        return jnp.transpose(jnp.fft.irfftn(whole_grid, s=(NY, NX, NZ), norm='ortho'), (0, 2, 1))
    return lax.map(inverse_one, mixed_modes)

def reference(carbon_input_volume, cotangent, spec_weight, lin_weight, conv_fine, bias_fine, conv_coarse, bias_coarse):
    source = carbon_input_volume.astype(jnp.float32)
    spectral_out, spectral_back = jax.vjp(spectral, source, spec_weight)
    linear_out = jnp.einsum('oc,cyzx->oyzx', lin_weight.astype(jnp.float32), source, precision=highest)
    fine_act = jnp.maximum(convolve(carbon_input_volume, conv_fine) + bias_fine[:, None, None, None], 0.0).astype(jnp.bfloat16)
    pooled = averaging_voxels(fine_act.astype(jnp.float32)).astype(jnp.bfloat16)
    coarse = jnp.maximum(convolve(pooled, conv_coarse) + bias_coarse[:, None, None, None], 0.0).astype(jnp.bfloat16)
    pre_act = spectral_out + linear_out + fine_act.astype(jnp.float32) + upsample(coarse.astype(jnp.float32))
    activated_output, gelu_slope = gelu_pair(pre_act)
    predicted_plume_output = activated_output.astype(jnp.bfloat16)
    grad_pre = cotangent.astype(jnp.float32) * gelu_slope
    grad_spectral, fourier_kernel_sensitivity = spectral_back(grad_pre)
    grad_round = grad_pre.astype(jnp.bfloat16)
    grad_linear = jnp.einsum('oc,oyzx->cyzx', lin_weight.astype(jnp.float32), grad_round.astype(jnp.float32), precision=highest)
    grad_coarse = jnp.where(coarse > 0, block_total(grad_pre), 0.0).astype(jnp.bfloat16)
    grad_pooled = convolve_adjoint(grad_coarse, conv_coarse)
    grad_fine = jnp.where(fine_act > 0, grad_pre + 0.125 * upsample(grad_pooled), 0.0).astype(jnp.bfloat16)
    grad_conv = convolve_adjoint(grad_fine, conv_fine)
    input_sensitivity = (grad_spectral + grad_linear + grad_conv).astype(jnp.bfloat16)
    return (predicted_plume_output, input_sensitivity, fourier_kernel_sensitivity)
```

```python
import math

import jax
import jax.numpy as jnp
import ml_dtypes
import numpy as np
from jax import lax
from jax.experimental import pallas as pl
from jax.experimental.pallas import tpu as pltpu
from jax.sharding import PartitionSpec as P

MX = 32
MY = 32
MZ = 8
CH = 32
BOTH = ("gy", "gz")

f32 = jnp.float32
bf16 = jnp.bfloat16
root_coef = math.sqrt(2.0 / math.pi)
NN = (((1,), (0,)), ((), ()))
NT = (((1,), (1,)), ((), ()))
TN = (((0,), (0,)), ((), ()))


def dot(a, b, form=NN):
    return lax.dot_general(a, b, form, preferred_element_type=f32)


def halves(value):
    high = value.astype(bf16)
    return high, (value - high.astype(f32)).astype(bf16)


def iota(shape, dim):
    return lax.broadcasted_iota(jnp.int32, shape, dim)


def call(kernel, outs, scratch=(), grid=None, in_specs=None, out_specs=None, flops=0):
    extra = {}
    if grid is not None:
        extra = dict(grid=grid, in_specs=in_specs, out_specs=out_specs)
    return pl.pallas_call(
        kernel,
        out_shape=outs,
        scratch_shapes=list(scratch),
        compiler_params=pltpu.CompilerParams(vmem_limit_bytes=56 << 20),
        cost_estimate=pl.CostEstimate(flops=flops, bytes_accessed=1 << 20, transcendentals=0),
        **extra,
    )


def kept(count, length):
    position = np.arange(count)
    return np.where(position < count // 2, position, length - count + position)


def split_np(table):
    high = table.astype(ml_dtypes.bfloat16)
    return high, (table - high.astype(np.float64)).astype(ml_dtypes.bfloat16)


def x_tables(cells_x, blocks):
    local = MX // blocks
    freqs = kept(MX, cells_x).reshape(blocks, local).T
    angles = 2.0 * np.pi * ((freqs[:, :, None] * np.arange(cells_x)) % cells_x) / cells_x
    table = np.stack([np.cos(angles), -np.sin(angles)], axis=2).reshape(2 * MX, cells_x)
    return np.concatenate(split_np(table), axis=0)


def x_back_table(cells_x, gy, gz):
    local = MX // gy
    freqs = kept(MX, cells_x).reshape(gy, local).T
    angles = 2.0 * np.pi * ((freqs[:, :, None] * np.arange(cells_x)) % cells_x) / cells_x
    table = np.stack([np.cos(angles), -np.sin(angles)], axis=2)
    table = np.broadcast_to(table[:, :, None], (local, gy, gz, 2, cells_x))
    return np.concatenate(split_np(table.reshape(-1, cells_x)), axis=0)


def yz_angles(xp, freqs_y, gy, gz, rows_y, rows_z):
    span_y, span_z = gy * rows_y, gz * rows_z
    phase_y = (freqs_y[:, None] * xp.arange(span_y)[None]) % span_y
    phase_z = (xp.arange(MZ)[:, None] * xp.arange(span_z)[None]) % span_z
    phase_y = phase_y.reshape(-1, 1, gy, 1, rows_y, 1)
    phase_z = phase_z.reshape(1, MZ, 1, gz, 1, rows_z)
    turn = (phase_y * span_z + phase_z * span_y) % (span_y * span_z)
    return turn.reshape(turn.shape[0] * MZ, gy * gz, rows_y * rows_z)


def yz_table(xp, freqs_y, gy, gz, rows_y, rows_z):
    cells = gy * gz * rows_y * rows_z
    turn = yz_angles(xp, freqs_y, gy, gz, rows_y, rows_z)
    angles = 2.0 * math.pi / cells * turn
    cosine, sine = xp.cos(angles), xp.sin(angles)
    table = xp.stack([xp.stack([cosine, sine], 2), xp.stack([-sine, cosine], 2)], 0)
    return table.reshape(2 * turn.shape[0], -1)


def mode_tables(gy, gz, rows_y, rows_z, scale):
    local = MY // gz
    cells = gy * gz * rows_y * rows_z
    freqs = kept(MY, gy * rows_y).reshape(gz, local)
    where = lax.axis_index("gz")
    if gz * 2 * local * MZ * 2 * cells <= 1 << 20:
        there, back = [], []
        for block in range(gz):
            high, low = split_np(scale * yz_table(np, freqs[block], gy, gz, rows_y, rows_z))
            there.append(np.concatenate([high, low], 0))
            back.append(np.concatenate([high.T, low.T], 1))
        pick = lambda tables: lax.dynamic_index_in_dim(
            jnp.asarray(np.stack(tables)), where, keepdims=False
        )
        return pick(there), pick(back)
    mine = lax.dynamic_index_in_dim(jnp.asarray(freqs, jnp.int32), where, keepdims=False)
    high, low = halves(scale * yz_table(jnp, mine, gy, gz, rows_y, rows_z).astype(f32))
    return jnp.concatenate([high, low], 0), jnp.concatenate([high.T, low.T], 1)


def put_x_modes(product, local, blocks, copies, cells, scratch, send_ref):
    rows = 2 * blocks
    for cell in range(cells):
        piece = product[:, cell * CH : (cell + 1) * CH]
        value = jnp.concatenate([piece[k * rows : (k + 1) * rows] for k in range(local)], axis=1)
        scratch[pl.ds(cell, rows, stride=cells), :] = value
    for block in range(blocks):
        value = scratch[block * 2 * cells : (block + 1) * 2 * cells].astype(bf16)
        for copy in range(copies):
            send_ref[block * copies + copy] = value


def spread_kernel(local, blocks, copies, cells, u_ref, table_ref, send_ref, scratch):
    both = dot(table_ref[...], u_ref[...].reshape(cells * CH, -1), NT)
    product = both[: 2 * MX] + both[2 * MX :]
    put_x_modes(product, local, blocks, copies, cells, scratch, send_ref)


def mode_values(rec_ref, there_ref, rows):
    both = dot(there_ref[...], rec_ref[...].reshape(-1, rec_ref.shape[2]))
    return both[:rows] + both[rows:]


def put_back(values, back_ref, send_ref):
    high, low = halves(values)
    rows = values.shape[0]
    result = dot(back_ref[...], jnp.concatenate([high, high], 0))
    result = result + dot(back_ref[:, :rows], low)
    send_ref[...] = result.astype(bf16).reshape(send_ref.shape)


def kz_weight(shape):
    return jnp.where(iota(shape, 0) % MZ == 0, 1.0, 2.0).astype(f32)


def same_mode(rows, lanes):
    return (iota((rows, lanes), 0) % MZ) == ((iota((rows, lanes), 1) // CH) % MZ)


def mix_kernel(local, rec_ref, there_ref, high_ref, low_ref, back_ref, v_ref, send_ref):
    rows = there_ref.shape[0] // 2
    modes = rows // 2
    wide = local * CH
    v = mode_values(rec_ref, there_ref, rows)
    v_ref[...] = v
    real, imag = v[:modes], v[modes:]
    pair = (
        jnp.concatenate([real, -imag], 1),
        jnp.concatenate([imag, real], 1),
    )
    lane_k = (iota((MZ, 2 * wide), 1) // CH) % local
    size = MZ * CH
    diag = same_mode(2 * MZ * local, size)
    placed = [[[None] * (modes // MZ) for _ in range(local)] for _ in range(2)]
    for g in range(modes // MZ):
        pieces = []
        for k in range(local):
            for part in range(2):
                piece = pair[part][g * MZ : (g + 1) * MZ]
                pieces.append(jnp.where(lane_k == k, piece, 0.0))
        left_high, left_low = halves(jnp.concatenate(pieces, 0))
        w_high = high_ref[g * size : (g + 1) * size]
        w_low = low_ref[g * size : (g + 1) * size]
        count = left_high.shape[0]
        both = dot(jnp.concatenate([left_high, left_low], 0), w_high, NT)
        value = both[:count] + both[count:] + dot(left_high, w_low, NT)
        value = jnp.where(diag, value, 0.0)
        for k in range(local):
            for part in range(2):
                at = (2 * k + part) * MZ
                placed[part][k][g] = value[at : at + MZ]
    columns = [jnp.concatenate(placed[0][k] + placed[1][k], 0) for k in range(local)]
    all_values = jnp.concatenate(columns, 1)
    shape = (local * size, wide)
    fold = (iota(shape, 0) // size == iota(shape, 1) // CH) & (
        iota(shape, 0) % CH == iota(shape, 1) % CH
    )
    fold = fold.astype(bf16)
    high, low = halves(all_values)
    mixed = dot(high, fold) + dot(low, fold)
    put_back(mixed * kz_weight(mixed.shape), back_ref, send_ref)


def adjoint_kernel(local, rec_ref, there_ref, high_ref, back_ref, d_ref, send_ref):
    rows = there_ref.shape[0] // 2
    modes = rows // 2
    wide = local * CH
    size = MZ * CH
    d = mode_values(rec_ref, there_ref, rows)
    d = d * kz_weight(d.shape)
    d_ref[...] = d
    shape = (wide, local * size)
    rep = (iota(shape, 1) // size == iota(shape, 0) // CH) & (
        iota(shape, 1) % CH == iota(shape, 0) % CH
    )
    rep = rep.astype(bf16)
    high, low = halves(d)
    spread = dot(high, rep) + dot(low, rep)
    spread = jnp.where(same_mode(rows, local * size), spread, 0.0)
    lane_k = (iota((2 * MZ, 2 * wide), 1) // CH) % local
    parts = ([], [])
    for g in range(modes // MZ):
        pieces = []
        for k in range(local):
            for part in range(2):
                at = part * modes + g * MZ
                pieces.append(spread[at : at + MZ, k * size : (k + 1) * size])
        left_high, left_low = halves(jnp.concatenate(pieces, 0))
        count = left_high.shape[0]
        both = dot(
            jnp.concatenate([left_high, left_low], 0), high_ref[g * size : (g + 1) * size]
        )
        value = both[:count] + both[count:]
        total = None
        for k in range(local):
            piece = jnp.where(lane_k == k, value[2 * k * MZ : 2 * (k + 1) * MZ], 0.0)
            total = piece if total is None else total + piece
        parts[0].append(total[:MZ])
        parts[1].append(total[MZ:])
    real = jnp.concatenate(parts[0], 0)
    imag = jnp.concatenate(parts[1], 0)
    back = jnp.concatenate(
        [real[:, :wide] + imag[:, wide:], imag[:, :wide] - real[:, wide:]], 0
    )
    put_back(back, back_ref, send_ref)


def pack_kernel(local, w_ref, high_ref, low_ref):
    pieces = [w_ref[part, k] for part in range(2) for k in range(local)]
    high, low = halves(jnp.concatenate(pieces, 1))
    high_ref[...] = high
    low_ref[...] = low


def weight_grad_kernel(d_ref, v_ref, out_ref):
    step = pl.program_id(0)
    rows, wide = d_ref.shape
    modes = rows // 2
    size = MZ * CH
    shape = (wide, size)
    rep = (iota(shape, 0) == step * CH + iota(shape, 1) % CH).astype(bf16)
    shape = (wide, CH)
    sel = (iota(shape, 0) == step * CH + iota(shape, 1)).astype(bf16)
    keep = same_mode(rows, size)
    d_high, d_low = halves(d_ref[...])
    d_high = jnp.where(keep, dot(d_high, rep), 0.0)
    d_low = jnp.where(keep, dot(d_low, rep), 0.0)
    v_high, v_low = halves(v_ref[...])
    v_high, v_low = dot(v_high, sel), dot(v_low, sel)
    for g in range(modes // MZ):
        real = slice(g * MZ, (g + 1) * MZ)
        imag = slice(modes + g * MZ, modes + (g + 1) * MZ)
        left = jnp.concatenate(
            [d_high[real], d_high[imag], d_low[real], d_low[imag], d_high[real], d_high[imag]], 0
        ).astype(bf16)
        for part in range(2):
            rights = []
            for v in (v_high, v_high, v_low):
                rights += [v[real], v[imag]] if part == 0 else [-v[imag], v[real]]
            right = jnp.concatenate(rights, 0).astype(bf16)
            out_ref[part, 0, g * size : (g + 1) * size, :] = dot(left, right, TN)


def inverse_x(rec_ref, table_ref, local, cells, wide, left):
    wide[...] = rec_ref[...].reshape(-1, rec_ref.shape[2]).astype(f32)
    rows = wide.shape[0] // cells
    for cell in range(cells):
        turned = wide[pl.ds(cell, rows, stride=cells), :].T.astype(bf16)
        for k in range(local):
            left[cell * CH : (cell + 1) * CH, k * rows : (k + 1) * rows] = turned[
                k * CH : (k + 1) * CH
            ]
    depth = local * rows
    value = left[...]
    return dot(value, table_ref[:depth]) + dot(value, table_ref[depth:])


def gelu_pair(pre_act):
    cube_term = pre_act * pre_act * pre_act
    tanh_result = jnp.tanh(root_coef * (pre_act + 0.044715 * cube_term))
    activated_output = 0.5 * pre_act * (1.0 + tanh_result)
    gelu_slope = 0.5 * (1.0 + tanh_result) + 0.5 * pre_act * (
        1.0 - tanh_result * tanh_result
    ) * root_coef * (1.0 + 3.0 * 0.044715 * pre_act * pre_act)
    return (activated_output, gelu_slope)


def middle_kernel(
    local,
    blocks,
    copies,
    cells,
    rec_ref,
    back_ref,
    base_ref,
    cot_ref,
    table_ref,
    out_ref,
    grad_ref,
    send_ref,
    wide,
    left,
    scratch,
):
    pre_act = inverse_x(rec_ref, back_ref, local, cells, wide, left)
    pre_act = pre_act + base_ref[...].reshape(pre_act.shape)
    activated, slope = gelu_pair(pre_act)
    out_ref[...] = activated.astype(bf16).reshape(out_ref.shape)
    grad = cot_ref[...].astype(f32).reshape(pre_act.shape) * slope
    grad_ref[...] = grad.reshape(grad_ref.shape)
    high, low = halves(grad)
    both = dot(table_ref[...], high, NT)
    product = both[: 2 * MX] + both[2 * MX :] + dot(table_ref[: 2 * MX], low, NT)
    put_x_modes(product, local, blocks, copies, cells, scratch, send_ref)


def last_kernel(local, cells, rec_ref, back_ref, base_ref, out_ref, wide, left):
    value = inverse_x(rec_ref, back_ref, local, cells, wide, left)
    value = value + base_ref[...].reshape(value.shape)
    out_ref[...] = value.astype(bf16).reshape(out_ref.shape)


def bands_kernel(adjoint, k_ref, out_ref):
    zero = jnp.zeros((CH, CH), f32)
    for a in range(3):
        for e in range(3):
            taps = []
            for b in range(3):
                if adjoint:
                    tap = k_ref[9 * (2 - a) + 3 * (2 - b) + 2 - e].astype(f32).T
                else:
                    tap = k_ref[9 * a + 3 * b + e].astype(f32)
                taps.append(tap)
            for z in range(4):
                row = jnp.concatenate([zero] * z + taps + [zero] * (3 - z), 1)
                at = (e * 4 + z) * CH
                out_ref[a, at : at + CH, :] = row.astype(bf16)


def x_sum(low, same, high):
    span = same.shape[1]
    lane = iota(same.shape, 1)
    before = jnp.where(lane == 0, 0.0, pltpu.roll(low, 1, axis=1))
    after = jnp.where(lane == span - 1, 0.0, pltpu.roll(high, span - 1, axis=1))
    return same + before + after


def band_conv(bands_ref, rows_of, out_z=4):
    deep = (out_z + 2) * CH
    high = out_z * CH
    parts = []
    for e in range(3):
        total = None
        for a in range(3):
            left = bands_ref[a, e * 4 * CH : e * 4 * CH + high, :deep]
            value = dot(left, rows_of(a))
            total = value if total is None else total + value
        parts.append(total)
    return x_sum(*parts)


def pool_matrix(span):
    shape = (span, span // 2)
    return (iota(shape, 0) // 2 == iota(shape, 1)).astype(bf16)


def up_matrix(span):
    shape = (span // 2, span)
    return (iota(shape, 1) // 2 == iota(shape, 0)).astype(bf16)


def forward_conv_kernel(
    edge_ref,
    u_ref,
    zlo_ref,
    zhi_ref,
    ylo_ref,
    yhi_ref,
    lin_ref,
    fine_bands_ref,
    bias_fine_ref,
    coarse_bands_ref,
    bias_coarse_ref,
    base_ref,
    fine_ref,
    coarse_ref,
    grid,
    pooled,
):
    span = u_ref.shape[3]
    for y in range(4):
        for z in range(3):
            grid[y + 3, z * CH : (z + 1) * CH] = zlo_ref[y, z]
            grid[y + 3, (z + 7) * CH : (z + 8) * CH] = zhi_ref[y, z]
        for z in range(4):
            grid[y + 3, (z + 3) * CH : (z + 4) * CH] = u_ref[y, z]
    for y in range(3):
        for z in range(10):
            grid[y, z * CH : (z + 1) * CH] = ylo_ref[y, z]
            grid[y + 7, z * CH : (z + 1) * CH] = yhi_ref[y, z]
    bias = jnp.concatenate([bias_fine_ref[...]] * 4, 0)
    half = 4 * CH
    row_z = iota((half, span), 0) // CH
    pool = pool_matrix(span)
    pools = []
    for y in range(8):
        sums = []
        if y < 2:
            y_in = edge_ref[0] == 0
        elif y >= 6:
            y_in = edge_ref[1] == 0
        else:
            y_in = None
        for h in range(2):
            at = h * half
            value = band_conv(fine_bands_ref, lambda a: grid[y + a, at : at + 6 * CH, :])
            value = jnp.maximum(value + bias, 0.0)
            if h == 0:
                inside = (row_z >= 2) | (edge_ref[2] == 0)
            else:
                inside = (row_z < 2) | (edge_ref[3] == 0)
            if y_in is not None:
                inside = inside & y_in
            value = jnp.where(inside, value, 0.0).astype(bf16)
            fine_ref[y, at : at + half, :] = value
            sums.append(dot(value, pool))
        pools.append(jnp.concatenate(sums, 0))
    for yc in range(4):
        both = pools[2 * yc] + pools[2 * yc + 1]
        for zc in range(4):
            at = 2 * zc * CH
            value = both[at : at + CH] + both[at + CH : at + 2 * CH]
            pooled[yc, zc * CH : (zc + 1) * CH, :] = (0.125 * value).astype(bf16)
    up = up_matrix(span)
    bias = jnp.concatenate([bias_coarse_ref[...]] * 2, 0)
    for yc in range(2):
        value = band_conv(coarse_bands_ref, lambda a: pooled[yc + a], 2)
        value = jnp.maximum(value + bias, 0.0).astype(bf16)
        lifted = dot(value, up)
        for zc in range(2):
            coarse_ref[yc, zc] = value[zc * CH : (zc + 1) * CH]
            for y in (2 * yc, 2 * yc + 1):
                for z in (2 * zc, 2 * zc + 1):
                    total = dot(lin_ref[...], u_ref[y, z])
                    total = total + fine_ref[y + 2, (z + 2) * CH : (z + 3) * CH, :].astype(f32)
                    base_ref[y, z] = total + lifted[zc * CH : (zc + 1) * CH]


def block_kernel(grad_ref, coarse_ref, low_ref, high_ref):
    span = grad_ref.shape[3]
    pool = pool_matrix(span)
    for y in range(4):
        low_ref[y] = grad_ref[y, 0].astype(bf16)
        high_ref[y] = grad_ref[y, 3].astype(bf16)
    for yc in range(2):
        sums = []
        for zc in range(2):
            at = (2 * yc, 2 * zc)
            sums.append(
                grad_ref[at[0], at[1]]
                + grad_ref[at[0], at[1] + 1]
                + grad_ref[at[0] + 1, at[1]]
                + grad_ref[at[0] + 1, at[1] + 1]
            )
        high, low = halves(jnp.concatenate(sums, 0))
        total = dot(high, pool) + dot(low, pool)
        pieces = []
        for zc in range(2):
            value = total[zc * CH : (zc + 1) * CH]
            pieces.append(jnp.where(coarse_ref[yc, zc].astype(f32) > 0, value, 0.0))
        value = jnp.concatenate(pieces, 1).astype(bf16)
        low_ref[4 + yc] = value
        high_ref[4 + yc] = value


def backward_conv_kernel(
    grad_ref,
    own_ref,
    zlo_ref,
    zhi_ref,
    ylo_ref,
    yhi_ref,
    fine_ref,
    lin_ref,
    fine_bands_ref,
    coarse_bands_ref,
    base_ref,
    coarse_grid,
    fine_grid,
):
    span = grad_ref.shape[3]
    half = span // 2

    def place(yc, pair, value):
        for zc in range(2):
            at = (2 * pair + zc) * CH
            coarse_grid[yc, at : at + CH, :] = value[:, zc * half : (zc + 1) * half]

    for yc in range(2):
        place(2 + yc, 0, zlo_ref[4 + yc])
        place(2 + yc, 1, own_ref[4 + yc])
        place(2 + yc, 2, zhi_ref[4 + yc])
        for pair in range(3):
            place(yc, pair, ylo_ref[6 + 3 * yc + pair])
            place(4 + yc, pair, yhi_ref[6 + 3 * yc + pair])
    up = up_matrix(span)
    for yc in range(4):
        pooled = 0.125 * band_conv(coarse_bands_ref, lambda a: coarse_grid[yc + a])
        high, low = halves(pooled)
        lifted = dot(high, up) + dot(low, up)
        for y in range(6):
            if (y + 1) // 2 != yc:
                continue
            for z in range(6):
                zc = (z + 1) // 2
                if 1 <= y <= 4 and 1 <= z <= 4:
                    value = grad_ref[y - 1, z - 1]
                elif 1 <= y <= 4:
                    value = (zlo_ref if z == 0 else zhi_ref)[y - 1].astype(f32)
                else:
                    value = (ylo_ref if y == 0 else yhi_ref)[z].astype(f32)
                value = value + lifted[zc * CH : (zc + 1) * CH]
                fine = fine_ref[y + 1, (z + 1) * CH : (z + 2) * CH, :].astype(f32)
                value = jnp.where(fine > 0, value, 0.0).astype(bf16)
                fine_grid[y, z * CH : (z + 1) * CH, :] = value
    for y in range(4):
        value = band_conv(fine_bands_ref, lambda a: fine_grid[y + a])
        for z in range(4):
            linear = dot(lin_ref[...], grad_ref[y, z].astype(bf16), TN)
            base_ref[y, z] = value[z * CH : (z + 1) * CH] + linear


def shift(block, axis, step):
    count = lax.axis_size(axis)
    pairs = [(i, i + step) for i in range(count) if 0 <= i + step < count]
    return lax.ppermute(block, axis, pairs)


def exchange(block):
    return lax.all_to_all(block, BOTH, split_axis=0, concat_axis=0, tiled=True)


def shards(
    carbon_input_volume,
    cotangent,
    spec_weight,
    lin_weight,
    conv_fine,
    bias_fine,
    conv_coarse,
    bias_coarse,
):
    channels, rows_y, rows_z, span = carbon_input_volume.shape
    gy, gz = lax.axis_size("gy"), lax.axis_size("gz")
    devices = gy * gz
    cells = rows_y * rows_z
    local = MX // gy
    modes = (MY // gz) * MZ
    wide = local * CH
    scale = 1.0 / math.sqrt(span * cells * devices)
    there, back = mode_tables(gy, gz, rows_y, rows_z, scale)
    forward_x = jnp.asarray(x_tables(span, gy))
    inverse_table = jnp.asarray(x_back_table(span, gy, gz))

    def struct(shape, kind=f32):
        return jax.ShapeDtypeStruct(shape, kind)

    chunk = struct((devices, 2 * cells, wide), bf16)
    field = struct((rows_y, rows_z, CH, span))
    x_scratch = pltpu.VMEM((2 * gy * cells, wide), f32)
    wide_scratch = pltpu.VMEM((devices * 2 * cells, wide), f32)
    left_scratch = pltpu.VMEM((cells * CH, local * devices * 2), bf16)
    mode_field = struct((2 * modes, wide))

    u = jnp.transpose(carbon_input_volume, (1, 2, 0, 3))
    with jax.named_scope("spread_input"):
        send = call(
            lambda *refs: spread_kernel(local, gy, gz, cells, *refs),
            chunk,
            [x_scratch],
            flops=1 << 24,
        )(u, forward_x)
    received = exchange(send)

    zlo = shift(u[:, rows_z - 3 :], "gz", 1)
    zhi = shift(u[:, :3], "gz", -1)
    wide_z = jnp.concatenate([zlo, u, zhi], 1)
    ylo = shift(wide_z[rows_y - 3 :], "gy", 1)
    yhi = shift(wide_z[:3], "gy", -1)

    with jax.named_scope("pack_weights"):
        rows = modes * CH
        weights = spec_weight.reshape(2, local, rows, CH)
        step = MZ * CH
        w_high, w_low = call(
            lambda *refs: pack_kernel(local, *refs),
            [struct((rows, 2 * wide), bf16)] * 2,
            grid=(rows // step,),
            in_specs=[pl.BlockSpec((2, local, step, CH), lambda i: (0, 0, i, 0))],
            out_specs=[pl.BlockSpec((step, 2 * wide), lambda i: (i, 0))] * 2,
        )(weights)
    bands = struct((3, 12 * CH, 6 * CH), bf16)
    with jax.named_scope("bands"):
        make = lambda adjoint: call(lambda *refs: bands_kernel(adjoint, *refs), bands)
        fine_bands, coarse_bands = make(False)(conv_fine), make(False)(conv_coarse)
        fine_adjoint, coarse_adjoint = make(True)(conv_fine), make(True)(conv_coarse)

    with jax.named_scope("mix"):
        v, send = call(
            lambda *refs: mix_kernel(local, *refs), [mode_field, chunk], flops=1 << 26
        )(received, there, w_high, w_low, back)
    received = exchange(send)

    edge = jnp.stack(
        [
            lax.axis_index("gy") == 0,
            lax.axis_index("gy") == gy - 1,
            lax.axis_index("gz") == 0,
            lax.axis_index("gz") == gz - 1,
        ]
    ).astype(jnp.int32)
    vmem = pl.BlockSpec(memory_space=pltpu.VMEM)
    with jax.named_scope("forward_convs"):
        base, fine, coarse = pl.pallas_call(
            forward_conv_kernel,
            in_specs=[pl.BlockSpec(memory_space=pltpu.SMEM)] + [vmem] * 10,
            out_shape=[
                field,
                struct((8, 8 * CH, span), bf16),
                struct((2, 2, CH, span // 2), bf16),
            ],
            scratch_shapes=[
                pltpu.VMEM((10, 10 * CH, span), bf16),
                pltpu.VMEM((4, 4 * CH, span // 2), bf16),
            ],
            compiler_params=pltpu.CompilerParams(vmem_limit_bytes=56 << 20),
            cost_estimate=pl.CostEstimate(
                flops=1 << 30, bytes_accessed=1 << 22, transcendentals=0
            ),
        )(
            edge,
            u,
            zlo,
            zhi,
            ylo,
            yhi,
            lin_weight,
            fine_bands,
            bias_fine[:, None],
            coarse_bands,
            bias_coarse[:, None],
        )

    cot = jnp.transpose(cotangent, (1, 2, 0, 3))
    with jax.named_scope("middle"):
        activated, grad, send = call(
            lambda *refs: middle_kernel(local, gy, gz, cells, *refs),
            [struct(field.shape, bf16), field, chunk],
            [wide_scratch, left_scratch, x_scratch],
            flops=1 << 26,
        )(received, inverse_table, base, cot, forward_x)
    received = exchange(send)
    predicted = jnp.transpose(activated, (2, 0, 1, 3))

    with jax.named_scope("blocks"):
        message = struct((6, CH, span), bf16)
        to_low, to_high = call(block_kernel, [message, message])(grad, coarse)
    zlo = shift(to_high, "gz", 1)
    zhi = shift(to_low, "gz", -1)
    own = grad.astype(bf16)

    def y_message(y):
        return jnp.concatenate(
            [
                zlo[y : y + 1],
                own[y],
                zhi[y : y + 1],
                zlo[4:5],
                to_low[4:5],
                zhi[4:5],
                zlo[5:6],
                to_low[5:6],
                zhi[5:6],
            ],
            0,
        )

    ylo = shift(y_message(rows_y - 1), "gy", 1)
    yhi = shift(y_message(0), "gy", -1)

    with jax.named_scope("mix_adjoint"):
        d, send = call(
            lambda *refs: adjoint_kernel(local, *refs), [mode_field, chunk], flops=1 << 26
        )(received, there, w_high, back)
    received = exchange(send)

    with jax.named_scope("backward_convs"):
        base = call(
            backward_conv_kernel,
            field,
            [
                pltpu.VMEM((6, 6 * CH, span // 2), bf16),
                pltpu.VMEM((6, 6 * CH, span), bf16),
            ],
            flops=1 << 29,
        )(grad, to_low, zlo, zhi, ylo, yhi, fine, lin_weight, fine_adjoint, coarse_adjoint)

    with jax.named_scope("weight_grad"):
        full = pl.BlockSpec((2 * modes, wide), lambda i: (0, 0))
        weight_grad = call(
            weight_grad_kernel,
            struct((2, local, rows, CH)),
            grid=(local,),
            in_specs=[full, full],
            out_specs=pl.BlockSpec((2, 1, rows, CH), lambda i: (0, i, 0, 0)),
            flops=1 << 28,
        )(d, v)
    weight_grad = weight_grad.reshape(spec_weight.shape)

    with jax.named_scope("last"):
        total = call(
            lambda *refs: last_kernel(local, cells, *refs),
            struct(field.shape, bf16),
            [wide_scratch, left_scratch],
            flops=1 << 26,
        )(received, inverse_table, base)
    sensitivity = jnp.transpose(total, (2, 0, 1, 3))
    return (predicted, sensitivity, weight_grad)


def solution(mesh):
    field = P(None, "gy", "gz", None)
    modes = P(None, "gy", "gz", None, None, None)
    return jax.shard_map(
        shards,
        mesh=mesh,
        in_specs=(field, field, modes, P(), P(), P(), P(), P()),
        out_specs=(field, field, modes),
        check_vma=False,
    )
```

```python
import math

import jax
import jax.numpy as jnp
import ml_dtypes
import numpy as np
from jax import lax
from jax.experimental import pallas as pl
from jax.experimental.pallas import tpu as pltpu
from jax.sharding import PartitionSpec as P

MX = 32
MY = 32
MZ = 8
CH = 32
BOTH = ("gy", "gz")

f32 = jnp.float32
bf16 = jnp.bfloat16
root_coef = math.sqrt(2.0 / math.pi)
NN = (((1,), (0,)), ((), ()))
NT = (((1,), (1,)), ((), ()))
TN = (((0,), (0,)), ((), ()))


def dot(a, b, form=NN):
    return lax.dot_general(a, b, form, preferred_element_type=f32)


def halves(value):
    high = value.astype(bf16)
    return high, (value - high.astype(f32)).astype(bf16)


def iota(shape, dim):
    return lax.broadcasted_iota(jnp.int32, shape, dim)


IN_VMEM = pl.BlockSpec(memory_space=pltpu.VMEM)
IN_HBM = pl.BlockSpec(memory_space=pltpu.HBM)
ANYWHERE = pl.BlockSpec(memory_space=pl.ANY)


def struct(shape, kind=f32):
    return jax.ShapeDtypeStruct(shape, kind)


def run(kernel, ins, outs, limit, scratch=(), micros=1.0, copies=0, **grid):
    scratch = list(scratch)
    if copies:
        scratch.append(pltpu.SemaphoreType.DMA((copies,)))
    held = {id(IN_HBM): pltpu.HBM, id(IN_VMEM): pltpu.VMEM}

    def placed(spec, array):
        if id(spec) in held:
            return pltpu.with_memory_space_constraint(array, held[id(spec)])
        return array

    def shaped(spec, shape):
        if id(spec) in held:
            return held[id(spec)](shape.shape, shape.dtype)
        return shape

    return pl.pallas_call(
        kernel,
        in_specs=[spec for spec, _ in ins],
        out_specs=[spec for spec, _ in outs],
        out_shape=[shaped(spec, shape) for spec, shape in outs],
        scratch_shapes=scratch,
        compiler_params=pltpu.CompilerParams(vmem_limit_bytes=limit),
        cost_estimate=pl.CostEstimate(
            flops=int(micros * 1.1e9), bytes_accessed=1 << 16, transcendentals=0
        ),
        **grid,
    )(*[placed(spec, array) for spec, array in ins])


def begin(sem, first, *pairs):
    copies = [
        pltpu.make_async_copy(source, target, sem.at[first + i])
        for i, (source, target) in enumerate(pairs)
    ]
    for copy in copies:
        copy.start()
    return copies


def finish(*copies):
    for copy in copies:
        copy.wait()


def kept(count, length):
    position = np.arange(count)
    return np.where(position < count // 2, position, length - count + position)


def split_np(table):
    high = table.astype(ml_dtypes.bfloat16)
    return high, (table - high.astype(np.float64)).astype(ml_dtypes.bfloat16)


def x_tables(cells_x, blocks):
    local = MX // blocks
    freqs = kept(MX, cells_x).reshape(blocks, local).T
    angles = 2.0 * np.pi * ((freqs[:, :, None] * np.arange(cells_x)) % cells_x) / cells_x
    table = np.stack([np.cos(angles), -np.sin(angles)], axis=2).reshape(2 * MX, cells_x)
    return np.concatenate(split_np(table), axis=0)


def x_back_table(cells_x, gy, gz):
    local = MX // gy
    freqs = kept(MX, cells_x).reshape(gy, local).T
    angles = 2.0 * np.pi * ((freqs[:, :, None] * np.arange(cells_x)) % cells_x) / cells_x
    table = np.stack([np.cos(angles), -np.sin(angles)], axis=2)
    table = np.broadcast_to(table[:, :, None], (local, gy, gz, 2, cells_x))
    return np.concatenate(split_np(table.reshape(-1, cells_x)), axis=0)


def yz_angles(xp, freqs_y, gy, gz, rows_y, rows_z):
    span_y, span_z = gy * rows_y, gz * rows_z
    phase_y = (freqs_y[:, None] * xp.arange(span_y)[None]) % span_y
    phase_z = (xp.arange(MZ)[:, None] * xp.arange(span_z)[None]) % span_z
    phase_y = phase_y.reshape(-1, 1, gy, 1, rows_y, 1)
    phase_z = phase_z.reshape(1, MZ, 1, gz, 1, rows_z)
    turn = (phase_y * span_z + phase_z * span_y) % (span_y * span_z)
    return turn.reshape(turn.shape[0] * MZ, gy * gz, rows_y * rows_z)


def yz_table(xp, freqs_y, gy, gz, rows_y, rows_z):
    cells = gy * gz * rows_y * rows_z
    turn = yz_angles(xp, freqs_y, gy, gz, rows_y, rows_z)
    angles = 2.0 * math.pi / cells * turn
    cosine, sine = xp.cos(angles), xp.sin(angles)
    table = xp.stack([xp.stack([cosine, sine], 2), xp.stack([-sine, cosine], 2)], 0)
    return table.reshape(2 * turn.shape[0], -1)


def mode_tables(gy, gz, rows_y, rows_z, scale):
    local = MY // gz
    cells = gy * gz * rows_y * rows_z
    freqs = kept(MY, gy * rows_y).reshape(gz, local)
    if gz * 2 * local * MZ * 2 * cells <= 1 << 20:
        there, back = [], []
        for block in range(gz):
            high, low = split_np(scale * yz_table(np, freqs[block], gy, gz, rows_y, rows_z))
            there.append(np.concatenate([high, low], 0))
            back.append(np.concatenate([high.T, low.T], 1))
        return jnp.asarray(np.stack(there)), jnp.asarray(np.stack(back))
    where = lax.axis_index("gz")
    mine = lax.dynamic_index_in_dim(jnp.asarray(freqs, jnp.int32), where, keepdims=False)
    high, low = halves(scale * yz_table(jnp, mine, gy, gz, rows_y, rows_z).astype(f32))
    return jnp.concatenate([high, low], 0)[None], jnp.concatenate([high.T, low.T], 1)[None]


def put_x_modes(product, local, blocks, copies, cells, scratch, sent, send_ref, sem, first):
    rows = 2 * blocks
    for cell in range(cells):
        piece = product[:, cell * CH : (cell + 1) * CH]
        value = jnp.concatenate([piece[k * rows : (k + 1) * rows] for k in range(local)], axis=1)
        scratch[pl.ds(cell, rows, stride=cells), :] = value
    moves = []
    half = blocks // 2
    for block in range(blocks):
        value = scratch[block * 2 * cells : (block + 1) * 2 * cells].astype(bf16)
        for copy in range(copies):
            sent[block * copies + copy] = value
        if (block + 1) % half == 0:
            part = pl.ds((block + 1 - half) * copies, half * copies)
            moves += begin(sem, first + len(moves), (sent.at[part], send_ref.at[part]))
    return moves


def spread_kernel(
    local,
    blocks,
    copies,
    raw_ref,
    table_ref,
    u_ref,
    low_ref,
    high_ref,
    send_ref,
    raw,
    table,
    turned,
    scratch,
    sent,
    sem,
):
    load_raw, load_table = begin(sem, 0, (raw_ref, raw), (table_ref, table))
    finish(load_raw)
    u = jnp.transpose(raw[...], (1, 2, 0, 3))
    turned[...] = u
    store = begin(sem, 2, (turned, u_ref))
    low_ref[...] = u[:, :3]
    high_ref[...] = u[:, 1:]
    finish(load_table)
    cells = u.shape[0] * u.shape[1]
    both = dot(table[...], u.reshape(cells * CH, -1), NT)
    product = both[: 2 * MX] + both[2 * MX :]
    moves = put_x_modes(product, local, blocks, copies, cells, scratch, sent, send_ref, sem, 3)
    finish(*store, *moves)


def pick(tables_ref):
    if tables_ref.shape[0] == 1:
        return tables_ref.at[0]
    return tables_ref.at[lax.axis_index("gz")]


def mode_values(rec_ref, there, rows):
    both = dot(there[...], rec_ref[...].reshape(-1, rec_ref.shape[2]))
    return both[:rows] + both[rows:]


def put_back(values, back, sent, send_ref, sem, first):
    high, low = halves(values)
    twice = jnp.concatenate([high, high], 0)
    rows = values.shape[0]
    devices, depth, wide = sent.shape
    part = devices // 4
    moves = []
    for step in range(4):
        at = slice(step * part * depth, (step + 1) * part * depth)
        result = dot(back[at], twice) + dot(back[at, :rows], low)
        sent[step * part : (step + 1) * part] = result.astype(bf16).reshape(part, depth, wide)
        span = pl.ds(step * part, part)
        moves += begin(sem, first + step, (sent.at[span], send_ref.at[span]))
    finish(*moves)


def kz_weight(shape):
    return jnp.where(iota(shape, 0) % MZ == 0, 1.0, 2.0).astype(f32)


def same_mode(rows, lanes):
    return (iota((rows, lanes), 0) % MZ) == ((iota((rows, lanes), 1) // CH) % MZ)


def mix_kernel(
    local,
    rec_ref,
    there_ref,
    w_high_ref,
    w_low_ref,
    back_ref,
    v_ref,
    send_ref,
    there,
    high_ref,
    low_ref,
    back,
    kept_v,
    sent,
    sem,
):
    loads = begin(
        sem,
        0,
        (pick(there_ref), there),
        (w_high_ref, high_ref),
        (w_low_ref, low_ref),
        (pick(back_ref), back),
    )
    rows = there.shape[0] // 2
    modes = rows // 2
    wide = local * CH
    finish(loads[0])
    v = mode_values(rec_ref, there, rows)
    kept_v[...] = v
    store = begin(sem, 4, (kept_v, v_ref))
    finish(loads[1], loads[2])
    real, imag = v[:modes], v[modes:]
    pair = (
        jnp.concatenate([real, -imag], 1),
        jnp.concatenate([imag, real], 1),
    )
    lane_k = (iota((MZ, 2 * wide), 1) // CH) % local
    size = MZ * CH
    diag = same_mode(2 * MZ * local, size)
    placed = [[[None] * (modes // MZ) for _ in range(local)] for _ in range(2)]
    for g in range(modes // MZ):
        pieces = []
        for k in range(local):
            for part in range(2):
                piece = pair[part][g * MZ : (g + 1) * MZ]
                pieces.append(jnp.where(lane_k == k, piece, 0.0))
        left_high, left_low = halves(jnp.concatenate(pieces, 0))
        w_high = high_ref[g * size : (g + 1) * size]
        w_low = low_ref[g * size : (g + 1) * size]
        count = left_high.shape[0]
        both = dot(jnp.concatenate([left_high, left_low], 0), w_high, NT)
        value = both[:count] + both[count:] + dot(left_high, w_low, NT)
        value = jnp.where(diag, value, 0.0)
        for k in range(local):
            for part in range(2):
                at = (2 * k + part) * MZ
                placed[part][k][g] = value[at : at + MZ]
    columns = [jnp.concatenate(placed[0][k] + placed[1][k], 0) for k in range(local)]
    all_values = jnp.concatenate(columns, 1)
    shape = (local * size, wide)
    fold = (iota(shape, 0) // size == iota(shape, 1) // CH) & (
        iota(shape, 0) % CH == iota(shape, 1) % CH
    )
    fold = fold.astype(bf16)
    high, low = halves(all_values)
    mixed = dot(high, fold) + dot(low, fold)
    finish(loads[3])
    put_back(mixed * kz_weight(mixed.shape), back, sent, send_ref, sem, 5)
    finish(*store)


def adjoint_kernel(
    local,
    rec_ref,
    there_ref,
    w_high_ref,
    back_ref,
    d_ref,
    send_ref,
    there,
    high_ref,
    back,
    kept_d,
    sent,
    sem,
):
    loads = begin(
        sem, 0, (pick(there_ref), there), (w_high_ref, high_ref), (pick(back_ref), back)
    )
    rows = there.shape[0] // 2
    modes = rows // 2
    wide = local * CH
    size = MZ * CH
    finish(loads[0])
    d = mode_values(rec_ref, there, rows)
    d = d * kz_weight(d.shape)
    kept_d[...] = d
    store = begin(sem, 3, (kept_d, d_ref))
    shape = (wide, local * size)
    rep = (iota(shape, 1) // size == iota(shape, 0) // CH) & (
        iota(shape, 1) % CH == iota(shape, 0) % CH
    )
    rep = rep.astype(bf16)
    high, low = halves(d)
    spread = dot(high, rep) + dot(low, rep)
    spread = jnp.where(same_mode(rows, local * size), spread, 0.0)
    lane_k = (iota((2 * MZ, 2 * wide), 1) // CH) % local
    parts = ([], [])
    finish(loads[1])
    for g in range(modes // MZ):
        pieces = []
        for k in range(local):
            for part in range(2):
                at = part * modes + g * MZ
                pieces.append(spread[at : at + MZ, k * size : (k + 1) * size])
        left_high, left_low = halves(jnp.concatenate(pieces, 0))
        count = left_high.shape[0]
        both = dot(
            jnp.concatenate([left_high, left_low], 0), high_ref[g * size : (g + 1) * size]
        )
        value = both[:count] + both[count:]
        total = None
        for k in range(local):
            piece = jnp.where(lane_k == k, value[2 * k * MZ : 2 * (k + 1) * MZ], 0.0)
            total = piece if total is None else total + piece
        parts[0].append(total[:MZ])
        parts[1].append(total[MZ:])
    real = jnp.concatenate(parts[0], 0)
    imag = jnp.concatenate(parts[1], 0)
    value = jnp.concatenate(
        [real[:, :wide] + imag[:, wide:], imag[:, :wide] - real[:, wide:]], 0
    )
    finish(loads[2])
    put_back(value, back, sent, send_ref, sem, 4)
    finish(*store)


def pack_kernel(local, w_ref, high_ref, low_ref, w, high, low, sem):
    parts = 4
    rows = w.shape[2] // parts
    spans = [pl.ds(step * rows, rows) for step in range(parts)]
    loads = begin(sem, 0, *[(w_ref.at[:, :, span], w.at[:, :, span]) for span in spans])
    stores = []
    for step in range(parts):
        at = slice(step * rows, (step + 1) * rows)
        finish(loads[step])
        pieces = [w[part, k, at] for part in range(2) for k in range(local)]
        high[at], low[at] = halves(jnp.concatenate(pieces, 1))
        stores += begin(
            sem,
            parts + 2 * step,
            (high.at[spans[step]], high_ref.at[spans[step]]),
            (low.at[spans[step]], low_ref.at[spans[step]]),
        )
    finish(*stores)


def weight_grad_kernel(d_ref, v_ref, out_ref):
    step = pl.program_id(0)
    rows, wide = d_ref.shape
    modes = rows // 2
    size = MZ * CH
    shape = (wide, size)
    rep = (iota(shape, 0) == step * CH + iota(shape, 1) % CH).astype(bf16)
    shape = (wide, CH)
    sel = (iota(shape, 0) == step * CH + iota(shape, 1)).astype(bf16)
    keep = same_mode(rows, size)
    d_high, d_low = halves(d_ref[...])
    d_high = jnp.where(keep, dot(d_high, rep), 0.0)
    d_low = jnp.where(keep, dot(d_low, rep), 0.0)
    v_high, v_low = halves(v_ref[...])
    v_high, v_low = dot(v_high, sel), dot(v_low, sel)
    for g in range(modes // MZ):
        real = slice(g * MZ, (g + 1) * MZ)
        imag = slice(modes + g * MZ, modes + (g + 1) * MZ)
        left = jnp.concatenate(
            [d_high[real], d_high[imag], d_low[real], d_low[imag], d_high[real], d_high[imag]], 0
        ).astype(bf16)
        for part in range(2):
            rights = []
            for v in (v_high, v_high, v_low):
                rights += [v[real], v[imag]] if part == 0 else [-v[imag], v[real]]
            right = jnp.concatenate(rights, 0).astype(bf16)
            out_ref[part, 0, g * size : (g + 1) * size, :] = dot(left, right, TN)


def inverse_x(rec_ref, table, local, cells, wide, left, load):
    wide[...] = rec_ref[...].reshape(-1, rec_ref.shape[2]).astype(f32)
    rows = wide.shape[0] // cells
    for cell in range(cells):
        turned = wide[pl.ds(cell, rows, stride=cells), :].T.astype(bf16)
        for k in range(local):
            left[cell * CH : (cell + 1) * CH, k * rows : (k + 1) * rows] = turned[
                k * CH : (k + 1) * CH
            ]
    depth = local * rows
    value = left[...]
    finish(load)
    return dot(value, table[:depth]) + dot(value, table[depth:])


def gelu_pair(pre_act):
    cube_term = pre_act * pre_act * pre_act
    tanh_result = jnp.tanh(root_coef * (pre_act + 0.044715 * cube_term))
    activated_output = 0.5 * pre_act * (1.0 + tanh_result)
    gelu_slope = 0.5 * (1.0 + tanh_result) + 0.5 * pre_act * (
        1.0 - tanh_result * tanh_result
    ) * root_coef * (1.0 + 3.0 * 0.044715 * pre_act * pre_act)
    return (activated_output, gelu_slope)


def middle_kernel(
    local,
    blocks,
    copies,
    rec_ref,
    back_ref,
    base_ref,
    cot_ref,
    coarse_ref,
    table_ref,
    out_ref,
    grad_ref,
    round_ref,
    low_ref,
    high_ref,
    send_ref,
    back,
    base,
    cot,
    coarse,
    table,
    out,
    grad,
    rounded,
    wide,
    left,
    scratch,
    sent,
    sem,
):
    loads = begin(
        sem,
        0,
        (back_ref, back),
        (base_ref, base),
        (cot_ref, cot),
        (table_ref, table),
        (coarse_ref, coarse),
    )
    rows_y, rows_z, _, span = base.shape
    cells = rows_y * rows_z
    pre_act = inverse_x(rec_ref, back, local, cells, wide, left, loads[0])
    finish(*loads[1:])
    pre_act = pre_act + base[...].reshape(pre_act.shape)
    activated, slope = gelu_pair(pre_act)
    out[...] = activated.astype(bf16).reshape(out.shape)
    value = cot[...].astype(f32).reshape(pre_act.shape) * slope
    grad[...] = value.reshape(grad.shape)
    stores = begin(sem, 5, (out, out_ref), (grad, grad_ref))
    high, low = halves(value)
    both = dot(table[...], high, NT)
    product = both[: 2 * MX] + both[2 * MX :] + dot(table[: 2 * MX], low, NT)
    stores += put_x_modes(
        product, local, blocks, copies, cells, scratch, sent, send_ref, sem, 7
    )
    rounded[:cells] = high.reshape(cells, CH, span)
    for y in range(rows_y):
        low_ref[y] = rounded[rows_z * y]
        high_ref[y] = rounded[rows_z * y + rows_z - 1]
    pool = pool_matrix(span)
    for yc in range(2):
        sums = []
        for zc in range(2):
            y, z = 2 * yc, 2 * zc
            sums.append(grad[y, z] + grad[y, z + 1] + grad[y + 1, z] + grad[y + 1, z + 1])
        total_high, total_low = halves(jnp.concatenate(sums, 0))
        total = dot(total_high, pool) + dot(total_low, pool)
        pieces = []
        for zc in range(2):
            piece = total[zc * CH : (zc + 1) * CH]
            pieces.append(jnp.where(coarse[yc, zc].astype(f32) > 0, piece, 0.0))
        piece = jnp.concatenate(pieces, 1).astype(bf16)
        rounded[cells + yc] = piece
        low_ref[rows_y + yc] = piece
        high_ref[rows_y + yc] = piece
    finish(*begin(sem, 9, (rounded, round_ref)), *stores)


def last_kernel(local, rec_ref, back_ref, base_ref, out_ref, back, base, out, wide, left, sem):
    loads = begin(sem, 0, (back_ref, back), (base_ref, base))
    cells = base.shape[0] * base.shape[1]
    value = inverse_x(rec_ref, back, local, cells, wide, left, loads[0])
    finish(loads[1])
    value = value.reshape(base.shape) + base[...]
    out[...] = jnp.transpose(value.astype(bf16), (2, 0, 1, 3))
    finish(*begin(sem, 2, (out, out_ref)))


def turn_kernel(value_ref, out_ref, value, out, sem):
    finish(*begin(sem, 0, (value_ref, value)))
    out[...] = jnp.transpose(value[...], (2, 0, 1, 3))
    finish(*begin(sem, 1, (out, out_ref)))


def bands_kernel(adjoint, fine_ref, coarse_ref, out_ref, out, sem):
    stores = []
    for index, k_ref in enumerate((fine_ref, coarse_ref)):
        for a in range(3):
            for e in range(3):
                taps = []
                for b in range(3):
                    if adjoint:
                        tap = k_ref[9 * (2 - a) + 3 * (2 - b) + 2 - e].astype(f32).T
                    else:
                        tap = k_ref[9 * a + 3 * b + e].astype(f32)
                    taps.append(tap)
                taps = jnp.concatenate(taps, 1)
                for z in range(4):
                    pieces = [taps, jnp.zeros((CH, (5 - z) * CH), f32)]
                    if z > 0:
                        pieces.insert(0, jnp.zeros((CH, z * CH), f32))
                    row = jnp.concatenate(pieces, 1)
                    at = (e * 4 + z) * CH
                    out[index, at : at + CH, a * 8 * CH : (a + 1) * 8 * CH] = row.astype(bf16)
        stores += begin(sem, index, (out.at[index], out_ref.at[index]))
    finish(*stores)


def x_sum(low, same, high):
    span = same.shape[1]
    lane = iota(same.shape, 1)
    before = jnp.where(lane == 0, 0.0, pltpu.roll(low, 1, axis=1))
    after = jnp.where(lane == span - 1, 0.0, pltpu.roll(high, span - 1, axis=1))
    return same + before + after


def band_conv(bands, planes):
    value = dot(bands, jnp.concatenate(planes, 0))
    size = 4 * CH
    return x_sum(value[:size], value[size : 2 * size], value[2 * size :])


def column(row_ref, copies):
    eye = iota((CH, CH), 0) == iota((CH, CH), 1)
    value = jnp.sum(jnp.where(eye, row_ref[...], 0.0), axis=1, keepdims=True)
    return jnp.concatenate([value] * copies, 0)


def pool_matrix(span):
    shape = (span, span // 2)
    return (iota(shape, 0) // 2 == iota(shape, 1)).astype(bf16)


def up_matrix(span):
    shape = (span // 2, span)
    return (iota(shape, 1) // 2 == iota(shape, 0)).astype(bf16)


def y_message_kernel(u_ref, zlo_ref, zhi_ref, rows_ref, low_ref, high_ref, u, rows, sem):
    (load,) = begin(sem, 0, (u_ref, u))
    for y in range(4):
        for z in range(3):
            rows[y, z * CH : (z + 1) * CH] = zlo_ref[y, z]
            rows[y, (z + 7) * CH : (z + 8) * CH] = zhi_ref[y, z]
    finish(load)
    for y in range(4):
        for z in range(4):
            rows[y, (z + 3) * CH : (z + 4) * CH] = u[y, z]
    (store,) = begin(sem, 1, (rows, rows_ref))
    low_ref[...] = rows[:3]
    high_ref[...] = rows[1:]
    finish(store)


def forward_conv_kernel(
    rows_ref,
    ylo_ref,
    yhi_ref,
    lin_ref,
    bands_ref,
    bias_fine_ref,
    bias_coarse_ref,
    base_ref,
    fine_ref,
    coarse_ref,
    grid,
    bands,
    pooled,
    base,
    fine,
    coarse,
    sem,
):
    span = grid.shape[2]
    inner = pl.ds(0, 10 * CH)
    loads = begin(
        sem,
        0,
        (bands_ref.at[0], bands.at[0]),
        (rows_ref, grid.at[pl.ds(3, 4), inner]),
        (ylo_ref, grid.at[pl.ds(0, 3), inner]),
        (yhi_ref, grid.at[pl.ds(7, 3), inner]),
        (bands_ref.at[1], bands.at[1]),
    )
    edges = [
        lax.axis_index("gy") > 0,
        lax.axis_index("gy") < lax.axis_size("gy") - 1,
        lax.axis_index("gz") > 0,
        lax.axis_index("gz") < lax.axis_size("gz") - 1,
    ]
    grid[:, 10 * CH :, :] = jnp.zeros((10, 2 * CH, span), bf16)
    pooled[:, 4 * CH :, :] = jnp.zeros((4, 4 * CH, span // 2), bf16)
    bias = column(bias_fine_ref, 4)
    half = 4 * CH
    row_z = iota((half, span), 0) // CH
    pool = pool_matrix(span)
    pools = [None] * 8
    finish(loads[0], loads[1])
    for y in (3, 4, 2, 1, 0, 5, 6, 7):
        if y == 2:
            finish(loads[2])
        if y == 5:
            finish(loads[3])
        sums = []
        y_in = None
        if y < 2:
            y_in = edges[0]
        elif y >= 6:
            y_in = edges[1]
        for h in range(2):
            at = h * half
            value = band_conv(bands[0], [grid[y + a, at : at + 8 * CH, :] for a in range(3)])
            value = jnp.maximum(value + bias, 0.0)
            inside = (row_z >= 2) | edges[2] if h == 0 else (row_z < 2) | edges[3]
            if y_in is not None:
                inside = inside & y_in
            value = jnp.where(inside, value, 0.0).astype(bf16)
            fine[y, at : at + half, :] = value
            sums.append(dot(value, pool))
        pools[y] = jnp.concatenate(sums, 0)
    stores = begin(sem, 5, (fine, fine_ref))
    for yc in range(4):
        both = pools[2 * yc] + pools[2 * yc + 1]
        for zc in range(4):
            at = 2 * zc * CH
            value = both[at : at + CH] + both[at + CH : at + 2 * CH]
            pooled[yc, zc * CH : (zc + 1) * CH, :] = (0.125 * value).astype(bf16)
    up = up_matrix(span)
    bias = column(bias_coarse_ref, 2)
    finish(loads[4])
    for yc in range(2):
        value = band_conv(bands[1], [pooled[yc + a] for a in range(3)])
        value = jnp.maximum(value[: 2 * CH] + bias, 0.0).astype(bf16)
        lifted = dot(value, up)
        for zc in range(2):
            coarse[yc, zc] = value[zc * CH : (zc + 1) * CH]
            for y in (2 * yc, 2 * yc + 1):
                for z in (2 * zc, 2 * zc + 1):
                    total = dot(lin_ref[...], grid[y + 3, (z + 3) * CH : (z + 4) * CH, :])
                    total = total + fine[y + 2, (z + 2) * CH : (z + 3) * CH, :].astype(f32)
                    base[y, z] = total + lifted[zc * CH : (zc + 1) * CH]
    finish(*begin(sem, 6, (base, base_ref), (coarse, coarse_ref)), *stores)


def y_gradient_kernel(round_ref, zlo_ref, zhi_ref, kept_ref, low_ref, high_ref, own, sem):
    (load,) = begin(sem, 0, (round_ref, own))
    stores = begin(
        sem, 1, (zlo_ref, kept_ref.at[pl.ds(0, 6)]), (zhi_ref, kept_ref.at[pl.ds(6, 6)])
    )
    finish(load)
    for out_ref, y in ((low_ref, 0), (high_ref, 3)):
        out_ref[0] = zlo_ref[y]
        out_ref[1:5] = own[4 * y : 4 * y + 4]
        out_ref[5] = zhi_ref[y]
        for yc in range(2):
            out_ref[6 + 3 * yc] = zlo_ref[4 + yc]
            out_ref[7 + 3 * yc] = own[16 + yc]
            out_ref[8 + 3 * yc] = zhi_ref[4 + yc]
    finish(*stores)


def backward_conv_kernel(
    grad_ref,
    round_ref,
    kept_ref,
    ylo_ref,
    yhi_ref,
    fine_ref,
    lin_ref,
    bands_ref,
    base_ref,
    grad,
    rounded,
    kept,
    ylo,
    yhi,
    fine,
    bands,
    coarse_grid,
    fine_grid,
    base,
    sem,
):
    loads = begin(
        sem,
        0,
        (bands_ref.at[1], bands.at[1]),
        (round_ref, rounded),
        (kept_ref, kept),
        (ylo_ref, ylo),
        (yhi_ref, yhi),
        (grad_ref, grad),
        (fine_ref, fine),
        (bands_ref.at[0], bands.at[0]),
    )
    span = grad.shape[3]
    half = span // 2
    coarse_grid[:, 6 * CH :, :] = jnp.zeros((6, 2 * CH, half), bf16)
    fine_grid[:, 6 * CH :, :] = jnp.zeros((6, 2 * CH, span), bf16)

    def place(yc, pair, value):
        for zc in range(2):
            at = (2 * pair + zc) * CH
            coarse_grid[yc, at : at + CH, :] = value[:, zc * half : (zc + 1) * half]

    finish(*loads[:5])
    for yc in range(2):
        place(2 + yc, 0, kept[4 + yc])
        place(2 + yc, 1, rounded[16 + yc])
        place(2 + yc, 2, kept[10 + yc])
        for pair in range(3):
            place(yc, pair, ylo[6 + 3 * yc + pair])
            place(4 + yc, pair, yhi[6 + 3 * yc + pair])
    up = up_matrix(span)
    finish(*loads[5:7])
    for yc in range(4):
        pooled = 0.125 * band_conv(bands[1], [coarse_grid[yc + a] for a in range(3)])
        high, low = halves(pooled)
        lifted = dot(high, up) + dot(low, up)
        for y in range(6):
            if (y + 1) // 2 != yc:
                continue
            for z in range(6):
                zc = (z + 1) // 2
                if 1 <= y <= 4 and 1 <= z <= 4:
                    value = grad[y - 1, z - 1]
                elif 1 <= y <= 4:
                    value = kept[y - 1 if z == 0 else y + 5].astype(f32)
                else:
                    value = (ylo if y == 0 else yhi)[z].astype(f32)
                value = value + lifted[zc * CH : (zc + 1) * CH]
                mask = fine[y + 1, (z + 1) * CH : (z + 2) * CH, :].astype(f32) > 0
                fine_grid[y, z * CH : (z + 1) * CH, :] = jnp.where(mask, value, 0.0).astype(bf16)
    finish(loads[7])
    for y in range(4):
        value = band_conv(bands[0], [fine_grid[y + a] for a in range(3)])
        for z in range(4):
            linear = dot(lin_ref[...], rounded[4 * y + z], TN)
            base[y, z] = value[z * CH : (z + 1) * CH] + linear
    finish(*begin(sem, 8, (base, base_ref)))


def shift(block, axis, step):
    count = lax.axis_size(axis)
    pairs = [(i, i + step) for i in range(count) if 0 <= i + step < count]
    return lax.ppermute(block, axis, pairs)


def exchange(block):
    return lax.all_to_all(block, BOTH, split_axis=0, concat_axis=0, tiled=True)


def shards(
    carbon_input_volume,
    cotangent,
    spec_weight,
    lin_weight,
    conv_fine,
    bias_fine,
    conv_coarse,
    bias_coarse,
):
    channels, rows_y, rows_z, span = carbon_input_volume.shape
    gy, gz = lax.axis_size("gy"), lax.axis_size("gz")
    devices = gy * gz
    cells = rows_y * rows_z
    local = MX // gy
    modes = (MY // gz) * MZ
    wide = local * CH
    scale = 1.0 / math.sqrt(span * cells * devices)
    there, back = mode_tables(gy, gz, rows_y, rows_z, scale)
    forward_x = jnp.asarray(x_tables(span, gy))
    inverse_table = jnp.asarray(x_back_table(span, gy, gz))

    limit = (14 << 20) + devices * (64 << 10)
    chunk = struct((devices, 2 * cells, wide), bf16)
    sent = pltpu.VMEM(chunk.shape, bf16)
    field = struct((rows_y, rows_z, CH, span))
    field_v = pltpu.VMEM(field.shape, f32)
    round_field = struct(field.shape, bf16)
    round_v = pltpu.VMEM(field.shape, bf16)
    raw = struct(carbon_input_volume.shape, bf16)
    raw_v = pltpu.VMEM(raw.shape, bf16)
    table_v = pltpu.VMEM(forward_x.shape, bf16)
    inverse_v = pltpu.VMEM(inverse_table.shape, bf16)
    there_v = pltpu.VMEM(there.shape[1:], bf16)
    back_v = pltpu.VMEM(back.shape[1:], bf16)
    x_scratch = pltpu.VMEM((2 * gy * cells, wide), f32)
    wide_scratch = pltpu.VMEM((devices * 2 * cells, wide), f32)
    left_scratch = pltpu.VMEM((cells * CH, local * devices * 2), bf16)
    mode_field = struct((2 * modes, wide))
    mode_v = pltpu.VMEM(mode_field.shape, f32)
    rows = modes * CH
    packed = struct((rows, 2 * wide), bf16)
    packed_v = pltpu.VMEM(packed.shape, bf16)
    bands = struct((2, 12 * CH, 24 * CH), bf16)
    bands_v = pltpu.VMEM(bands.shape, bf16)
    side = struct((rows_y, 3, CH, span), bf16)
    message = struct((6, CH, span), bf16)
    y_side = struct((3, 10 * CH, span), bf16)
    y_message = struct((12, CH, span), bf16)

    with jax.named_scope("spread_input"):
        u, low, high, send = run(
            lambda *refs: spread_kernel(local, gy, gz, *refs),
            [(IN_HBM, carbon_input_volume), (IN_HBM, forward_x)],
            [(IN_HBM, round_field), (IN_VMEM, side), (IN_VMEM, side), (IN_HBM, chunk)],
            limit,
            [raw_v, table_v, round_v, x_scratch, sent],
            copies=5,
        )
    zlo = shift(high, "gz", 1)
    zhi = shift(low, "gz", -1)
    received = exchange(send)

    with jax.named_scope("y_message"):
        field_rows, low, high = run(
            y_message_kernel,
            [(IN_HBM, u), (IN_VMEM, zlo), (IN_VMEM, zhi)],
            [
                (IN_HBM, struct((rows_y, 10 * CH, span), bf16)),
                (IN_VMEM, y_side),
                (IN_VMEM, y_side),
            ],
            limit,
            [round_v, pltpu.VMEM((rows_y, 10 * CH, span), bf16)],
            copies=2,
        )
    ylo = shift(high, "gy", 1)
    yhi = shift(low, "gy", -1)

    with jax.named_scope("pack_weights"):
        w_high, w_low = run(
            lambda *refs: pack_kernel(local, *refs),
            [(IN_HBM, spec_weight.reshape(2, local, rows, CH))],
            [(IN_HBM, packed), (IN_HBM, packed)],
            limit + (10 << 20),
            [pltpu.VMEM((2, local, rows, CH), f32), packed_v, packed_v],
            copies=12,
            micros=4,
        )

    def make_bands(adjoint):
        with jax.named_scope("bands"):
            return run(
                lambda *refs: bands_kernel(adjoint, *refs),
                [(IN_VMEM, conv_fine), (IN_VMEM, conv_coarse)],
                [(IN_HBM, bands)],
                limit,
                [bands_v],
                copies=2,
                micros=2,
            )[0]

    forward_bands = make_bands(False)
    cot = jnp.transpose(cotangent, (1, 2, 0, 3))

    with jax.named_scope("mix"):
        v, send = run(
            lambda *refs: mix_kernel(local, *refs),
            [
                (IN_VMEM, received),
                (IN_HBM, there),
                (IN_HBM, w_high),
                (IN_HBM, w_low),
                (IN_HBM, back),
            ],
            [(IN_HBM, mode_field), (IN_HBM, chunk)],
            limit,
            [there_v, packed_v, packed_v, back_v, mode_v, sent],
            copies=9,
            micros=3,
        )
    received = exchange(send)

    with jax.named_scope("forward_convs"):
        base, fine, coarse = run(
            forward_conv_kernel,
            [
                (IN_HBM, field_rows),
                (ANYWHERE, ylo),
                (ANYWHERE, yhi),
                (IN_VMEM, lin_weight),
                (IN_HBM, forward_bands),
                (IN_VMEM, bias_fine[None]),
                (IN_VMEM, bias_coarse[None]),
            ],
            [
                (IN_HBM, field),
                (IN_HBM, struct((8, 8 * CH, span), bf16)),
                (IN_HBM, struct((2, 2, CH, span // 2), bf16)),
            ],
            limit,
            [
                pltpu.VMEM((10, 12 * CH, span), bf16),
                bands_v,
                pltpu.VMEM((4, 8 * CH, span // 2), bf16),
                field_v,
                pltpu.VMEM((8, 8 * CH, span), bf16),
                pltpu.VMEM((2, 2, CH, span // 2), bf16),
            ],
            copies=8,
            micros=8,
        )

    with jax.named_scope("middle"):
        activated, grad, grad_round, low, high, send = run(
            lambda *refs: middle_kernel(local, gy, gz, *refs),
            [
                (IN_VMEM, received),
                (IN_HBM, inverse_table),
                (IN_HBM, base),
                (IN_HBM, cot),
                (IN_HBM, coarse),
                (IN_HBM, forward_x),
            ],
            [
                (IN_HBM, round_field),
                (IN_HBM, field),
                (IN_HBM, struct((cells + 2, CH, span), bf16)),
                (IN_VMEM, message),
                (IN_VMEM, message),
                (IN_HBM, chunk),
            ],
            limit,
            [
                inverse_v,
                field_v,
                round_v,
                pltpu.VMEM((2, 2, CH, span // 2), bf16),
                table_v,
                round_v,
                field_v,
                pltpu.VMEM((cells + 2, CH, span), bf16),
                wide_scratch,
                left_scratch,
                x_scratch,
                sent,
            ],
            copies=10,
            micros=3,
        )
    zlo = shift(high, "gz", 1)
    zhi = shift(low, "gz", -1)
    received = exchange(send)

    with jax.named_scope("y_gradient"):
        kept_z, low, high = run(
            y_gradient_kernel,
            [(IN_HBM, grad_round), (IN_VMEM, zlo), (IN_VMEM, zhi)],
            [(IN_HBM, y_message), (IN_VMEM, y_message), (IN_VMEM, y_message)],
            limit,
            [pltpu.VMEM((cells + 2, CH, span), bf16)],
            copies=3,
        )
    ylo = shift(high, "gy", 1)
    yhi = shift(low, "gy", -1)
    backward_bands = make_bands(True)
    with jax.named_scope("turn"):
        (predicted,) = run(
            turn_kernel, [(IN_HBM, activated)], [(IN_HBM, raw)], limit, [round_v, raw_v], copies=2
        )

    with jax.named_scope("mix_adjoint"):
        d, send = run(
            lambda *refs: adjoint_kernel(local, *refs),
            [(IN_VMEM, received), (IN_HBM, there), (IN_HBM, w_high), (IN_HBM, back)],
            [(IN_HBM, mode_field), (IN_HBM, chunk)],
            limit,
            [there_v, packed_v, back_v, mode_v, sent],
            copies=8,
            micros=2,
        )
    received = exchange(send)

    with jax.named_scope("weight_grad"):
        full = pl.BlockSpec((2 * modes, wide), lambda i: (0, 0))
        (weight_grad,) = run(
            weight_grad_kernel,
            [(full, d), (full, v)],
            [
                (
                    pl.BlockSpec((2, 1, rows, CH), lambda i: (0, i, 0, 0)),
                    struct((2, local, rows, CH)),
                )
            ],
            limit,
            grid=(local,),
            micros=4,
        )
    weight_grad = weight_grad.reshape(spec_weight.shape)

    with jax.named_scope("backward_convs"):
        (base,) = run(
            backward_conv_kernel,
            [
                (IN_HBM, grad),
                (IN_HBM, grad_round),
                (IN_HBM, kept_z),
                (ANYWHERE, ylo),
                (ANYWHERE, yhi),
                (IN_HBM, fine),
                (IN_VMEM, lin_weight),
                (IN_HBM, backward_bands),
            ],
            [(IN_HBM, field)],
            limit,
            [
                field_v,
                pltpu.VMEM((cells + 2, CH, span), bf16),
                pltpu.VMEM(y_message.shape, bf16),
                pltpu.VMEM(y_message.shape, bf16),
                pltpu.VMEM(y_message.shape, bf16),
                pltpu.VMEM((8, 8 * CH, span), bf16),
                bands_v,
                pltpu.VMEM((6, 8 * CH, span // 2), bf16),
                pltpu.VMEM((6, 8 * CH, span), bf16),
                field_v,
            ],
            copies=9,
            micros=4,
        )

    with jax.named_scope("last"):
        (sensitivity,) = run(
            lambda *refs: last_kernel(local, *refs),
            [(IN_VMEM, received), (IN_HBM, inverse_table), (IN_HBM, base)],
            [(IN_HBM, raw)],
            limit,
            [inverse_v, field_v, raw_v, wide_scratch, left_scratch],
            copies=3,
            micros=2,
        )
    return (predicted, sensitivity, weight_grad)


def solution(mesh):
    field = P(None, "gy", "gz", None)
    modes = P(None, "gy", "gz", None, None, None)
    return jax.shard_map(
        shards,
        mesh=mesh,
        in_specs=(field, field, modes, P(), P(), P(), P(), P()),
        out_specs=(field, field, modes),
        check_vma=False,
    )
```

```python
import math

import jax
import jax.numpy as jnp
import ml_dtypes
import numpy as np
from jax import lax
from jax.experimental import pallas as pl
from jax.experimental.pallas import tpu as pltpu
from jax.sharding import PartitionSpec as P

MX = 32
MY = 32
MZ = 8
CH = 32
BOTH = ("gy", "gz")

f32 = jnp.float32
bf16 = jnp.bfloat16
root_coef = math.sqrt(2.0 / math.pi)
NN = (((1,), (0,)), ((), ()))
NT = (((1,), (1,)), ((), ()))
TN = (((0,), (0,)), ((), ()))


def dot(a, b, form=NN):
    return lax.dot_general(a, b, form, preferred_element_type=f32)


def halves(value):
    high = value.astype(bf16)
    return high, (value - high.astype(f32)).astype(bf16)


def iota(shape, dim):
    return lax.broadcasted_iota(jnp.int32, shape, dim)


IN_VMEM = pl.BlockSpec(memory_space=pltpu.VMEM)
IN_HBM = pl.BlockSpec(memory_space=pltpu.HBM)


def struct(shape, kind=f32):
    return jax.ShapeDtypeStruct(shape, kind)


def run(kernel, ins, outs, limit, scratch=(), micros=1.0, copies=0, **grid):
    scratch = list(scratch)
    if copies:
        scratch.append(pltpu.SemaphoreType.DMA((copies,)))
    held = {id(IN_HBM): pltpu.HBM, id(IN_VMEM): pltpu.VMEM}

    def placed(spec, array):
        if id(spec) in held:
            return pltpu.with_memory_space_constraint(array, held[id(spec)])
        return array

    def shaped(spec, shape):
        if id(spec) in held:
            return held[id(spec)](shape.shape, shape.dtype)
        return shape

    return pl.pallas_call(
        kernel,
        in_specs=[spec for spec, _ in ins],
        out_specs=[spec for spec, _ in outs],
        out_shape=[shaped(spec, shape) for spec, shape in outs],
        scratch_shapes=scratch,
        compiler_params=pltpu.CompilerParams(vmem_limit_bytes=limit),
        cost_estimate=pl.CostEstimate(
            flops=int(micros * 1.1e9), bytes_accessed=1 << 16, transcendentals=0
        ),
        **grid,
    )(*[placed(spec, array) for spec, array in ins])


def begin(sem, first, *pairs):
    copies = [
        pltpu.make_async_copy(source, target, sem.at[first + i])
        for i, (source, target) in enumerate(pairs)
    ]
    for copy in copies:
        copy.start()
    return copies


def finish(*copies):
    for copy in copies:
        copy.wait()


def kept(count, length):
    position = np.arange(count)
    return np.where(position < count // 2, position, length - count + position)


def split_np(table):
    high = table.astype(ml_dtypes.bfloat16)
    return high, (table - high.astype(np.float64)).astype(ml_dtypes.bfloat16)


def x_tables(cells_x, blocks):
    local = MX // blocks
    freqs = kept(MX, cells_x).reshape(blocks, local).T
    angles = 2.0 * np.pi * ((freqs[:, :, None] * np.arange(cells_x)) % cells_x) / cells_x
    table = np.stack([np.cos(angles), -np.sin(angles)], axis=2).reshape(2 * MX, cells_x)
    return np.concatenate(split_np(table), axis=0)


def x_back_table(cells_x, gy, gz):
    local = MX // gy
    freqs = kept(MX, cells_x).reshape(gy, local).T
    angles = 2.0 * np.pi * ((freqs[:, :, None] * np.arange(cells_x)) % cells_x) / cells_x
    table = np.stack([np.cos(angles), -np.sin(angles)], axis=2)
    table = np.broadcast_to(table[:, :, None], (local, gy, gz, 2, cells_x))
    return np.concatenate(split_np(table.reshape(-1, cells_x)), axis=0)


def yz_angles(xp, freqs_y, gy, gz, rows_y, rows_z):
    span_y, span_z = gy * rows_y, gz * rows_z
    phase_y = (freqs_y[:, None] * xp.arange(span_y)[None]) % span_y
    phase_z = (xp.arange(MZ)[:, None] * xp.arange(span_z)[None]) % span_z
    phase_y = phase_y.reshape(-1, 1, gy, 1, rows_y, 1)
    phase_z = phase_z.reshape(1, MZ, 1, gz, 1, rows_z)
    turn = (phase_y * span_z + phase_z * span_y) % (span_y * span_z)
    return turn.reshape(turn.shape[0] * MZ, gy * gz, rows_y * rows_z)


def yz_table(xp, freqs_y, gy, gz, rows_y, rows_z):
    cells = gy * gz * rows_y * rows_z
    turn = yz_angles(xp, freqs_y, gy, gz, rows_y, rows_z)
    angles = 2.0 * math.pi / cells * turn
    cosine, sine = xp.cos(angles), xp.sin(angles)
    table = xp.stack([xp.stack([cosine, sine], 2), xp.stack([-sine, cosine], 2)], 0)
    return table.reshape(2 * turn.shape[0], -1)


def mode_tables(gy, gz, rows_y, rows_z, scale):
    local = MY // gz
    cells = gy * gz * rows_y * rows_z
    freqs = kept(MY, gy * rows_y).reshape(gz, local)
    if gz * 2 * local * MZ * 2 * cells <= 1 << 20:
        there, back = [], []
        for block in range(gz):
            high, low = split_np(scale * yz_table(np, freqs[block], gy, gz, rows_y, rows_z))
            there.append(np.concatenate([high, low], 0))
            back.append(np.concatenate([high.T, low.T], 1))
        return jnp.asarray(np.stack(there)), jnp.asarray(np.stack(back))
    where = lax.axis_index("gz")
    mine = lax.dynamic_index_in_dim(jnp.asarray(freqs, jnp.int32), where, keepdims=False)
    high, low = halves(scale * yz_table(jnp, mine, gy, gz, rows_y, rows_z).astype(f32))
    return jnp.concatenate([high, low], 0)[None], jnp.concatenate([high.T, low.T], 1)[None]


def put_x_modes(product, local, blocks, copies, cells, scratch, sent, send_ref, sem, first):
    rows = 2 * blocks
    for cell in range(cells):
        piece = product[:, cell * CH : (cell + 1) * CH]
        value = jnp.concatenate([piece[k * rows : (k + 1) * rows] for k in range(local)], axis=1)
        scratch[pl.ds(cell, rows, stride=cells), :] = value
    moves = []
    half = blocks // 2
    for block in range(blocks):
        value = scratch[block * 2 * cells : (block + 1) * 2 * cells].astype(bf16)
        for copy in range(copies):
            sent[block * copies + copy] = value
        if (block + 1) % half == 0:
            part = pl.ds((block + 1 - half) * copies, half * copies)
            moves += begin(sem, first + len(moves), (sent.at[part], send_ref.at[part]))
    return moves


def arrive_kernel(raw_ref, table_ref, u_ref, low_ref, high_ref, my_table_ref, raw, sem):
    loads = begin(sem, 0, (raw_ref, raw), (table_ref, my_table_ref))
    finish(*loads)
    u = jnp.transpose(raw[...], (1, 2, 0, 3))
    u_ref[...] = u
    low_ref[...] = u[:, :3]
    high_ref[...] = u[:, 1:]


def spread_kernel(
    exact, local, blocks, copies, u_ref, table, send_ref, scratch, sent, sem
):
    cells = u_ref.shape[0] * u_ref.shape[1]
    u = u_ref[...].reshape(cells * CH, -1)
    if exact:
        both = dot(table[...], u, NT)
        product = both[: 2 * MX] + both[2 * MX :]
    else:
        high, low = halves(u)
        both = dot(table[...], high, NT)
        product = both[: 2 * MX] + both[2 * MX :] + dot(table[: 2 * MX], low, NT)
    finish(*put_x_modes(product, local, blocks, copies, cells, scratch, sent, send_ref, sem, 0))


def pick(tables_ref):
    if tables_ref.shape[0] == 1:
        return tables_ref.at[0]
    return tables_ref.at[lax.axis_index("gz")]


def mode_values(rec_ref, there, rows):
    both = dot(there[...], rec_ref[...].reshape(-1, rec_ref.shape[2]))
    return both[:rows] + both[rows:]


def put_back(values, back_ref, sent, send_ref, sem, first):
    high, low = halves(values)
    twice = jnp.concatenate([high, high], 0)
    rows = values.shape[0]
    devices, depth, wide = sent.shape
    part = devices // 4
    moves = []
    for step in range(4):
        at = slice(step * part * depth, (step + 1) * part * depth)
        result = dot(back_ref[at], twice) + dot(back_ref[at, :rows], low)
        sent[step * part : (step + 1) * part] = result.astype(bf16).reshape(part, depth, wide)
        span = pl.ds(step * part, part)
        moves += begin(sem, first + step, (sent.at[span], send_ref.at[span]))
    finish(*moves)


def kz_weight(shape):
    return jnp.where(iota(shape, 0) % MZ == 0, 1.0, 2.0).astype(f32)


def same_mode(rows, lanes):
    return (iota((rows, lanes), 0) % MZ) == ((iota((rows, lanes), 1) // CH) % MZ)


def mix_kernel(
    local,
    rec_ref,
    there_ref,
    high_ref,
    low_ref,
    back_ref,
    v_ref,
    send_ref,
    kept_v,
    sent,
    sem,
):
    rows = there_ref.shape[0] // 2
    modes = rows // 2
    wide = local * CH
    v = mode_values(rec_ref, there_ref, rows)
    kept_v[...] = v
    store = begin(sem, 0, (kept_v, v_ref))
    real, imag = v[:modes], v[modes:]
    pair = (
        jnp.concatenate([real, -imag], 1),
        jnp.concatenate([imag, real], 1),
    )
    lane_k = (iota((MZ, 2 * wide), 1) // CH) % local
    size = MZ * CH
    diag = same_mode(2 * MZ * local, size)
    placed = [[[None] * (modes // MZ) for _ in range(local)] for _ in range(2)]
    for g in range(modes // MZ):
        pieces = []
        for k in range(local):
            for part in range(2):
                piece = pair[part][g * MZ : (g + 1) * MZ]
                pieces.append(jnp.where(lane_k == k, piece, 0.0))
        left_high, left_low = halves(jnp.concatenate(pieces, 0))
        w_high = high_ref[g * size : (g + 1) * size]
        w_low = low_ref[g * size : (g + 1) * size]
        count = left_high.shape[0]
        both = dot(jnp.concatenate([left_high, left_low], 0), w_high, NT)
        value = both[:count] + both[count:] + dot(left_high, w_low, NT)
        value = jnp.where(diag, value, 0.0)
        for k in range(local):
            for part in range(2):
                at = (2 * k + part) * MZ
                placed[part][k][g] = value[at : at + MZ]
    columns = [jnp.concatenate(placed[0][k] + placed[1][k], 0) for k in range(local)]
    all_values = jnp.concatenate(columns, 1)
    shape = (local * size, wide)
    fold = (iota(shape, 0) // size == iota(shape, 1) // CH) & (
        iota(shape, 0) % CH == iota(shape, 1) % CH
    )
    fold = fold.astype(bf16)
    high, low = halves(all_values)
    mixed = dot(high, fold) + dot(low, fold)
    put_back(mixed * kz_weight(mixed.shape), back_ref, sent, send_ref, sem, 1)
    finish(*store)


def adjoint_kernel(
    local,
    rec_ref,
    there_ref,
    high_ref,
    back_ref,
    d_ref,
    send_ref,
    sent,
    sem,
):
    rows = there_ref.shape[0] // 2
    modes = rows // 2
    wide = local * CH
    size = MZ * CH
    d = mode_values(rec_ref, there_ref, rows)
    d = d * kz_weight(d.shape)
    d_ref[...] = d
    shape = (wide, local * size)
    rep = (iota(shape, 1) // size == iota(shape, 0) // CH) & (
        iota(shape, 1) % CH == iota(shape, 0) % CH
    )
    rep = rep.astype(bf16)
    high, low = halves(d)
    spread = dot(high, rep) + dot(low, rep)
    spread = jnp.where(same_mode(rows, local * size), spread, 0.0)
    lane_k = (iota((2 * MZ, 2 * wide), 1) // CH) % local
    parts = ([], [])
    for g in range(modes // MZ):
        pieces = []
        for k in range(local):
            for part in range(2):
                at = part * modes + g * MZ
                pieces.append(spread[at : at + MZ, k * size : (k + 1) * size])
        left_high, left_low = halves(jnp.concatenate(pieces, 0))
        count = left_high.shape[0]
        both = dot(
            jnp.concatenate([left_high, left_low], 0), high_ref[g * size : (g + 1) * size]
        )
        value = both[:count] + both[count:]
        total = None
        for k in range(local):
            piece = jnp.where(lane_k == k, value[2 * k * MZ : 2 * (k + 1) * MZ], 0.0)
            total = piece if total is None else total + piece
        parts[0].append(total[:MZ])
        parts[1].append(total[MZ:])
    real = jnp.concatenate(parts[0], 0)
    imag = jnp.concatenate(parts[1], 0)
    value = jnp.concatenate(
        [real[:, :wide] + imag[:, wide:], imag[:, :wide] - real[:, wide:]], 0
    )
    put_back(value, back_ref, sent, send_ref, sem, 0)


def setup_kernel(
    local,
    w_ref,
    there_ref,
    back_ref,
    high_ref,
    low_ref,
    my_there_ref,
    my_back_ref,
    kept_ref,
    w,
    sem,
):
    parts = 4
    rows = w.shape[2] // parts
    spans = [pl.ds(step * rows, rows) for step in range(parts)]
    loads = begin(sem, 0, *[(w_ref.at[:, :, span], w.at[:, :, span]) for span in spans])
    tables = begin(
        sem, parts, (pick(there_ref), my_there_ref), (pick(back_ref), my_back_ref)
    )
    stores = []
    for step in range(parts):
        at = slice(step * rows, (step + 1) * rows)
        finish(loads[step])
        pieces = [w[part, k, at] for part in range(2) for k in range(local)]
        high_ref[at], low_ref[at] = halves(jnp.concatenate(pieces, 1))
        stores += begin(sem, parts + 2 + step, (high_ref.at[spans[step]], kept_ref.at[spans[step]]))
    finish(*tables, *stores)


def put_weight_grad(d_ref, v_ref, out, out_ref, sem, first):
    rows, wide = d_ref.shape
    modes = rows // 2
    size = MZ * CH
    keep = same_mode(rows, size)
    d_halves = halves(d_ref[...])
    v_halves = halves(v_ref[...])
    stores = []
    for k in range(wide // CH):
        shape = (wide, size)
        rep = (iota(shape, 0) == k * CH + iota(shape, 1) % CH).astype(bf16)
        d_high, d_low = [jnp.where(keep, dot(value, rep), 0.0) for value in d_halves]
        at = slice(k * CH, (k + 1) * CH)
        v_high, v_low = [value[:, at].astype(f32) for value in v_halves]
        for g in range(modes // MZ):
            real = slice(g * MZ, (g + 1) * MZ)
            imag = slice(modes + g * MZ, modes + (g + 1) * MZ)
            left = jnp.concatenate(
                [d_high[real], d_high[imag], d_low[real], d_low[imag], d_high[real], d_high[imag]],
                0,
            ).astype(bf16)
            for part in range(2):
                rights = []
                for v in (v_high, v_high, v_low):
                    rights += [v[real], v[imag]] if part == 0 else [-v[imag], v[real]]
                right = jnp.concatenate(rights, 0).astype(bf16)
                out[part, k, g * size : (g + 1) * size, :] = dot(left, right, TN)
        stores += begin(sem, first + k, (out.at[:, k], out_ref.at[:, k]))
    return stores


def inverse_x(rec_ref, table, local, cells, wide, left):
    wide[...] = rec_ref[...].reshape(-1, rec_ref.shape[2]).astype(f32)
    rows = wide.shape[0] // cells
    for cell in range(cells):
        turned = wide[pl.ds(cell, rows, stride=cells), :].T.astype(bf16)
        for k in range(local):
            left[cell * CH : (cell + 1) * CH, k * rows : (k + 1) * rows] = turned[
                k * CH : (k + 1) * CH
            ]
    depth = local * rows
    value = left[...]
    return dot(value, table[:depth]) + dot(value, table[depth:])


def gelu_pair(pre_act):
    cube_term = pre_act * pre_act * pre_act
    tanh_result = jnp.tanh(root_coef * (pre_act + 0.044715 * cube_term))
    activated_output = 0.5 * pre_act * (1.0 + tanh_result)
    gelu_slope = 0.5 * (1.0 + tanh_result) + 0.5 * pre_act * (
        1.0 - tanh_result * tanh_result
    ) * root_coef * (1.0 + 3.0 * 0.044715 * pre_act * pre_act)
    return (activated_output, gelu_slope)


def middle_kernel(
    local,
    rec_ref,
    back_ref,
    base_ref,
    cot_ref,
    coarse_ref,
    out_ref,
    grad_ref,
    kept_ref,
    round_ref,
    low_ref,
    high_ref,
    out,
    rounded,
    wide,
    left,
    sem,
):
    rows_y, rows_z, _, span = base_ref.shape
    cells = rows_y * rows_z
    pre_act = inverse_x(rec_ref, back_ref, local, cells, wide, left)
    pre_act = pre_act + base_ref[...].reshape(pre_act.shape)
    activated, slope = gelu_pair(pre_act)
    out[...] = activated.astype(bf16).reshape(out.shape)
    value = cot_ref[...].astype(f32).reshape(pre_act.shape) * slope
    grad_ref[...] = value.reshape(grad_ref.shape)
    stores = begin(sem, 0, (out, out_ref), (grad_ref, kept_ref))
    rounded[:cells] = value.astype(bf16).reshape(cells, CH, span)
    for y in range(rows_y):
        low_ref[y] = rounded[rows_z * y]
        high_ref[y] = rounded[rows_z * y + rows_z - 1]
    pool = pool_matrix(span)
    for yc in range(2):
        sums = []
        for zc in range(2):
            y, z = 2 * yc, 2 * zc
            sums.append(
                grad_ref[y, z] + grad_ref[y, z + 1] + grad_ref[y + 1, z] + grad_ref[y + 1, z + 1]
            )
        total_high, total_low = halves(jnp.concatenate(sums, 0))
        total = dot(total_high, pool) + dot(total_low, pool)
        pieces = []
        for zc in range(2):
            piece = total[zc * CH : (zc + 1) * CH]
            pieces.append(jnp.where(coarse_ref[yc, zc].astype(f32) > 0, piece, 0.0))
        piece = jnp.concatenate(pieces, 1).astype(bf16)
        rounded[cells + yc] = piece
        low_ref[rows_y + yc] = piece
        high_ref[rows_y + yc] = piece
    finish(*begin(sem, 2, (rounded, round_ref)), *stores)


def last_kernel(local, rec_ref, back_ref, base_ref, out_ref, out, wide, left, sem):
    cells = base_ref.shape[0] * base_ref.shape[1]
    value = inverse_x(rec_ref, back_ref, local, cells, wide, left)
    value = value.reshape(base_ref.shape) + base_ref[...]
    out[...] = jnp.transpose(value.astype(bf16), (2, 0, 1, 3))
    finish(*begin(sem, 0, (out, out_ref)))


def turn_kernel(
    value_ref,
    there_ref,
    w_ref,
    back_ref,
    out_ref,
    my_there_ref,
    my_w_ref,
    my_back_ref,
    value,
    out,
    sem,
):
    loads = begin(
        sem,
        0,
        (value_ref, value),
        (pick(there_ref), my_there_ref),
        (w_ref, my_w_ref),
        (pick(back_ref), my_back_ref),
    )
    finish(loads[0])
    out[...] = jnp.transpose(value[...], (2, 0, 1, 3))
    finish(*begin(sem, 4, (out, out_ref)), *loads[1:])


def write_bands(adjoint, k_ref, out, index):
    for a in range(3):
        for e in range(3):
            taps = []
            for b in range(3):
                if adjoint:
                    tap = k_ref[9 * (2 - a) + 3 * (2 - b) + 2 - e].astype(f32).T
                else:
                    tap = k_ref[9 * a + 3 * b + e].astype(f32)
                taps.append(tap)
            taps = jnp.concatenate(taps, 1)
            for z in range(4):
                pieces = [taps, jnp.zeros((CH, (5 - z) * CH), f32)]
                if z > 0:
                    pieces.insert(0, jnp.zeros((CH, z * CH), f32))
                row = jnp.concatenate(pieces, 1)
                at = (e * 4 + z) * CH
                out[index, at : at + CH, a * 8 * CH : (a + 1) * 8 * CH] = row.astype(bf16)


def x_sum(low, same, high):
    span = same.shape[1]
    lane = iota(same.shape, 1)
    before = jnp.where(lane == 0, 0.0, pltpu.roll(low, 1, axis=1))
    after = jnp.where(lane == span - 1, 0.0, pltpu.roll(high, span - 1, axis=1))
    return same + before + after


def band_conv(bands, planes):
    value = dot(bands, jnp.concatenate(planes, 0))
    size = 4 * CH
    return x_sum(value[:size], value[size : 2 * size], value[2 * size :])


def column(row_ref, copies):
    eye = iota((CH, CH), 0) == iota((CH, CH), 1)
    value = jnp.sum(jnp.where(eye, row_ref[...], 0.0), axis=1, keepdims=True)
    return jnp.concatenate([value] * copies, 0)


def block_diagonal(matrix):
    shape = (4 * CH, 4 * CH)
    wide = jnp.concatenate([matrix.astype(f32)] * 4, 1)
    tiled = jnp.concatenate([wide] * 4, 0)
    return jnp.where(iota(shape, 0) // CH == iota(shape, 1) // CH, tiled, 0.0).astype(bf16)


def pool_matrix(span):
    shape = (span, span // 2)
    return (iota(shape, 0) // 2 == iota(shape, 1)).astype(bf16)


def up_matrix(span):
    shape = (span // 2, span)
    return (iota(shape, 1) // 2 == iota(shape, 0)).astype(bf16)


def y_message_kernel(u_ref, zlo_ref, zhi_ref, low_ref, high_ref, rows, sem):
    for y in range(4):
        for z in range(3):
            rows[y, z * CH : (z + 1) * CH] = zlo_ref[y, z]
            rows[y, (z + 7) * CH : (z + 8) * CH] = zhi_ref[y, z]
        for z in range(4):
            rows[y, (z + 3) * CH : (z + 4) * CH] = u_ref[y, z]
    finish(
        *begin(sem, 0, (rows.at[pl.ds(0, 3)], low_ref), (rows.at[pl.ds(1, 3)], high_ref))
    )


def forward_conv_kernel(
    low_ref,
    high_ref,
    ylo_ref,
    yhi_ref,
    lin_ref,
    taps_fine_ref,
    taps_coarse_ref,
    bias_fine_ref,
    bias_coarse_ref,
    cot_ref,
    table_ref,
    x_ref,
    base,
    fine_ref,
    coarse,
    my_cot_ref,
    my_table_ref,
    my_x_ref,
    grid,
    taps_fine,
    taps_coarse,
    raw,
    bands,
    pooled,
    fine,
    sem,
):
    span = grid.shape[2]
    inner = pl.ds(0, 10 * CH)
    loads = begin(
        sem,
        0,
        (taps_fine_ref, taps_fine),
        (low_ref, grid.at[pl.ds(3, 3), inner]),
        (high_ref.at[pl.ds(2, 1)], grid.at[pl.ds(6, 1), inner]),
        (ylo_ref, grid.at[pl.ds(0, 3), inner]),
        (yhi_ref, grid.at[pl.ds(7, 3), inner]),
        (taps_coarse_ref, taps_coarse),
        (cot_ref, raw),
        (table_ref, my_table_ref),
        (x_ref, my_x_ref),
    )
    edges = [
        lax.axis_index("gy") > 0,
        lax.axis_index("gy") < lax.axis_size("gy") - 1,
        lax.axis_index("gz") > 0,
        lax.axis_index("gz") < lax.axis_size("gz") - 1,
    ]
    grid[:, 10 * CH :, :] = jnp.zeros((10, 2 * CH, span), bf16)
    pooled[:, 4 * CH :, :] = jnp.zeros((4, 4 * CH, span // 2), bf16)
    bias = column(bias_fine_ref, 4)
    half = 4 * CH
    row_z = iota((half, span), 0) // CH
    finish(loads[0])
    write_bands(False, taps_fine, bands, 0)
    finish(*loads[1:3])
    for y in (3, 4, 2, 1, 0, 5, 6, 7):
        if y == 2:
            finish(loads[3])
        if y == 5:
            finish(loads[4])
        y_in = None
        if y < 2:
            y_in = edges[0]
        elif y >= 6:
            y_in = edges[1]
        for h in range(2):
            at = h * half
            value = band_conv(bands[0], [grid[y + a, at : at + 8 * CH, :] for a in range(3)])
            value = jnp.maximum(value + bias, 0.0)
            inside = (row_z >= 2) | edges[2] if h == 0 else (row_z < 2) | edges[3]
            if y_in is not None:
                inside = inside & y_in
            fine[y, at : at + half, :] = jnp.where(inside, value, 0.0).astype(bf16)
    (store,) = begin(sem, 9, (fine, fine_ref))
    sums = []
    for yc in range(4):
        both = fine[2 * yc].astype(f32) + fine[2 * yc + 1].astype(f32)
        for zc in range(4):
            at = 2 * zc * CH
            sums.append(both[at : at + CH] + both[at + CH : at + 2 * CH])
    pool = pool_matrix(span)
    high, low = halves(jnp.concatenate(sums, 0))
    pools = (0.125 * (dot(high, pool) + dot(low, pool))).astype(bf16)
    pooled[:, : 4 * CH, :] = pools.reshape(4, 4 * CH, span // 2)
    bias = column(bias_coarse_ref, 4)
    finish(loads[5])
    write_bands(False, taps_coarse, bands, 1)
    planes = [jnp.concatenate([pooled[a], pooled[a + 1]], 1) for a in range(3)]
    value = dot(bands[1], jnp.concatenate(planes, 0))
    parts = [value[e * half : (e + 1) * half] for e in range(3)]
    for yc in range(2):
        at = slice(yc * span // 2, (yc + 1) * span // 2)
        value = x_sum(*[part[:, at] for part in parts])
        value = jnp.maximum(value + bias, 0.0).astype(bf16)
        coarse[yc] = value[: 2 * CH].reshape(2, CH, span // 2)
    lifted = dot(coarse[...].reshape(half, span // 2), up_matrix(span))
    lin = block_diagonal(lin_ref[...])
    for y in range(4):
        total = dot(lin, grid[y + 3, 3 * CH : 7 * CH, :])
        total = total + fine[y + 2, 2 * CH : 6 * CH, :].astype(f32)
        for z in range(4):
            at = (y // 2 * 2 + z // 2) * CH
            base[y, z] = total[z * CH : (z + 1) * CH] + lifted[at : at + CH]
    finish(loads[6])
    my_cot_ref[...] = jnp.transpose(raw[...], (1, 2, 0, 3))
    finish(store, *loads[7:])


def y_gradient_kernel(round_ref, zlo_ref, zhi_ref, kept_ref, low_ref, high_ref, own, sem):
    (load,) = begin(sem, 0, (round_ref, own))
    stores = begin(
        sem, 1, (zlo_ref, kept_ref.at[pl.ds(0, 6)]), (zhi_ref, kept_ref.at[pl.ds(6, 6)])
    )
    finish(load)
    for out_ref, y in ((low_ref, 0), (high_ref, 3)):
        out_ref[0] = zlo_ref[y]
        out_ref[1:5] = own[4 * y : 4 * y + 4]
        out_ref[5] = zhi_ref[y]
        for yc in range(2):
            out_ref[6 + 3 * yc] = zlo_ref[4 + yc]
            out_ref[7 + 3 * yc] = own[16 + yc]
            out_ref[8 + 3 * yc] = zhi_ref[4 + yc]
    finish(*stores)


def backward_kernel(
    d_ref,
    v_ref,
    grad_ref,
    round_ref,
    kept_ref,
    ylo_ref,
    yhi_ref,
    fine_ref,
    lin_ref,
    taps_fine_ref,
    taps_coarse_ref,
    table_ref,
    weight_ref,
    base,
    my_table_ref,
    weights,
    grad,
    rounded,
    kept,
    ylo,
    yhi,
    fine,
    taps_fine,
    taps_coarse,
    bands,
    coarse_grid,
    fine_grid,
    sem,
):
    loads = begin(
        sem,
        0,
        (taps_coarse_ref, taps_coarse),
        (round_ref, rounded),
        (kept_ref, kept),
        (ylo_ref, ylo),
        (yhi_ref, yhi),
        (grad_ref, grad),
        (fine_ref, fine),
        (taps_fine_ref, taps_fine),
        (table_ref, my_table_ref),
    )
    stores = put_weight_grad(d_ref, v_ref, weights, weight_ref, sem, 9)
    finish(loads[0], loads[7])
    write_bands(True, taps_coarse, bands, 1)
    write_bands(True, taps_fine, bands, 0)
    span = grad.shape[3]
    half = span // 2
    coarse_grid[:, 6 * CH :, :] = jnp.zeros((6, 2 * CH, half), bf16)
    fine_grid[:, 6 * CH :, :] = jnp.zeros((6, 2 * CH, span), bf16)

    def place(yc, pair, value):
        for zc in range(2):
            at = (2 * pair + zc) * CH
            coarse_grid[yc, at : at + CH, :] = value[:, zc * half : (zc + 1) * half]

    finish(*loads[1:5])
    for yc in range(2):
        place(2 + yc, 0, kept[4 + yc])
        place(2 + yc, 1, rounded[16 + yc])
        place(2 + yc, 2, kept[10 + yc])
        for pair in range(3):
            place(yc, pair, ylo[6 + 3 * yc + pair])
            place(4 + yc, pair, yhi[6 + 3 * yc + pair])
    pooled = [
        0.125 * band_conv(bands[1], [coarse_grid[yc + a] for a in range(3)]) for yc in range(4)
    ]
    high, low = halves(jnp.concatenate(pooled, 0))
    up = up_matrix(span)
    lifted = dot(high, up) + dot(low, up)
    finish(*loads[5:7])
    for y in range(6):
        yc = (y + 1) // 2
        for z in range(6):
            at = (4 * yc + (z + 1) // 2) * CH
            if 1 <= y <= 4 and 1 <= z <= 4:
                value = grad[y - 1, z - 1]
            elif 1 <= y <= 4:
                value = kept[y - 1 if z == 0 else y + 5].astype(f32)
            else:
                value = (ylo if y == 0 else yhi)[z].astype(f32)
            value = value + lifted[at : at + CH]
            mask = fine[y + 1, (z + 1) * CH : (z + 2) * CH, :].astype(f32) > 0
            fine_grid[y, z * CH : (z + 1) * CH, :] = jnp.where(mask, value, 0.0).astype(bf16)
    lin = block_diagonal(lin_ref[...].astype(f32).T.astype(bf16))
    for y in range(4):
        value = band_conv(bands[0], [fine_grid[y + a] for a in range(3)])
        value = value + dot(lin, rounded[4 * y : 4 * y + 4].reshape(4 * CH, span))
        base[y] = value.reshape(4, CH, span)
    finish(loads[8], *stores)


def shift(block, axis, step):
    count = lax.axis_size(axis)
    pairs = [(i, i + step) for i in range(count) if 0 <= i + step < count]
    return lax.ppermute(block, axis, pairs)


def exchange(block):
    return lax.all_to_all(block, BOTH, split_axis=0, concat_axis=0, tiled=True)


def shards(
    carbon_input_volume,
    cotangent,
    spec_weight,
    lin_weight,
    conv_fine,
    bias_fine,
    conv_coarse,
    bias_coarse,
):
    channels, rows_y, rows_z, span = carbon_input_volume.shape
    gy, gz = lax.axis_size("gy"), lax.axis_size("gz")
    devices = gy * gz
    cells = rows_y * rows_z
    local = MX // gy
    modes = (MY // gz) * MZ
    wide = local * CH
    scale = 1.0 / math.sqrt(span * cells * devices)
    there, back = mode_tables(gy, gz, rows_y, rows_z, scale)
    forward_x = jnp.asarray(x_tables(span, gy))
    inverse_table = jnp.asarray(x_back_table(span, gy, gz))

    limit = (14 << 20) + devices * (64 << 10)
    chunk = struct((devices, 2 * cells, wide), bf16)
    sent = pltpu.VMEM(chunk.shape, bf16)
    field = struct((rows_y, rows_z, CH, span))
    field_v = pltpu.VMEM(field.shape, f32)
    round_field = struct(field.shape, bf16)
    round_v = pltpu.VMEM(field.shape, bf16)
    raw = struct(carbon_input_volume.shape, bf16)
    raw_v = pltpu.VMEM(raw.shape, bf16)
    taps_v = pltpu.VMEM(conv_fine.shape, bf16)
    x_scratch = pltpu.VMEM((2 * gy * cells, wide), f32)
    wide_scratch = pltpu.VMEM((devices * 2 * cells, wide), f32)
    left_scratch = pltpu.VMEM((cells * CH, local * devices * 2), bf16)
    mode_field = struct((2 * modes, wide))
    mode_v = pltpu.VMEM(mode_field.shape, f32)
    rows = modes * CH
    packed = struct((rows, 2 * wide), bf16)
    bands_v = pltpu.VMEM((2, 12 * CH, 24 * CH), bf16)
    side = struct((rows_y, 3, CH, span), bf16)
    message = struct((6, CH, span), bf16)
    y_side = struct((3, 10 * CH, span), bf16)
    y_message = struct((12, CH, span), bf16)

    with jax.named_scope("arrive"):
        u, low, high, my_x = run(
            arrive_kernel,
            [(IN_HBM, carbon_input_volume), (IN_HBM, forward_x)],
            [
                (IN_VMEM, round_field),
                (IN_VMEM, side),
                (IN_VMEM, side),
                (IN_VMEM, struct(forward_x.shape, bf16)),
            ],
            limit,
            [raw_v],
            copies=2,
        )
    zlo = shift(high, "gz", 1)
    zhi = shift(low, "gz", -1)

    def spread(values, table, exact):
        with jax.named_scope("spread"):
            return run(
                lambda *refs: spread_kernel(exact, local, gy, gz, *refs),
                [(IN_VMEM, values), (IN_VMEM, table)],
                [(IN_HBM, chunk)],
                limit,
                [x_scratch, sent],
                copies=2,
                micros=1.2,
            )[0]

    received = exchange(spread(u, my_x, True))

    with jax.named_scope("y_message"):
        low, high = run(
            y_message_kernel,
            [(IN_VMEM, u), (IN_VMEM, zlo), (IN_VMEM, zhi)],
            [(IN_HBM, y_side), (IN_HBM, y_side)],
            limit,
            [pltpu.VMEM((rows_y, 10 * CH, span), bf16)],
            copies=2,
        )
    ylo = shift(high, "gy", 1)
    yhi = shift(low, "gy", -1)

    with jax.named_scope("setup"):
        w_high, w_low, my_there, my_back, w_kept = run(
            lambda *refs: setup_kernel(local, *refs),
            [
                (IN_HBM, spec_weight.reshape(2, local, rows, CH)),
                (IN_HBM, there),
                (IN_HBM, back),
            ],
            [
                (IN_VMEM, packed),
                (IN_VMEM, packed),
                (IN_VMEM, struct(there.shape[1:], bf16)),
                (IN_VMEM, struct(back.shape[1:], bf16)),
                (IN_HBM, packed),
            ],
            limit + (10 << 20),
            [pltpu.VMEM((2, local, rows, CH), f32)],
            copies=10,
            micros=4.5,
        )

    with jax.named_scope("mix"):
        v, send = run(
            lambda *refs: mix_kernel(local, *refs),
            [
                (IN_VMEM, received),
                (IN_VMEM, my_there),
                (IN_VMEM, w_high),
                (IN_VMEM, w_low),
                (IN_VMEM, my_back),
            ],
            [(IN_HBM, mode_field), (IN_HBM, chunk)],
            limit,
            [mode_v, sent],
            copies=5,
            micros=3,
        )
    received = exchange(send)

    with jax.named_scope("forward_convs"):
        base, fine, coarse, cot, my_inverse, my_x = run(
            forward_conv_kernel,
            [
                (IN_HBM, low),
                (IN_HBM, high),
                (IN_HBM, ylo),
                (IN_HBM, yhi),
                (IN_VMEM, lin_weight),
                (IN_HBM, conv_fine),
                (IN_HBM, conv_coarse),
                (IN_VMEM, bias_fine[None]),
                (IN_VMEM, bias_coarse[None]),
                (IN_HBM, cotangent),
                (IN_HBM, inverse_table),
                (IN_HBM, forward_x),
            ],
            [
                (IN_VMEM, field),
                (IN_HBM, struct((8, 8 * CH, span), bf16)),
                (IN_VMEM, struct((2, 2, CH, span // 2), bf16)),
                (IN_VMEM, round_field),
                (IN_VMEM, struct(inverse_table.shape, bf16)),
                (IN_VMEM, struct(forward_x.shape, bf16)),
            ],
            limit,
            [
                pltpu.VMEM((10, 12 * CH, span), bf16),
                taps_v,
                taps_v,
                raw_v,
                bands_v,
                pltpu.VMEM((4, 8 * CH, span // 2), bf16),
                pltpu.VMEM((8, 8 * CH, span), bf16),
            ],
            copies=10,
            micros=7,
        )

    with jax.named_scope("middle"):
        activated, grad, grad_kept, grad_round, low, high = run(
            lambda *refs: middle_kernel(local, *refs),
            [
                (IN_VMEM, received),
                (IN_VMEM, my_inverse),
                (IN_VMEM, base),
                (IN_VMEM, cot),
                (IN_VMEM, coarse),
            ],
            [
                (IN_HBM, round_field),
                (IN_VMEM, field),
                (IN_HBM, field),
                (IN_HBM, struct((cells + 2, CH, span), bf16)),
                (IN_VMEM, message),
                (IN_VMEM, message),
            ],
            limit,
            [
                round_v,
                pltpu.VMEM((cells + 2, CH, span), bf16),
                wide_scratch,
                left_scratch,
            ],
            copies=3,
            micros=2,
        )
    zlo = shift(high, "gz", 1)
    zhi = shift(low, "gz", -1)
    received = exchange(spread(grad, my_x, False))

    with jax.named_scope("y_gradient"):
        kept_z, low, high = run(
            y_gradient_kernel,
            [(IN_HBM, grad_round), (IN_VMEM, zlo), (IN_VMEM, zhi)],
            [(IN_HBM, y_message), (IN_VMEM, y_message), (IN_VMEM, y_message)],
            limit,
            [pltpu.VMEM((cells + 2, CH, span), bf16)],
            copies=3,
            micros=20,
        )
    ylo = shift(high, "gy", 1)
    yhi = shift(low, "gy", -1)
    with jax.named_scope("turn"):
        predicted, my_there, my_w, my_back = run(
            turn_kernel,
            [(IN_HBM, activated), (IN_HBM, there), (IN_HBM, w_kept), (IN_HBM, back)],
            [
                (IN_HBM, raw),
                (IN_VMEM, struct(there.shape[1:], bf16)),
                (IN_VMEM, packed),
                (IN_VMEM, struct(back.shape[1:], bf16)),
            ],
            limit,
            [round_v, raw_v],
            copies=5,
            micros=2,
        )

    with jax.named_scope("mix_adjoint"):
        d, send = run(
            lambda *refs: adjoint_kernel(local, *refs),
            [(IN_VMEM, received), (IN_VMEM, my_there), (IN_VMEM, my_w), (IN_VMEM, my_back)],
            [(IN_VMEM, mode_field), (IN_HBM, chunk)],
            limit,
            [sent],
            copies=4,
            micros=2,
        )
    received = exchange(send)

    with jax.named_scope("backward"):
        weight_grad, base, my_inverse = run(
            backward_kernel,
            [
                (IN_VMEM, d),
                (IN_VMEM, v),
                (IN_HBM, grad_kept),
                (IN_HBM, grad_round),
                (IN_HBM, kept_z),
                (IN_HBM, ylo),
                (IN_HBM, yhi),
                (IN_HBM, fine),
                (IN_VMEM, lin_weight),
                (IN_HBM, conv_fine),
                (IN_HBM, conv_coarse),
                (IN_HBM, inverse_table),
            ],
            [
                (IN_HBM, struct((2, local, rows, CH))),
                (IN_VMEM, field),
                (IN_VMEM, struct(inverse_table.shape, bf16)),
            ],
            limit + (10 << 20),
            [
                pltpu.VMEM((2, local, rows, CH), f32),
                field_v,
                pltpu.VMEM((cells + 2, CH, span), bf16),
                pltpu.VMEM(y_message.shape, bf16),
                pltpu.VMEM(y_message.shape, bf16),
                pltpu.VMEM(y_message.shape, bf16),
                pltpu.VMEM((8, 8 * CH, span), bf16),
                taps_v,
                taps_v,
                bands_v,
                pltpu.VMEM((6, 8 * CH, span // 2), bf16),
                pltpu.VMEM((6, 8 * CH, span), bf16),
            ],
            copies=9 + local,
            micros=6,
        )
    weight_grad = weight_grad.reshape(spec_weight.shape)

    with jax.named_scope("last"):
        (sensitivity,) = run(
            lambda *refs: last_kernel(local, *refs),
            [(IN_VMEM, received), (IN_VMEM, my_inverse), (IN_VMEM, base)],
            [(IN_HBM, raw)],
            limit,
            [raw_v, wide_scratch, left_scratch],
            copies=1,
            micros=2,
        )
    return (predicted, sensitivity, weight_grad)


def solution(mesh):
    field = P(None, "gy", "gz", None)
    modes = P(None, "gy", "gz", None, None, None)
    return jax.shard_map(
        shards,
        mesh=mesh,
        in_specs=(field, field, modes, P(), P(), P(), P(), P()),
        out_specs=(field, field, modes),
        check_vma=False,
    )
```

```python
import math

import jax
import jax.numpy as jnp
import ml_dtypes
import numpy as np
from jax import lax
from jax.experimental import pallas as pl
from jax.experimental.pallas import tpu as pltpu
from jax.sharding import PartitionSpec as P

MX = 32
MY = 32
MZ = 8
CH = 32
BOTH = ("gy", "gz")

f32 = jnp.float32
bf16 = jnp.bfloat16
root_coef = math.sqrt(2.0 / math.pi)
NN = (((1,), (0,)), ((), ()))
NT = (((1,), (1,)), ((), ()))
TN = (((0,), (0,)), ((), ()))


def dot(a, b, form=NN):
    return lax.dot_general(a, b, form, preferred_element_type=f32)


def halves(value):
    high = value.astype(bf16)
    return high, (value - high.astype(f32)).astype(bf16)


def iota(shape, dim):
    return lax.broadcasted_iota(jnp.int32, shape, dim)


IN_VMEM = pl.BlockSpec(memory_space=pltpu.VMEM)
IN_HBM = pl.BlockSpec(memory_space=pltpu.HBM)


def struct(shape, kind=f32):
    return jax.ShapeDtypeStruct(shape, kind)


def run(kernel, ins, outs, limit, scratch=(), micros=1.0, copies=0, **grid):
    scratch = list(scratch)
    if copies:
        scratch.append(pltpu.SemaphoreType.DMA((copies,)))
    held = {id(IN_HBM): pltpu.HBM, id(IN_VMEM): pltpu.VMEM}

    def placed(spec, array):
        if id(spec) in held:
            return pltpu.with_memory_space_constraint(array, held[id(spec)])
        return array

    def shaped(spec, shape):
        if id(spec) in held:
            return held[id(spec)](shape.shape, shape.dtype)
        return shape

    return pl.pallas_call(
        kernel,
        in_specs=[spec for spec, _ in ins],
        out_specs=[spec for spec, _ in outs],
        out_shape=[shaped(spec, shape) for spec, shape in outs],
        scratch_shapes=scratch,
        compiler_params=pltpu.CompilerParams(vmem_limit_bytes=limit),
        cost_estimate=pl.CostEstimate(
            flops=int(micros * 1.1e9), bytes_accessed=1 << 16, transcendentals=0
        ),
        **grid,
    )(*[placed(spec, array) for spec, array in ins])


def begin(sem, first, *pairs):
    copies = [
        pltpu.make_async_copy(source, target, sem.at[first + i])
        for i, (source, target) in enumerate(pairs)
    ]
    for copy in copies:
        copy.start()
    return copies


def finish(*copies):
    for copy in copies:
        copy.wait()


def kept(count, length):
    position = np.arange(count)
    return np.where(position < count // 2, position, length - count + position)


def split_np(table):
    high = table.astype(ml_dtypes.bfloat16)
    return high, (table - high.astype(np.float64)).astype(ml_dtypes.bfloat16)


def x_tables(cells_x, blocks):
    local = MX // blocks
    freqs = kept(MX, cells_x).reshape(blocks, local).T
    angles = 2.0 * np.pi * ((freqs[:, :, None] * np.arange(cells_x)) % cells_x) / cells_x
    table = np.stack([np.cos(angles), -np.sin(angles)], axis=2).reshape(2 * MX, cells_x)
    return np.concatenate(split_np(table), axis=0)


def x_back_table(cells_x, gy, gz):
    local = MX // gy
    freqs = kept(MX, cells_x).reshape(gy, local).T
    angles = 2.0 * np.pi * ((freqs[:, :, None] * np.arange(cells_x)) % cells_x) / cells_x
    table = np.stack([np.cos(angles), -np.sin(angles)], axis=2)
    table = np.broadcast_to(table[:, :, None], (local, gy, gz, 2, cells_x))
    return np.concatenate(split_np(table.reshape(-1, cells_x)), axis=0)


def yz_angles(xp, freqs_y, gy, gz, rows_y, rows_z):
    span_y, span_z = gy * rows_y, gz * rows_z
    phase_y = (freqs_y[:, None] * xp.arange(span_y)[None]) % span_y
    phase_z = (xp.arange(MZ)[:, None] * xp.arange(span_z)[None]) % span_z
    phase_y = phase_y.reshape(-1, 1, gy, 1, rows_y, 1)
    phase_z = phase_z.reshape(1, MZ, 1, gz, 1, rows_z)
    turn = (phase_y * span_z + phase_z * span_y) % (span_y * span_z)
    return turn.reshape(turn.shape[0] * MZ, gy * gz, rows_y * rows_z)


def yz_table(xp, freqs_y, gy, gz, rows_y, rows_z):
    cells = gy * gz * rows_y * rows_z
    turn = yz_angles(xp, freqs_y, gy, gz, rows_y, rows_z)
    angles = 2.0 * math.pi / cells * turn
    cosine, sine = xp.cos(angles), xp.sin(angles)
    table = xp.stack([xp.stack([cosine, sine], 2), xp.stack([-sine, cosine], 2)], 0)
    return table.reshape(2 * turn.shape[0], -1)


def mode_tables(gy, gz, rows_y, rows_z, scale):
    local = MY // gz
    cells = gy * gz * rows_y * rows_z
    freqs = kept(MY, gy * rows_y).reshape(gz, local)
    if gz * 2 * local * MZ * 2 * cells <= 1 << 20:
        there, back = [], []
        for block in range(gz):
            high, low = split_np(scale * yz_table(np, freqs[block], gy, gz, rows_y, rows_z))
            there.append(np.concatenate([high, low], 0))
            back.append(np.concatenate([high.T, low.T], 1))
        return jnp.asarray(np.stack(there)), jnp.asarray(np.stack(back))
    where = lax.axis_index("gz")
    mine = lax.dynamic_index_in_dim(jnp.asarray(freqs, jnp.int32), where, keepdims=False)
    high, low = halves(scale * yz_table(jnp, mine, gy, gz, rows_y, rows_z).astype(f32))
    return jnp.concatenate([high, low], 0)[None], jnp.concatenate([high.T, low.T], 1)[None]


def put_x_modes(product, local, blocks, copies, cells, scratch, sent, send_ref, sem, first):
    rows = 2 * blocks
    for cell in range(cells):
        piece = product[:, cell * CH : (cell + 1) * CH]
        value = jnp.concatenate([piece[k * rows : (k + 1) * rows] for k in range(local)], axis=1)
        scratch[pl.ds(cell, rows, stride=cells), :] = value
    moves = []
    half = blocks // 2
    for block in range(blocks):
        value = scratch[block * 2 * cells : (block + 1) * 2 * cells].astype(bf16)
        for copy in range(copies):
            sent[block * copies + copy] = value
        if (block + 1) % half == 0:
            part = pl.ds((block + 1 - half) * copies, half * copies)
            moves += begin(sem, first + len(moves), (sent.at[part], send_ref.at[part]))
    return moves


def odd(axis):
    return lax.axis_index(axis) & 1


def first(axis):
    return lax.axis_index(axis) == 0


def last(axis):
    return lax.axis_index(axis) == lax.axis_size(axis) - 1


def arrive_kernel(raw_ref, table_ref, u_ref, one_ref, two_ref, my_table_ref, raw, sem):
    loads = begin(sem, 0, (raw_ref, raw), (table_ref, my_table_ref))
    finish(*loads)
    u = jnp.transpose(raw[...], (1, 2, 0, 3))
    u_ref[...] = u
    side = odd("gz")
    one_ref[...] = u_ref[:, pl.ds(1 - side, 3)]
    two_ref[...] = u_ref[:, pl.ds(side, 3)]


def spread_kernel(
    exact, local, blocks, copies, u_ref, table, send_ref, scratch, sent, sem
):
    cells = u_ref.shape[0] * u_ref.shape[1]
    u = u_ref[...].reshape(cells * CH, -1)
    if exact:
        both = dot(table[...], u, NT)
        product = both[: 2 * MX] + both[2 * MX :]
    else:
        high, low = halves(u)
        both = dot(table[...], high, NT)
        product = both[: 2 * MX] + both[2 * MX :] + dot(table[: 2 * MX], low, NT)
    finish(*put_x_modes(product, local, blocks, copies, cells, scratch, sent, send_ref, sem, 0))


def pick(tables_ref):
    if tables_ref.shape[0] == 1:
        return tables_ref.at[0]
    return tables_ref.at[lax.axis_index("gz")]


def mode_values(rec_ref, there, rows):
    both = dot(there[...], rec_ref[...].reshape(-1, rec_ref.shape[2]))
    return both[:rows] + both[rows:]


def put_back(values, back_ref, sent, send_ref, sem, first):
    high, low = halves(values)
    twice = jnp.concatenate([high, high], 0)
    rows = values.shape[0]
    devices, depth, wide = sent.shape
    part = devices // 4
    moves = []
    for step in range(4):
        at = slice(step * part * depth, (step + 1) * part * depth)
        result = dot(back_ref[at], twice) + dot(back_ref[at, :rows], low)
        sent[step * part : (step + 1) * part] = result.astype(bf16).reshape(part, depth, wide)
        span = pl.ds(step * part, part)
        moves += begin(sem, first + step, (sent.at[span], send_ref.at[span]))
    finish(*moves)


def kz_weight(shape):
    return jnp.where(iota(shape, 0) % MZ == 0, 1.0, 2.0).astype(f32)


def same_mode(rows, lanes):
    return (iota((rows, lanes), 0) % MZ) == ((iota((rows, lanes), 1) // CH) % MZ)


def mix_kernel(
    local,
    rec_ref,
    there_ref,
    high_ref,
    low_ref,
    back_ref,
    v_ref,
    send_ref,
    kept_v,
    sent,
    sem,
):
    rows = there_ref.shape[0] // 2
    modes = rows // 2
    wide = local * CH
    v = mode_values(rec_ref, there_ref, rows)
    kept_v[...] = v
    store = begin(sem, 0, (kept_v, v_ref))
    real, imag = v[:modes], v[modes:]
    pair = (
        jnp.concatenate([real, -imag], 1),
        jnp.concatenate([imag, real], 1),
    )
    lane_k = (iota((MZ, 2 * wide), 1) // CH) % local
    size = MZ * CH
    diag = same_mode(2 * MZ * local, size)
    placed = [[[None] * (modes // MZ) for _ in range(local)] for _ in range(2)]
    for g in range(modes // MZ):
        pieces = []
        for k in range(local):
            for part in range(2):
                piece = pair[part][g * MZ : (g + 1) * MZ]
                pieces.append(jnp.where(lane_k == k, piece, 0.0))
        left_high, left_low = halves(jnp.concatenate(pieces, 0))
        w_high = high_ref[g * size : (g + 1) * size]
        w_low = low_ref[g * size : (g + 1) * size]
        count = left_high.shape[0]
        both = dot(jnp.concatenate([left_high, left_low], 0), w_high, NT)
        value = both[:count] + both[count:] + dot(left_high, w_low, NT)
        value = jnp.where(diag, value, 0.0)
        for k in range(local):
            for part in range(2):
                at = (2 * k + part) * MZ
                placed[part][k][g] = value[at : at + MZ]
    columns = [jnp.concatenate(placed[0][k] + placed[1][k], 0) for k in range(local)]
    all_values = jnp.concatenate(columns, 1)
    shape = (local * size, wide)
    fold = (iota(shape, 0) // size == iota(shape, 1) // CH) & (
        iota(shape, 0) % CH == iota(shape, 1) % CH
    )
    fold = fold.astype(bf16)
    high, low = halves(all_values)
    mixed = dot(high, fold) + dot(low, fold)
    put_back(mixed * kz_weight(mixed.shape), back_ref, sent, send_ref, sem, 1)
    finish(*store)


def adjoint_kernel(
    local,
    rec_ref,
    there_ref,
    high_ref,
    back_ref,
    d_ref,
    send_ref,
    sent,
    sem,
):
    rows = there_ref.shape[0] // 2
    modes = rows // 2
    wide = local * CH
    size = MZ * CH
    d = mode_values(rec_ref, there_ref, rows)
    d = d * kz_weight(d.shape)
    d_ref[...] = d
    shape = (wide, local * size)
    rep = (iota(shape, 1) // size == iota(shape, 0) // CH) & (
        iota(shape, 1) % CH == iota(shape, 0) % CH
    )
    rep = rep.astype(bf16)
    high, low = halves(d)
    spread = dot(high, rep) + dot(low, rep)
    spread = jnp.where(same_mode(rows, local * size), spread, 0.0)
    lane_k = (iota((2 * MZ, 2 * wide), 1) // CH) % local
    parts = ([], [])
    for g in range(modes // MZ):
        pieces = []
        for k in range(local):
            for part in range(2):
                at = part * modes + g * MZ
                pieces.append(spread[at : at + MZ, k * size : (k + 1) * size])
        left_high, left_low = halves(jnp.concatenate(pieces, 0))
        count = left_high.shape[0]
        both = dot(
            jnp.concatenate([left_high, left_low], 0), high_ref[g * size : (g + 1) * size]
        )
        value = both[:count] + both[count:]
        total = None
        for k in range(local):
            piece = jnp.where(lane_k == k, value[2 * k * MZ : 2 * (k + 1) * MZ], 0.0)
            total = piece if total is None else total + piece
        parts[0].append(total[:MZ])
        parts[1].append(total[MZ:])
    real = jnp.concatenate(parts[0], 0)
    imag = jnp.concatenate(parts[1], 0)
    value = jnp.concatenate(
        [real[:, :wide] + imag[:, wide:], imag[:, :wide] - real[:, wide:]], 0
    )
    put_back(value, back_ref, sent, send_ref, sem, 0)


def setup_kernel(
    local,
    w_ref,
    there_ref,
    back_ref,
    high_ref,
    low_ref,
    my_there_ref,
    my_back_ref,
    kept_ref,
    w,
    sem,
):
    parts = 4
    rows = w.shape[2] // parts
    spans = [pl.ds(step * rows, rows) for step in range(parts)]
    loads = begin(sem, 0, *[(w_ref.at[:, :, span], w.at[:, :, span]) for span in spans])
    tables = begin(
        sem, parts, (pick(there_ref), my_there_ref), (pick(back_ref), my_back_ref)
    )
    stores = []
    for step in range(parts):
        at = slice(step * rows, (step + 1) * rows)
        finish(loads[step])
        pieces = [w[part, k, at] for part in range(2) for k in range(local)]
        high_ref[at], low_ref[at] = halves(jnp.concatenate(pieces, 1))
        stores += begin(sem, parts + 2 + step, (high_ref.at[spans[step]], kept_ref.at[spans[step]]))
    finish(*tables, *stores)


def put_weight_grad(d_ref, v_ref, out, out_ref, sem, first):
    rows, wide = d_ref.shape
    modes = rows // 2
    size = MZ * CH
    keep = same_mode(rows, size)
    d_halves = halves(d_ref[...])
    v_halves = halves(v_ref[...])
    stores = []
    for k in range(wide // CH):
        shape = (wide, size)
        rep = (iota(shape, 0) == k * CH + iota(shape, 1) % CH).astype(bf16)
        d_high, d_low = [jnp.where(keep, dot(value, rep), 0.0) for value in d_halves]
        at = slice(k * CH, (k + 1) * CH)
        v_high, v_low = [value[:, at].astype(f32) for value in v_halves]
        for g in range(modes // MZ):
            real = slice(g * MZ, (g + 1) * MZ)
            imag = slice(modes + g * MZ, modes + (g + 1) * MZ)
            left = jnp.concatenate(
                [d_high[real], d_high[imag], d_low[real], d_low[imag], d_high[real], d_high[imag]],
                0,
            ).astype(bf16)
            for part in range(2):
                rights = []
                for v in (v_high, v_high, v_low):
                    rights += [v[real], v[imag]] if part == 0 else [-v[imag], v[real]]
                right = jnp.concatenate(rights, 0).astype(bf16)
                out[part, k, g * size : (g + 1) * size, :] = dot(left, right, TN)
        stores += begin(sem, first + k, (out.at[:, k], out_ref.at[:, k]))
    return stores


def inverse_x(rec_ref, table, local, cells, wide, left):
    wide[...] = rec_ref[...].reshape(-1, rec_ref.shape[2]).astype(f32)
    rows = wide.shape[0] // cells
    for cell in range(cells):
        turned = wide[pl.ds(cell, rows, stride=cells), :].T.astype(bf16)
        for k in range(local):
            left[cell * CH : (cell + 1) * CH, k * rows : (k + 1) * rows] = turned[
                k * CH : (k + 1) * CH
            ]
    depth = local * rows
    value = left[...]
    return dot(value, table[:depth]) + dot(value, table[depth:])


def gelu_pair(pre_act):
    cube_term = pre_act * pre_act * pre_act
    tanh_result = jnp.tanh(root_coef * (pre_act + 0.044715 * cube_term))
    activated_output = 0.5 * pre_act * (1.0 + tanh_result)
    gelu_slope = 0.5 * (1.0 + tanh_result) + 0.5 * pre_act * (
        1.0 - tanh_result * tanh_result
    ) * root_coef * (1.0 + 3.0 * 0.044715 * pre_act * pre_act)
    return (activated_output, gelu_slope)


def middle_kernel(
    local,
    rec_ref,
    back_ref,
    base_ref,
    cot_ref,
    coarse_ref,
    out_ref,
    grad_ref,
    kept_ref,
    round_ref,
    one_ref,
    two_ref,
    out,
    rounded,
    wide,
    left,
    sem,
):
    rows_y, rows_z, _, span = base_ref.shape
    cells = rows_y * rows_z
    pre_act = inverse_x(rec_ref, back_ref, local, cells, wide, left)
    pre_act = pre_act + base_ref[...].reshape(pre_act.shape)
    activated, slope = gelu_pair(pre_act)
    out[...] = activated.astype(bf16).reshape(out.shape)
    value = cot_ref[...].astype(f32).reshape(pre_act.shape) * slope
    grad_ref[...] = value.reshape(grad_ref.shape)
    stores = begin(sem, 0, (out, out_ref), (grad_ref, kept_ref))
    rounded[:cells] = value.astype(bf16).reshape(cells, CH, span)
    side = odd("gz")
    for y in range(rows_y):
        one_ref[y] = rounded[rows_z * y + (rows_z - 1) * (1 - side)]
        two_ref[y] = rounded[rows_z * y + (rows_z - 1) * side]
    pool = pool_matrix(span)
    for yc in range(2):
        sums = []
        for zc in range(2):
            y, z = 2 * yc, 2 * zc
            sums.append(
                grad_ref[y, z] + grad_ref[y, z + 1] + grad_ref[y + 1, z] + grad_ref[y + 1, z + 1]
            )
        total_high, total_low = halves(jnp.concatenate(sums, 0))
        total = dot(total_high, pool) + dot(total_low, pool)
        pieces = []
        for zc in range(2):
            piece = total[zc * CH : (zc + 1) * CH]
            pieces.append(jnp.where(coarse_ref[yc, zc].astype(f32) > 0, piece, 0.0))
        piece = jnp.concatenate(pieces, 1).astype(bf16)
        rounded[cells + yc] = piece
        one_ref[rows_y + yc] = piece
        two_ref[rows_y + yc] = piece
    finish(*begin(sem, 2, (rounded, round_ref)), *stores)


def last_kernel(local, rec_ref, back_ref, base_ref, out_ref, out, wide, left, sem):
    cells = base_ref.shape[0] * base_ref.shape[1]
    value = inverse_x(rec_ref, back_ref, local, cells, wide, left)
    value = value.reshape(base_ref.shape) + base_ref[...]
    out[...] = jnp.transpose(value.astype(bf16), (2, 0, 1, 3))
    finish(*begin(sem, 0, (out, out_ref)))


def turn_kernel(
    value_ref,
    there_ref,
    w_ref,
    back_ref,
    out_ref,
    my_there_ref,
    my_w_ref,
    my_back_ref,
    value,
    out,
    sem,
):
    loads = begin(
        sem,
        0,
        (value_ref, value),
        (pick(there_ref), my_there_ref),
        (w_ref, my_w_ref),
        (pick(back_ref), my_back_ref),
    )
    finish(loads[0])
    out[...] = jnp.transpose(value[...], (2, 0, 1, 3))
    finish(*begin(sem, 4, (out, out_ref)), *loads[1:])


def write_bands(adjoint, k_ref, out, index):
    for a in range(3):
        for e in range(3):
            taps = []
            for b in range(3):
                if adjoint:
                    tap = k_ref[9 * (2 - a) + 3 * (2 - b) + 2 - e].astype(f32).T
                else:
                    tap = k_ref[9 * a + 3 * b + e].astype(f32)
                taps.append(tap)
            taps = jnp.concatenate(taps, 1)
            for z in range(4):
                pieces = [taps, jnp.zeros((CH, (5 - z) * CH), f32)]
                if z > 0:
                    pieces.insert(0, jnp.zeros((CH, z * CH), f32))
                row = jnp.concatenate(pieces, 1)
                at = (e * 4 + z) * CH
                out[index, at : at + CH, a * 8 * CH : (a + 1) * 8 * CH] = row.astype(bf16)


def x_sum(low, same, high):
    span = same.shape[1]
    lane = iota(same.shape, 1)
    before = jnp.where(lane == 0, 0.0, pltpu.roll(low, 1, axis=1))
    after = jnp.where(lane == span - 1, 0.0, pltpu.roll(high, span - 1, axis=1))
    return same + before + after


def band_conv(bands, planes):
    value = dot(bands, jnp.concatenate(planes, 0))
    size = 4 * CH
    return x_sum(value[:size], value[size : 2 * size], value[2 * size :])


def column(row_ref, copies):
    eye = iota((CH, CH), 0) == iota((CH, CH), 1)
    value = jnp.sum(jnp.where(eye, row_ref[...], 0.0), axis=1, keepdims=True)
    return jnp.concatenate([value] * copies, 0)


def block_diagonal(matrix):
    shape = (4 * CH, 4 * CH)
    wide = jnp.concatenate([matrix.astype(f32)] * 4, 1)
    tiled = jnp.concatenate([wide] * 4, 0)
    return jnp.where(iota(shape, 0) // CH == iota(shape, 1) // CH, tiled, 0.0).astype(bf16)


def pool_matrix(span):
    shape = (span, span // 2)
    return (iota(shape, 0) // 2 == iota(shape, 1)).astype(bf16)


def up_matrix(span):
    shape = (span // 2, span)
    return (iota(shape, 1) // 2 == iota(shape, 0)).astype(bf16)


def y_message_kernel(u_ref, z_one_ref, z_two_ref, one_ref, two_ref, rows, sem):
    side = odd("gz")
    for y in range(4):
        for z in range(3):
            at = pl.multiple_of((7 * (1 - side) + z) * CH, CH)
            rows[y, pl.ds(at, CH)] = z_one_ref[y, z]
            at = pl.multiple_of((7 * side + z) * CH, CH)
            rows[y, pl.ds(at, CH)] = z_two_ref[y, z]
        for z in range(4):
            rows[y, (z + 3) * CH : (z + 4) * CH] = u_ref[y, z]
    blank = jnp.zeros((4, 3 * CH, rows.shape[2]), bf16)

    @pl.when(first("gz"))
    def low_end():
        rows[:, : 3 * CH] = blank

    @pl.when(last("gz"))
    def high_end():
        rows[:, 7 * CH :] = blank

    side = odd("gy")
    finish(
        *begin(
            sem, 0, (rows.at[pl.ds(1 - side, 3)], one_ref), (rows.at[pl.ds(side, 3)], two_ref)
        )
    )


def forward_conv_kernel(
    own_one_ref,
    own_two_ref,
    y_one_ref,
    y_two_ref,
    lin_ref,
    taps_fine_ref,
    taps_coarse_ref,
    bias_fine_ref,
    bias_coarse_ref,
    cot_ref,
    table_ref,
    x_ref,
    base,
    fine_ref,
    coarse,
    my_cot_ref,
    my_table_ref,
    my_x_ref,
    grid,
    taps_fine,
    taps_coarse,
    raw,
    bands,
    pooled,
    fine,
    sem,
):
    span = grid.shape[2]
    inner = pl.ds(0, 10 * CH)
    side = odd("gy")
    loads = begin(
        sem,
        0,
        (taps_fine_ref, taps_fine),
        (own_one_ref, grid.at[pl.ds(4 - side, 3), inner]),
        (own_two_ref.at[pl.ds(2 * side, 1)], grid.at[pl.ds(3 + 3 * side, 1), inner]),
        (y_one_ref, grid.at[pl.ds(7 * (1 - side), 3), inner]),
        (y_two_ref, grid.at[pl.ds(7 * side, 3), inner]),
        (taps_coarse_ref, taps_coarse),
        (cot_ref, raw),
        (table_ref, my_table_ref),
        (x_ref, my_x_ref),
    )
    edges = [jnp.logical_not(end(axis)) for axis in ("gy", "gz") for end in (first, last)]
    grid[:, 10 * CH :, :] = jnp.zeros((10, 2 * CH, span), bf16)
    pooled[:, 4 * CH :, :] = jnp.zeros((4, 4 * CH, span // 2), bf16)
    bias = column(bias_fine_ref, 4)
    half = 4 * CH
    row_z = iota((half, span), 0) // CH
    finish(loads[0])
    write_bands(False, taps_fine, bands, 0)
    finish(*loads[1:3])
    for y in (3, 4, 2, 1, 0, 5, 6, 7):
        if y == 2:
            finish(loads[3], loads[4])

            @pl.when(first("gy"))
            def low_end():
                grid[:3] = jnp.zeros((3, 12 * CH, span), bf16)

            @pl.when(last("gy"))
            def high_end():
                grid[7:] = jnp.zeros((3, 12 * CH, span), bf16)

        y_in = None
        if y < 2:
            y_in = edges[0]
        elif y >= 6:
            y_in = edges[1]
        for h in range(2):
            at = h * half
            value = band_conv(bands[0], [grid[y + a, at : at + 8 * CH, :] for a in range(3)])
            value = jnp.maximum(value + bias, 0.0)
            inside = (row_z >= 2) | edges[2] if h == 0 else (row_z < 2) | edges[3]
            if y_in is not None:
                inside = inside & y_in
            fine[y, at : at + half, :] = jnp.where(inside, value, 0.0).astype(bf16)
    (store,) = begin(sem, 9, (fine, fine_ref))
    sums = []
    for yc in range(4):
        both = fine[2 * yc].astype(f32) + fine[2 * yc + 1].astype(f32)
        for zc in range(4):
            at = 2 * zc * CH
            sums.append(both[at : at + CH] + both[at + CH : at + 2 * CH])
    pool = pool_matrix(span)
    high, low = halves(jnp.concatenate(sums, 0))
    pools = (0.125 * (dot(high, pool) + dot(low, pool))).astype(bf16)
    pooled[:, : 4 * CH, :] = pools.reshape(4, 4 * CH, span // 2)
    bias = column(bias_coarse_ref, 4)
    finish(loads[5])
    write_bands(False, taps_coarse, bands, 1)
    planes = [jnp.concatenate([pooled[a], pooled[a + 1]], 1) for a in range(3)]
    value = dot(bands[1], jnp.concatenate(planes, 0))
    parts = [value[e * half : (e + 1) * half] for e in range(3)]
    for yc in range(2):
        at = slice(yc * span // 2, (yc + 1) * span // 2)
        value = x_sum(*[part[:, at] for part in parts])
        value = jnp.maximum(value + bias, 0.0).astype(bf16)
        coarse[yc] = value[: 2 * CH].reshape(2, CH, span // 2)
    lifted = dot(coarse[...].reshape(half, span // 2), up_matrix(span))
    lin = block_diagonal(lin_ref[...])
    for y in range(4):
        total = dot(lin, grid[y + 3, 3 * CH : 7 * CH, :])
        total = total + fine[y + 2, 2 * CH : 6 * CH, :].astype(f32)
        for z in range(4):
            at = (y // 2 * 2 + z // 2) * CH
            base[y, z] = total[z * CH : (z + 1) * CH] + lifted[at : at + CH]
    finish(loads[6])
    my_cot_ref[...] = jnp.transpose(raw[...], (1, 2, 0, 3))
    finish(store, *loads[7:])


def y_gradient_kernel(
    round_ref, z_one_ref, z_two_ref, kept_ref, one_ref, two_ref, own, halo, sem
):
    (load,) = begin(sem, 0, (round_ref, own))
    side = odd("gz")
    halo[1 - side] = z_one_ref[...]
    halo[side] = z_two_ref[...]

    @pl.when(first("gz"))
    def low_end():
        halo[0] = jnp.zeros(halo.shape[1:], bf16)

    @pl.when(last("gz"))
    def high_end():
        halo[1] = jnp.zeros(halo.shape[1:], bf16)

    (store,) = begin(sem, 1, (halo, kept_ref))
    finish(load)
    side = odd("gy")
    for out_ref, y in ((one_ref, 3 * (1 - side)), (two_ref, 3 * side)):
        out_ref[0] = halo[0, y]
        out_ref[1:5] = own[pl.ds(4 * y, 4)]
        out_ref[5] = halo[1, y]
        for yc in range(2):
            out_ref[6 + 3 * yc] = halo[0, 4 + yc]
            out_ref[7 + 3 * yc] = own[16 + yc]
            out_ref[8 + 3 * yc] = halo[1, 4 + yc]
    finish(store)


def backward_kernel(
    d_ref,
    v_ref,
    grad_ref,
    round_ref,
    kept_ref,
    y_one_ref,
    y_two_ref,
    fine_ref,
    lin_ref,
    taps_fine_ref,
    taps_coarse_ref,
    table_ref,
    weight_ref,
    base,
    my_table_ref,
    weights,
    grad,
    rounded,
    kept,
    beside,
    fine,
    taps_fine,
    taps_coarse,
    bands,
    coarse_grid,
    fine_grid,
    sem,
):
    side = odd("gy")
    loads = begin(
        sem,
        0,
        (taps_coarse_ref, taps_coarse),
        (round_ref, rounded),
        (kept_ref, kept),
        (y_one_ref, beside.at[1 - side]),
        (y_two_ref, beside.at[side]),
        (grad_ref, grad),
        (fine_ref, fine),
        (taps_fine_ref, taps_fine),
        (table_ref, my_table_ref),
    )
    stores = put_weight_grad(d_ref, v_ref, weights, weight_ref, sem, 9)
    finish(loads[0], loads[7])
    write_bands(True, taps_coarse, bands, 1)
    write_bands(True, taps_fine, bands, 0)
    span = grad.shape[3]
    half = span // 2
    coarse_grid[:, 6 * CH :, :] = jnp.zeros((6, 2 * CH, half), bf16)
    fine_grid[:, 6 * CH :, :] = jnp.zeros((6, 2 * CH, span), bf16)

    def place(yc, pair, value):
        for zc in range(2):
            at = (2 * pair + zc) * CH
            coarse_grid[yc, at : at + CH, :] = value[:, zc * half : (zc + 1) * half]

    finish(*loads[1:5])

    @pl.when(first("gy"))
    def low_end():
        beside[0] = jnp.zeros(beside.shape[1:], bf16)

    @pl.when(last("gy"))
    def high_end():
        beside[1] = jnp.zeros(beside.shape[1:], bf16)

    for yc in range(2):
        place(2 + yc, 0, kept[0, 4 + yc])
        place(2 + yc, 1, rounded[16 + yc])
        place(2 + yc, 2, kept[1, 4 + yc])
        for pair in range(3):
            place(yc, pair, beside[0, 6 + 3 * yc + pair])
            place(4 + yc, pair, beside[1, 6 + 3 * yc + pair])
    pooled = [
        0.125 * band_conv(bands[1], [coarse_grid[yc + a] for a in range(3)]) for yc in range(4)
    ]
    high, low = halves(jnp.concatenate(pooled, 0))
    up = up_matrix(span)
    lifted = dot(high, up) + dot(low, up)
    finish(*loads[5:7])
    for y in range(6):
        yc = (y + 1) // 2
        for z in range(6):
            at = (4 * yc + (z + 1) // 2) * CH
            if 1 <= y <= 4 and 1 <= z <= 4:
                value = grad[y - 1, z - 1]
            elif 1 <= y <= 4:
                value = kept[z // 5, y - 1].astype(f32)
            else:
                value = beside[y // 5, z].astype(f32)
            value = value + lifted[at : at + CH]
            mask = fine[y + 1, (z + 1) * CH : (z + 2) * CH, :].astype(f32) > 0
            fine_grid[y, z * CH : (z + 1) * CH, :] = jnp.where(mask, value, 0.0).astype(bf16)
    lin = block_diagonal(lin_ref[...].astype(f32).T.astype(bf16))
    for y in range(4):
        value = band_conv(bands[0], [fine_grid[y + a] for a in range(3)])
        value = value + dot(lin, rounded[4 * y : 4 * y + 4].reshape(4 * CH, span))
        base[y] = value.reshape(4, CH, span)
    finish(loads[8], *stores)


def swaps(blocks, axis):
    size_y, size_z = lax.axis_size("gy"), lax.axis_size("gz")
    results = []
    for start, block in enumerate(blocks):
        pairs = []
        for y in range(size_y):
            for z in range(size_z):
                step = 1 if ((y if axis == "gy" else z) - start) % 2 == 0 else -1
                to_y, to_z = y, z
                if axis == "gy":
                    to_y = (y + step) % size_y
                elif 0 <= z + step < size_z:
                    to_z = z + step
                else:
                    to_y = y ^ 1
                pairs.append((y * size_z + z, to_y * size_z + to_z))
        results.append(lax.ppermute(block, BOTH, pairs))
    return results


def exchange(block):
    return lax.all_to_all(block, BOTH, split_axis=0, concat_axis=0, tiled=True)


def shards(
    carbon_input_volume,
    cotangent,
    spec_weight,
    lin_weight,
    conv_fine,
    bias_fine,
    conv_coarse,
    bias_coarse,
):
    channels, rows_y, rows_z, span = carbon_input_volume.shape
    gy, gz = lax.axis_size("gy"), lax.axis_size("gz")
    devices = gy * gz
    cells = rows_y * rows_z
    local = MX // gy
    modes = (MY // gz) * MZ
    wide = local * CH
    scale = 1.0 / math.sqrt(span * cells * devices)
    there, back = mode_tables(gy, gz, rows_y, rows_z, scale)
    forward_x = jnp.asarray(x_tables(span, gy))
    inverse_table = jnp.asarray(x_back_table(span, gy, gz))

    limit = (14 << 20) + devices * (64 << 10)
    chunk = struct((devices, 2 * cells, wide), bf16)
    sent = pltpu.VMEM(chunk.shape, bf16)
    field = struct((rows_y, rows_z, CH, span))
    field_v = pltpu.VMEM(field.shape, f32)
    round_field = struct(field.shape, bf16)
    round_v = pltpu.VMEM(field.shape, bf16)
    raw = struct(carbon_input_volume.shape, bf16)
    raw_v = pltpu.VMEM(raw.shape, bf16)
    taps_v = pltpu.VMEM(conv_fine.shape, bf16)
    x_scratch = pltpu.VMEM((2 * gy * cells, wide), f32)
    wide_scratch = pltpu.VMEM((devices * 2 * cells, wide), f32)
    left_scratch = pltpu.VMEM((cells * CH, local * devices * 2), bf16)
    mode_field = struct((2 * modes, wide))
    mode_v = pltpu.VMEM(mode_field.shape, f32)
    rows = modes * CH
    packed = struct((rows, 2 * wide), bf16)
    bands_v = pltpu.VMEM((2, 12 * CH, 24 * CH), bf16)
    side = struct((rows_y, 3, CH, span), bf16)
    message = struct((6, CH, span), bf16)
    y_side = struct((3, 10 * CH, span), bf16)
    y_message = struct((12, CH, span), bf16)

    with jax.named_scope("arrive"):
        u, one, two, my_x = run(
            arrive_kernel,
            [(IN_HBM, carbon_input_volume), (IN_HBM, forward_x)],
            [
                (IN_VMEM, round_field),
                (IN_VMEM, side),
                (IN_VMEM, side),
                (IN_VMEM, struct(forward_x.shape, bf16)),
            ],
            limit,
            [raw_v],
            copies=2,
        )
    one, two = swaps((one, two), "gz")

    def spread(values, table, exact):
        with jax.named_scope("spread"):
            return run(
                lambda *refs: spread_kernel(exact, local, gy, gz, *refs),
                [(IN_VMEM, values), (IN_VMEM, table)],
                [(IN_HBM, chunk)],
                limit,
                [x_scratch, sent],
                copies=2,
                micros=1.2,
            )[0]

    received = exchange(spread(u, my_x, True))

    with jax.named_scope("y_message"):
        own_one, own_two = run(
            y_message_kernel,
            [(IN_VMEM, u), (IN_VMEM, one), (IN_VMEM, two)],
            [(IN_HBM, y_side), (IN_HBM, y_side)],
            limit,
            [pltpu.VMEM((rows_y, 10 * CH, span), bf16)],
            copies=2,
        )
    one, two = swaps((own_one, own_two), "gy")

    with jax.named_scope("setup"):
        w_high, w_low, my_there, my_back, w_kept = run(
            lambda *refs: setup_kernel(local, *refs),
            [
                (IN_HBM, spec_weight.reshape(2, local, rows, CH)),
                (IN_HBM, there),
                (IN_HBM, back),
            ],
            [
                (IN_VMEM, packed),
                (IN_VMEM, packed),
                (IN_VMEM, struct(there.shape[1:], bf16)),
                (IN_VMEM, struct(back.shape[1:], bf16)),
                (IN_HBM, packed),
            ],
            limit + (10 << 20),
            [pltpu.VMEM((2, local, rows, CH), f32)],
            copies=10,
            micros=4.5,
        )

    with jax.named_scope("mix"):
        v, send = run(
            lambda *refs: mix_kernel(local, *refs),
            [
                (IN_VMEM, received),
                (IN_VMEM, my_there),
                (IN_VMEM, w_high),
                (IN_VMEM, w_low),
                (IN_VMEM, my_back),
            ],
            [(IN_HBM, mode_field), (IN_HBM, chunk)],
            limit,
            [mode_v, sent],
            copies=5,
            micros=3,
        )
    received = exchange(send)

    with jax.named_scope("forward_convs"):
        base, fine, coarse, cot, my_inverse, my_x = run(
            forward_conv_kernel,
            [
                (IN_HBM, own_one),
                (IN_HBM, own_two),
                (IN_HBM, one),
                (IN_HBM, two),
                (IN_VMEM, lin_weight),
                (IN_HBM, conv_fine),
                (IN_HBM, conv_coarse),
                (IN_VMEM, bias_fine[None]),
                (IN_VMEM, bias_coarse[None]),
                (IN_HBM, cotangent),
                (IN_HBM, inverse_table),
                (IN_HBM, forward_x),
            ],
            [
                (IN_VMEM, field),
                (IN_HBM, struct((8, 8 * CH, span), bf16)),
                (IN_VMEM, struct((2, 2, CH, span // 2), bf16)),
                (IN_VMEM, round_field),
                (IN_VMEM, struct(inverse_table.shape, bf16)),
                (IN_VMEM, struct(forward_x.shape, bf16)),
            ],
            limit,
            [
                pltpu.VMEM((10, 12 * CH, span), bf16),
                taps_v,
                taps_v,
                raw_v,
                bands_v,
                pltpu.VMEM((4, 8 * CH, span // 2), bf16),
                pltpu.VMEM((8, 8 * CH, span), bf16),
            ],
            copies=10,
            micros=7,
        )

    with jax.named_scope("middle"):
        activated, grad, grad_kept, grad_round, one, two = run(
            lambda *refs: middle_kernel(local, *refs),
            [
                (IN_VMEM, received),
                (IN_VMEM, my_inverse),
                (IN_VMEM, base),
                (IN_VMEM, cot),
                (IN_VMEM, coarse),
            ],
            [
                (IN_HBM, round_field),
                (IN_VMEM, field),
                (IN_HBM, field),
                (IN_HBM, struct((cells + 2, CH, span), bf16)),
                (IN_VMEM, message),
                (IN_VMEM, message),
            ],
            limit,
            [
                round_v,
                pltpu.VMEM((cells + 2, CH, span), bf16),
                wide_scratch,
                left_scratch,
            ],
            copies=3,
            micros=2,
        )
    one, two = swaps((one, two), "gz")
    received = exchange(spread(grad, my_x, False))

    with jax.named_scope("y_gradient"):
        kept_z, one, two = run(
            y_gradient_kernel,
            [(IN_HBM, grad_round), (IN_VMEM, one), (IN_VMEM, two)],
            [
                (IN_HBM, struct((2,) + message.shape, bf16)),
                (IN_VMEM, y_message),
                (IN_VMEM, y_message),
            ],
            limit,
            [
                pltpu.VMEM((cells + 2, CH, span), bf16),
                pltpu.VMEM((2,) + message.shape, bf16),
            ],
            copies=3,
            micros=20,
        )
    one, two = swaps((one, two), "gy")
    with jax.named_scope("turn"):
        predicted, my_there, my_w, my_back = run(
            turn_kernel,
            [(IN_HBM, activated), (IN_HBM, there), (IN_HBM, w_kept), (IN_HBM, back)],
            [
                (IN_HBM, raw),
                (IN_VMEM, struct(there.shape[1:], bf16)),
                (IN_VMEM, packed),
                (IN_VMEM, struct(back.shape[1:], bf16)),
            ],
            limit,
            [round_v, raw_v],
            copies=5,
            micros=2,
        )

    with jax.named_scope("mix_adjoint"):
        d, send = run(
            lambda *refs: adjoint_kernel(local, *refs),
            [(IN_VMEM, received), (IN_VMEM, my_there), (IN_VMEM, my_w), (IN_VMEM, my_back)],
            [(IN_VMEM, mode_field), (IN_HBM, chunk)],
            limit,
            [sent],
            copies=4,
            micros=2,
        )
    received = exchange(send)

    with jax.named_scope("backward"):
        weight_grad, base, my_inverse = run(
            backward_kernel,
            [
                (IN_VMEM, d),
                (IN_VMEM, v),
                (IN_HBM, grad_kept),
                (IN_HBM, grad_round),
                (IN_HBM, kept_z),
                (IN_HBM, one),
                (IN_HBM, two),
                (IN_HBM, fine),
                (IN_VMEM, lin_weight),
                (IN_HBM, conv_fine),
                (IN_HBM, conv_coarse),
                (IN_HBM, inverse_table),
            ],
            [
                (IN_HBM, struct((2, local, rows, CH))),
                (IN_VMEM, field),
                (IN_VMEM, struct(inverse_table.shape, bf16)),
            ],
            limit + (10 << 20),
            [
                pltpu.VMEM((2, local, rows, CH), f32),
                field_v,
                pltpu.VMEM((cells + 2, CH, span), bf16),
                pltpu.VMEM((2,) + message.shape, bf16),
                pltpu.VMEM((2,) + y_message.shape, bf16),
                pltpu.VMEM((8, 8 * CH, span), bf16),
                taps_v,
                taps_v,
                bands_v,
                pltpu.VMEM((6, 8 * CH, span // 2), bf16),
                pltpu.VMEM((6, 8 * CH, span), bf16),
            ],
            copies=9 + local,
            micros=6,
        )
    weight_grad = weight_grad.reshape(spec_weight.shape)

    with jax.named_scope("last"):
        (sensitivity,) = run(
            lambda *refs: last_kernel(local, *refs),
            [(IN_VMEM, received), (IN_VMEM, my_inverse), (IN_VMEM, base)],
            [(IN_HBM, raw)],
            limit,
            [raw_v, wide_scratch, left_scratch],
            copies=1,
            micros=2,
        )
    return (predicted, sensitivity, weight_grad)


def solution(mesh):
    field = P(None, "gy", "gz", None)
    modes = P(None, "gy", "gz", None, None, None)
    return jax.shard_map(
        shards,
        mesh=mesh,
        in_specs=(field, field, modes, P(), P(), P(), P(), P()),
        out_specs=(field, field, modes),
        check_vma=False,
    )
```

```python
import math

import jax
import jax.numpy as jnp
import ml_dtypes
import numpy as np
from jax import lax
from jax.experimental import pallas as pl
from jax.experimental.pallas import tpu as pltpu
from jax.sharding import PartitionSpec as P

MX = 32
MY = 32
MZ = 8
CH = 32
BOTH = ("gy", "gz")

f32 = jnp.float32
bf16 = jnp.bfloat16
root_coef = math.sqrt(2.0 / math.pi)
NN = (((1,), (0,)), ((), ()))
NT = (((1,), (1,)), ((), ()))
TN = (((0,), (0,)), ((), ()))


def dot(a, b, form=NN):
    return lax.dot_general(a, b, form, preferred_element_type=f32)


def halves(value):
    high = value.astype(bf16)
    return high, (value - high.astype(f32)).astype(bf16)


def iota(shape, dim):
    return lax.broadcasted_iota(jnp.int32, shape, dim)


IN_VMEM = pl.BlockSpec(memory_space=pltpu.VMEM)
IN_HBM = pl.BlockSpec(memory_space=pltpu.HBM)


def struct(shape, kind=f32):
    return jax.ShapeDtypeStruct(shape, kind)


def run(kernel, ins, outs, limit, scratch=(), micros=1.0, copies=0, **grid):
    scratch = list(scratch)
    if copies:
        scratch.append(pltpu.SemaphoreType.DMA((copies,)))
    held = {id(IN_HBM): pltpu.HBM, id(IN_VMEM): pltpu.VMEM}

    def placed(spec, array):
        if id(spec) in held:
            return pltpu.with_memory_space_constraint(array, held[id(spec)])
        return array

    def shaped(spec, shape):
        if id(spec) in held:
            return held[id(spec)](shape.shape, shape.dtype)
        return shape

    return pl.pallas_call(
        kernel,
        in_specs=[spec for spec, _ in ins],
        out_specs=[spec for spec, _ in outs],
        out_shape=[shaped(spec, shape) for spec, shape in outs],
        scratch_shapes=scratch,
        compiler_params=pltpu.CompilerParams(vmem_limit_bytes=limit),
        cost_estimate=pl.CostEstimate(
            flops=int(micros * 1.1e9), bytes_accessed=1 << 16, transcendentals=0
        ),
        **grid,
    )(*[placed(spec, array) for spec, array in ins])


def begin(sem, first, *pairs):
    copies = [
        pltpu.make_async_copy(source, target, sem.at[first + i])
        for i, (source, target) in enumerate(pairs)
    ]
    for copy in copies:
        copy.start()
    return copies


def finish(*copies):
    for copy in copies:
        copy.wait()


def kept(count, length):
    position = np.arange(count)
    return np.where(position < count // 2, position, length - count + position)


def split_np(table):
    high = table.astype(ml_dtypes.bfloat16)
    return high, (table - high.astype(np.float64)).astype(ml_dtypes.bfloat16)


def x_tables(cells_x, blocks):
    local = MX // blocks
    freqs = kept(MX, cells_x).reshape(blocks, local).T
    angles = 2.0 * np.pi * ((freqs[:, :, None] * np.arange(cells_x)) % cells_x) / cells_x
    table = np.stack([np.cos(angles), -np.sin(angles)], axis=2).reshape(2 * MX, cells_x)
    return np.concatenate(split_np(table), axis=0)


def x_back_table(cells_x, gy, gz):
    local = MX // gy
    freqs = kept(MX, cells_x).reshape(gy, local).T
    angles = 2.0 * np.pi * ((freqs[:, :, None] * np.arange(cells_x)) % cells_x) / cells_x
    table = np.stack([np.cos(angles), -np.sin(angles)], axis=2)
    table = np.broadcast_to(table[:, :, None], (local, gy, gz, 2, cells_x))
    return np.concatenate(split_np(table.reshape(-1, cells_x)), axis=0)


def yz_angles(xp, freqs_y, gy, gz, rows_y, rows_z):
    span_y, span_z = gy * rows_y, gz * rows_z
    phase_y = (freqs_y[:, None] * xp.arange(span_y)[None]) % span_y
    phase_z = (xp.arange(MZ)[:, None] * xp.arange(span_z)[None]) % span_z
    phase_y = phase_y.reshape(-1, 1, gy, 1, rows_y, 1)
    phase_z = phase_z.reshape(1, MZ, 1, gz, 1, rows_z)
    turn = (phase_y * span_z + phase_z * span_y) % (span_y * span_z)
    return turn.reshape(turn.shape[0] * MZ, gy * gz, rows_y * rows_z)


def yz_table(xp, freqs_y, gy, gz, rows_y, rows_z):
    cells = gy * gz * rows_y * rows_z
    turn = yz_angles(xp, freqs_y, gy, gz, rows_y, rows_z)
    angles = 2.0 * math.pi / cells * turn
    cosine, sine = xp.cos(angles), xp.sin(angles)
    table = xp.stack([xp.stack([cosine, sine], 2), xp.stack([-sine, cosine], 2)], 0)
    return table.reshape(2 * turn.shape[0], -1)


def mode_tables(gy, gz, rows_y, rows_z, scale):
    local = MY // gz
    cells = gy * gz * rows_y * rows_z
    freqs = kept(MY, gy * rows_y).reshape(gz, local)
    if gz * 2 * local * MZ * 2 * cells <= 1 << 20:
        there, back = [], []
        for block in range(gz):
            high, low = split_np(scale * yz_table(np, freqs[block], gy, gz, rows_y, rows_z))
            there.append(np.concatenate([high, low], 0))
            back.append(np.concatenate([high.T, low.T], 1))
        return jnp.asarray(np.stack(there)), jnp.asarray(np.stack(back))
    where = lax.axis_index("gz")
    mine = lax.dynamic_index_in_dim(jnp.asarray(freqs, jnp.int32), where, keepdims=False)
    high, low = halves(scale * yz_table(jnp, mine, gy, gz, rows_y, rows_z).astype(f32))
    return jnp.concatenate([high, low], 0)[None], jnp.concatenate([high.T, low.T], 1)[None]


def put_x_modes(product, local, blocks, copies, cells, scratch, sent, send_ref, sem, first):
    rows = 2 * blocks
    for cell in range(cells):
        piece = product[:, cell * CH : (cell + 1) * CH]
        value = jnp.concatenate([piece[k * rows : (k + 1) * rows] for k in range(local)], axis=1)
        scratch[pl.ds(cell, rows, stride=cells), :] = value
    moves = []
    half = blocks // 2
    for block in range(blocks):
        value = scratch[block * 2 * cells : (block + 1) * 2 * cells].astype(bf16)
        for copy in range(copies):
            sent[block * copies + copy] = value
        if (block + 1) % half == 0:
            part = pl.ds((block + 1 - half) * copies, half * copies)
            moves += begin(sem, first + len(moves), (sent.at[part], send_ref.at[part]))
    return moves


def odd(axis):
    return lax.axis_index(axis) & 1


def first(axis):
    return lax.axis_index(axis) == 0


def last(axis):
    return lax.axis_index(axis) == lax.axis_size(axis) - 1


def arrive_kernel(raw_ref, table_ref, u_ref, one_ref, two_ref, my_table_ref, raw, sem):
    loads = begin(sem, 0, (raw_ref, raw), (table_ref, my_table_ref))
    finish(*loads)
    u = jnp.transpose(raw[...], (1, 2, 0, 3))
    u_ref[...] = u
    side = odd("gz")
    one_ref[...] = u_ref[:, pl.ds(1 - side, 3)]
    two_ref[...] = u_ref[:, pl.ds(side, 3)]


def spread_kernel(
    exact, local, blocks, copies, u_ref, table, *refs
):
    *refs, scratch, sent, sem = refs
    count = len(refs) // 2
    stores = begin(sem, 2, *zip(refs[:count], refs[count + 1 :]))
    send_ref = refs[count]
    cells = u_ref.shape[0] * u_ref.shape[1]
    u = u_ref[...].reshape(cells * CH, -1)
    if exact:
        both = dot(table[...], u, NT)
        product = both[: 2 * MX] + both[2 * MX :]
    else:
        high, low = halves(u)
        both = dot(table[...], high, NT)
        product = both[: 2 * MX] + both[2 * MX :] + dot(table[: 2 * MX], low, NT)
    moves = put_x_modes(product, local, blocks, copies, cells, scratch, sent, send_ref, sem, 0)
    finish(*moves, *stores)


def pick(tables_ref):
    if tables_ref.shape[0] == 1:
        return tables_ref.at[0]
    return tables_ref.at[lax.axis_index("gz")]


def mode_values(rec_ref, there, rows):
    both = dot(there[...], rec_ref[...].reshape(-1, rec_ref.shape[2]))
    return both[:rows] + both[rows:]


def put_back(values, back_ref, sent, send_ref, sem, first):
    high, low = halves(values)
    twice = jnp.concatenate([high, high], 0)
    rows = values.shape[0]
    devices, depth, wide = sent.shape
    part = devices // 4
    moves = []
    for step in range(4):
        at = slice(step * part * depth, (step + 1) * part * depth)
        result = dot(back_ref[at], twice) + dot(back_ref[at, :rows], low)
        sent[step * part : (step + 1) * part] = result.astype(bf16).reshape(part, depth, wide)
        span = pl.ds(step * part, part)
        moves += begin(sem, first + step, (sent.at[span], send_ref.at[span]))
    finish(*moves)


def kz_weight(shape):
    return jnp.where(iota(shape, 0) % MZ == 0, 1.0, 2.0).astype(f32)


def same_mode(rows, lanes):
    return (iota((rows, lanes), 0) % MZ) == ((iota((rows, lanes), 1) // CH) % MZ)


def mix_kernel(
    local,
    rec_ref,
    there_ref,
    high_ref,
    low_ref,
    back_ref,
    v_ref,
    send_ref,
    kept_v,
    sent,
    sem,
):
    rows = there_ref.shape[0] // 2
    modes = rows // 2
    wide = local * CH
    v = mode_values(rec_ref, there_ref, rows)
    kept_v[...] = v
    store = begin(sem, 0, (kept_v, v_ref))
    real, imag = v[:modes], v[modes:]
    pair = (
        jnp.concatenate([real, -imag], 1),
        jnp.concatenate([imag, real], 1),
    )
    lane_k = (iota((MZ, 2 * wide), 1) // CH) % local
    size = MZ * CH
    diag = same_mode(2 * MZ * local, size)
    placed = [[[None] * (modes // MZ) for _ in range(local)] for _ in range(2)]
    for g in range(modes // MZ):
        pieces = []
        for k in range(local):
            for part in range(2):
                piece = pair[part][g * MZ : (g + 1) * MZ]
                pieces.append(jnp.where(lane_k == k, piece, 0.0))
        left_high, left_low = halves(jnp.concatenate(pieces, 0))
        w_high = high_ref[g * size : (g + 1) * size]
        w_low = low_ref[g * size : (g + 1) * size]
        count = left_high.shape[0]
        both = dot(jnp.concatenate([left_high, left_low], 0), w_high, NT)
        value = both[:count] + both[count:] + dot(left_high, w_low, NT)
        value = jnp.where(diag, value, 0.0)
        for k in range(local):
            for part in range(2):
                at = (2 * k + part) * MZ
                placed[part][k][g] = value[at : at + MZ]
    columns = [jnp.concatenate(placed[0][k] + placed[1][k], 0) for k in range(local)]
    all_values = jnp.concatenate(columns, 1)
    shape = (local * size, wide)
    fold = (iota(shape, 0) // size == iota(shape, 1) // CH) & (
        iota(shape, 0) % CH == iota(shape, 1) % CH
    )
    fold = fold.astype(bf16)
    high, low = halves(all_values)
    mixed = dot(high, fold) + dot(low, fold)
    put_back(mixed * kz_weight(mixed.shape), back_ref, sent, send_ref, sem, 1)
    finish(*store)


def adjoint_kernel(
    local,
    rec_ref,
    there_ref,
    high_ref,
    back_ref,
    d_ref,
    send_ref,
    sent,
    sem,
):
    rows = there_ref.shape[0] // 2
    modes = rows // 2
    wide = local * CH
    size = MZ * CH
    d = mode_values(rec_ref, there_ref, rows)
    d = d * kz_weight(d.shape)
    d_ref[...] = d
    shape = (wide, local * size)
    rep = (iota(shape, 1) // size == iota(shape, 0) // CH) & (
        iota(shape, 1) % CH == iota(shape, 0) % CH
    )
    rep = rep.astype(bf16)
    high, low = halves(d)
    spread = dot(high, rep) + dot(low, rep)
    spread = jnp.where(same_mode(rows, local * size), spread, 0.0)
    lane_k = (iota((2 * MZ, 2 * wide), 1) // CH) % local
    parts = ([], [])
    for g in range(modes // MZ):
        pieces = []
        for k in range(local):
            for part in range(2):
                at = part * modes + g * MZ
                pieces.append(spread[at : at + MZ, k * size : (k + 1) * size])
        left_high, left_low = halves(jnp.concatenate(pieces, 0))
        count = left_high.shape[0]
        both = dot(
            jnp.concatenate([left_high, left_low], 0), high_ref[g * size : (g + 1) * size]
        )
        value = both[:count] + both[count:]
        total = None
        for k in range(local):
            piece = jnp.where(lane_k == k, value[2 * k * MZ : 2 * (k + 1) * MZ], 0.0)
            total = piece if total is None else total + piece
        parts[0].append(total[:MZ])
        parts[1].append(total[MZ:])
    real = jnp.concatenate(parts[0], 0)
    imag = jnp.concatenate(parts[1], 0)
    value = jnp.concatenate(
        [real[:, :wide] + imag[:, wide:], imag[:, :wide] - real[:, wide:]], 0
    )
    put_back(value, back_ref, sent, send_ref, sem, 0)


def setup_kernel(
    local,
    w_ref,
    there_ref,
    back_ref,
    high_ref,
    low_ref,
    my_there_ref,
    my_back_ref,
    kept_ref,
    w,
    sem,
):
    parts = 4
    rows = w.shape[2] // parts
    spans = [pl.ds(step * rows, rows) for step in range(parts)]
    loads = begin(sem, 0, *[(w_ref.at[:, :, span], w.at[:, :, span]) for span in spans])
    tables = begin(
        sem, parts, (pick(there_ref), my_there_ref), (pick(back_ref), my_back_ref)
    )
    stores = []
    for step in range(parts):
        at = slice(step * rows, (step + 1) * rows)
        finish(loads[step])
        pieces = [w[part, k, at] for part in range(2) for k in range(local)]
        high_ref[at], low_ref[at] = halves(jnp.concatenate(pieces, 1))
        stores += begin(sem, parts + 2 + step, (high_ref.at[spans[step]], kept_ref.at[spans[step]]))
    finish(*tables, *stores)


def put_weight_grad(d_ref, v_ref, out, out_ref, sem, first):
    rows, wide = d_ref.shape
    modes = rows // 2
    size = MZ * CH
    keep = same_mode(rows, size)
    d_halves = halves(d_ref[...])
    v_halves = halves(v_ref[...])
    stores = []
    for k in range(wide // CH):
        shape = (wide, size)
        rep = (iota(shape, 0) == k * CH + iota(shape, 1) % CH).astype(bf16)
        d_high, d_low = [jnp.where(keep, dot(value, rep), 0.0) for value in d_halves]
        at = slice(k * CH, (k + 1) * CH)
        v_high, v_low = [value[:, at].astype(f32) for value in v_halves]
        for g in range(modes // MZ):
            real = slice(g * MZ, (g + 1) * MZ)
            imag = slice(modes + g * MZ, modes + (g + 1) * MZ)
            left = jnp.concatenate(
                [d_high[real], d_high[imag], d_low[real], d_low[imag], d_high[real], d_high[imag]],
                0,
            ).astype(bf16)
            for part in range(2):
                rights = []
                for v in (v_high, v_high, v_low):
                    rights += [v[real], v[imag]] if part == 0 else [-v[imag], v[real]]
                right = jnp.concatenate(rights, 0).astype(bf16)
                out[part, k, g * size : (g + 1) * size, :] = dot(left, right, TN)
        stores += begin(sem, first + k, (out.at[:, k], out_ref.at[:, k]))
    return stores


def inverse_x(rec_ref, table, local, cells, wide, left):
    wide[...] = rec_ref[...].reshape(-1, rec_ref.shape[2]).astype(f32)
    rows = wide.shape[0] // cells
    for cell in range(cells):
        turned = wide[pl.ds(cell, rows, stride=cells), :].T.astype(bf16)
        for k in range(local):
            left[cell * CH : (cell + 1) * CH, k * rows : (k + 1) * rows] = turned[
                k * CH : (k + 1) * CH
            ]
    depth = local * rows
    value = left[...]
    return dot(value, table[:depth]) + dot(value, table[depth:])


def gelu_pair(pre_act):
    cube_term = pre_act * pre_act * pre_act
    tanh_result = jnp.tanh(root_coef * (pre_act + 0.044715 * cube_term))
    activated_output = 0.5 * pre_act * (1.0 + tanh_result)
    gelu_slope = 0.5 * (1.0 + tanh_result) + 0.5 * pre_act * (
        1.0 - tanh_result * tanh_result
    ) * root_coef * (1.0 + 3.0 * 0.044715 * pre_act * pre_act)
    return (activated_output, gelu_slope)


def middle_kernel(
    local,
    rec_ref,
    back_ref,
    base_ref,
    cot_ref,
    coarse_ref,
    out_ref,
    grad_ref,
    rounded,
    one_ref,
    two_ref,
    wide,
    left,
):
    rows_y, rows_z, _, span = base_ref.shape
    cells = rows_y * rows_z
    pre_act = inverse_x(rec_ref, back_ref, local, cells, wide, left)
    pre_act = pre_act + base_ref[...].reshape(pre_act.shape)
    activated, slope = gelu_pair(pre_act)
    out_ref[...] = activated.astype(bf16).reshape(out_ref.shape)
    value = cot_ref[...].astype(f32).reshape(pre_act.shape) * slope
    grad_ref[...] = value.reshape(grad_ref.shape)
    rounded[:cells] = value.astype(bf16).reshape(cells, CH, span)
    side = odd("gz")
    for y in range(rows_y):
        one_ref[y] = rounded[rows_z * y + (rows_z - 1) * (1 - side)]
        two_ref[y] = rounded[rows_z * y + (rows_z - 1) * side]
    pool = pool_matrix(span)
    for yc in range(2):
        sums = []
        for zc in range(2):
            y, z = 2 * yc, 2 * zc
            sums.append(
                grad_ref[y, z] + grad_ref[y, z + 1] + grad_ref[y + 1, z] + grad_ref[y + 1, z + 1]
            )
        total_high, total_low = halves(jnp.concatenate(sums, 0))
        total = dot(total_high, pool) + dot(total_low, pool)
        pieces = []
        for zc in range(2):
            piece = total[zc * CH : (zc + 1) * CH]
            pieces.append(jnp.where(coarse_ref[yc, zc].astype(f32) > 0, piece, 0.0))
        piece = jnp.concatenate(pieces, 1).astype(bf16)
        rounded[cells + yc] = piece
        one_ref[rows_y + yc] = piece
        two_ref[rows_y + yc] = piece


def last_kernel(local, rec_ref, back_ref, base_ref, out_ref, out, wide, left, sem):
    cells = base_ref.shape[0] * base_ref.shape[1]
    value = inverse_x(rec_ref, back_ref, local, cells, wide, left)
    value = value.reshape(base_ref.shape) + base_ref[...]
    out[...] = jnp.transpose(value.astype(bf16), (2, 0, 1, 3))
    finish(*begin(sem, 0, (out, out_ref)))


def turn_kernel(
    value_ref,
    there_ref,
    w_ref,
    back_ref,
    out_ref,
    my_there_ref,
    my_w_ref,
    my_back_ref,
    value,
    out,
    sem,
):
    loads = begin(
        sem,
        0,
        (value_ref, value),
        (pick(there_ref), my_there_ref),
        (w_ref, my_w_ref),
        (pick(back_ref), my_back_ref),
    )
    finish(loads[0])
    out[...] = jnp.transpose(value[...], (2, 0, 1, 3))
    finish(*begin(sem, 4, (out, out_ref)), *loads[1:])


def write_bands(adjoint, k_ref, out, index):
    for a in range(3):
        for e in range(3):
            taps = []
            for b in range(3):
                if adjoint:
                    tap = k_ref[9 * (2 - a) + 3 * (2 - b) + 2 - e].astype(f32).T
                else:
                    tap = k_ref[9 * a + 3 * b + e].astype(f32)
                taps.append(tap)
            taps = jnp.concatenate(taps, 1)
            for z in range(4):
                pieces = [taps, jnp.zeros((CH, (5 - z) * CH), f32)]
                if z > 0:
                    pieces.insert(0, jnp.zeros((CH, z * CH), f32))
                row = jnp.concatenate(pieces, 1)
                at = (e * 4 + z) * CH
                out[index, at : at + CH, a * 8 * CH : (a + 1) * 8 * CH] = row.astype(bf16)


def x_sum(low, same, high):
    span = same.shape[1]
    lane = iota(same.shape, 1)
    before = jnp.where(lane == 0, 0.0, pltpu.roll(low, 1, axis=1))
    after = jnp.where(lane == span - 1, 0.0, pltpu.roll(high, span - 1, axis=1))
    return same + before + after


def band_conv(bands, planes):
    value = dot(bands, jnp.concatenate(planes, 0))
    size = 4 * CH
    return x_sum(value[:size], value[size : 2 * size], value[2 * size :])


def column(row_ref, copies):
    eye = iota((CH, CH), 0) == iota((CH, CH), 1)
    value = jnp.sum(jnp.where(eye, row_ref[...], 0.0), axis=1, keepdims=True)
    return jnp.concatenate([value] * copies, 0)


def block_diagonal(matrix):
    shape = (4 * CH, 4 * CH)
    wide = jnp.concatenate([matrix.astype(f32)] * 4, 1)
    tiled = jnp.concatenate([wide] * 4, 0)
    return jnp.where(iota(shape, 0) // CH == iota(shape, 1) // CH, tiled, 0.0).astype(bf16)


def pool_matrix(span):
    shape = (span, span // 2)
    return (iota(shape, 0) // 2 == iota(shape, 1)).astype(bf16)


def up_matrix(span):
    shape = (span // 2, span)
    return (iota(shape, 1) // 2 == iota(shape, 0)).astype(bf16)


def y_message_kernel(u_ref, z_one_ref, z_two_ref, one_ref, two_ref, rows, sem):
    side = odd("gz")
    for y in range(4):
        for z in range(3):
            at = pl.multiple_of((7 * (1 - side) + z) * CH, CH)
            rows[y, pl.ds(at, CH)] = z_one_ref[y, z]
            at = pl.multiple_of((7 * side + z) * CH, CH)
            rows[y, pl.ds(at, CH)] = z_two_ref[y, z]
        for z in range(4):
            rows[y, (z + 3) * CH : (z + 4) * CH] = u_ref[y, z]
    blank = jnp.zeros((4, 3 * CH, rows.shape[2]), bf16)

    @pl.when(first("gz"))
    def low_end():
        rows[:, : 3 * CH] = blank

    @pl.when(last("gz"))
    def high_end():
        rows[:, 7 * CH :] = blank

    side = odd("gy")
    finish(
        *begin(
            sem, 0, (rows.at[pl.ds(1 - side, 3)], one_ref), (rows.at[pl.ds(side, 3)], two_ref)
        )
    )


def forward_conv_kernel(
    own_one_ref,
    own_two_ref,
    y_one_ref,
    y_two_ref,
    lin_ref,
    taps_fine_ref,
    taps_coarse_ref,
    bias_fine_ref,
    bias_coarse_ref,
    cot_ref,
    table_ref,
    x_ref,
    base,
    fine_ref,
    coarse,
    my_cot_ref,
    my_table_ref,
    my_x_ref,
    grid,
    taps_fine,
    taps_coarse,
    raw,
    bands,
    pooled,
    fine,
    sem,
):
    span = grid.shape[2]
    inner = pl.ds(0, 10 * CH)
    side = odd("gy")
    loads = begin(
        sem,
        0,
        (taps_fine_ref, taps_fine),
        (own_one_ref, grid.at[pl.ds(4 - side, 3), inner]),
        (own_two_ref.at[pl.ds(2 * side, 1)], grid.at[pl.ds(3 + 3 * side, 1), inner]),
        (y_one_ref, grid.at[pl.ds(7 * (1 - side), 3), inner]),
        (y_two_ref, grid.at[pl.ds(7 * side, 3), inner]),
        (taps_coarse_ref, taps_coarse),
        (cot_ref, raw),
        (table_ref, my_table_ref),
        (x_ref, my_x_ref),
    )
    edges = [jnp.logical_not(end(axis)) for axis in ("gy", "gz") for end in (first, last)]
    grid[:, 10 * CH :, :] = jnp.zeros((10, 2 * CH, span), bf16)
    pooled[:, 4 * CH :, :] = jnp.zeros((4, 4 * CH, span // 2), bf16)
    bias = column(bias_fine_ref, 4)
    half = 4 * CH
    row_z = iota((half, span), 0) // CH
    finish(loads[0])
    write_bands(False, taps_fine, bands, 0)
    finish(*loads[1:3])
    for y in (3, 4, 2, 1, 0, 5, 6, 7):
        if y == 2:
            finish(loads[3], loads[4])

            @pl.when(first("gy"))
            def low_end():
                grid[:3] = jnp.zeros((3, 12 * CH, span), bf16)

            @pl.when(last("gy"))
            def high_end():
                grid[7:] = jnp.zeros((3, 12 * CH, span), bf16)

        y_in = None
        if y < 2:
            y_in = edges[0]
        elif y >= 6:
            y_in = edges[1]
        for h in range(2):
            at = h * half
            value = band_conv(bands[0], [grid[y + a, at : at + 8 * CH, :] for a in range(3)])
            value = jnp.maximum(value + bias, 0.0)
            inside = (row_z >= 2) | edges[2] if h == 0 else (row_z < 2) | edges[3]
            if y_in is not None:
                inside = inside & y_in
            fine[y, at : at + half, :] = jnp.where(inside, value, 0.0).astype(bf16)
    (store,) = begin(sem, 9, (fine, fine_ref))
    sums = []
    for yc in range(4):
        both = fine[2 * yc].astype(f32) + fine[2 * yc + 1].astype(f32)
        for zc in range(4):
            at = 2 * zc * CH
            sums.append(both[at : at + CH] + both[at + CH : at + 2 * CH])
    pool = pool_matrix(span)
    high, low = halves(jnp.concatenate(sums, 0))
    pools = (0.125 * (dot(high, pool) + dot(low, pool))).astype(bf16)
    pooled[:, : 4 * CH, :] = pools.reshape(4, 4 * CH, span // 2)
    bias = column(bias_coarse_ref, 4)
    finish(loads[5])
    write_bands(False, taps_coarse, bands, 1)
    planes = [jnp.concatenate([pooled[a], pooled[a + 1]], 1) for a in range(3)]
    value = dot(bands[1], jnp.concatenate(planes, 0))
    parts = [value[e * half : (e + 1) * half] for e in range(3)]
    for yc in range(2):
        at = slice(yc * span // 2, (yc + 1) * span // 2)
        value = x_sum(*[part[:, at] for part in parts])
        value = jnp.maximum(value + bias, 0.0).astype(bf16)
        coarse[yc] = value[: 2 * CH].reshape(2, CH, span // 2)
    lifted = dot(coarse[...].reshape(half, span // 2), up_matrix(span))
    lin = block_diagonal(lin_ref[...])
    for y in range(4):
        total = dot(lin, grid[y + 3, 3 * CH : 7 * CH, :])
        total = total + fine[y + 2, 2 * CH : 6 * CH, :].astype(f32)
        for z in range(4):
            at = (y // 2 * 2 + z // 2) * CH
            base[y, z] = total[z * CH : (z + 1) * CH] + lifted[at : at + CH]
    finish(loads[6])
    my_cot_ref[...] = jnp.transpose(raw[...], (1, 2, 0, 3))
    finish(store, *loads[7:])


def y_gradient_kernel(
    round_ref, z_one_ref, z_two_ref, kept_ref, one_ref, two_ref, own, halo, sem
):
    (load,) = begin(sem, 0, (round_ref, own))
    side = odd("gz")
    halo[1 - side] = z_one_ref[...]
    halo[side] = z_two_ref[...]

    @pl.when(first("gz"))
    def low_end():
        halo[0] = jnp.zeros(halo.shape[1:], bf16)

    @pl.when(last("gz"))
    def high_end():
        halo[1] = jnp.zeros(halo.shape[1:], bf16)

    (store,) = begin(sem, 1, (halo, kept_ref))
    finish(load)
    side = odd("gy")
    for out_ref, y in ((one_ref, 3 * (1 - side)), (two_ref, 3 * side)):
        out_ref[0] = halo[0, y]
        out_ref[1:5] = own[pl.ds(4 * y, 4)]
        out_ref[5] = halo[1, y]
        for yc in range(2):
            out_ref[6 + 3 * yc] = halo[0, 4 + yc]
            out_ref[7 + 3 * yc] = own[16 + yc]
            out_ref[8 + 3 * yc] = halo[1, 4 + yc]
    finish(store)


def backward_kernel(
    d_ref,
    v_ref,
    grad_ref,
    round_ref,
    kept_ref,
    y_one_ref,
    y_two_ref,
    fine_ref,
    lin_ref,
    taps_fine_ref,
    taps_coarse_ref,
    table_ref,
    weight_ref,
    base,
    my_table_ref,
    weights,
    grad,
    rounded,
    kept,
    beside,
    fine,
    taps_fine,
    taps_coarse,
    bands,
    coarse_grid,
    fine_grid,
    sem,
):
    side = odd("gy")
    loads = begin(
        sem,
        0,
        (taps_coarse_ref, taps_coarse),
        (round_ref, rounded),
        (kept_ref, kept),
        (y_one_ref, beside.at[1 - side]),
        (y_two_ref, beside.at[side]),
        (grad_ref, grad),
        (fine_ref, fine),
        (taps_fine_ref, taps_fine),
        (table_ref, my_table_ref),
    )
    stores = put_weight_grad(d_ref, v_ref, weights, weight_ref, sem, 9)
    finish(loads[0], loads[7])
    write_bands(True, taps_coarse, bands, 1)
    write_bands(True, taps_fine, bands, 0)
    span = grad.shape[3]
    half = span // 2
    coarse_grid[:, 6 * CH :, :] = jnp.zeros((6, 2 * CH, half), bf16)
    fine_grid[:, 6 * CH :, :] = jnp.zeros((6, 2 * CH, span), bf16)

    def place(yc, pair, value):
        for zc in range(2):
            at = (2 * pair + zc) * CH
            coarse_grid[yc, at : at + CH, :] = value[:, zc * half : (zc + 1) * half]

    finish(*loads[1:5])

    @pl.when(first("gy"))
    def low_end():
        beside[0] = jnp.zeros(beside.shape[1:], bf16)

    @pl.when(last("gy"))
    def high_end():
        beside[1] = jnp.zeros(beside.shape[1:], bf16)

    for yc in range(2):
        place(2 + yc, 0, kept[0, 4 + yc])
        place(2 + yc, 1, rounded[16 + yc])
        place(2 + yc, 2, kept[1, 4 + yc])
        for pair in range(3):
            place(yc, pair, beside[0, 6 + 3 * yc + pair])
            place(4 + yc, pair, beside[1, 6 + 3 * yc + pair])
    pooled = [
        0.125 * band_conv(bands[1], [coarse_grid[yc + a] for a in range(3)]) for yc in range(4)
    ]
    high, low = halves(jnp.concatenate(pooled, 0))
    up = up_matrix(span)
    lifted = dot(high, up) + dot(low, up)
    finish(*loads[5:7])
    for y in range(6):
        yc = (y + 1) // 2
        for z in range(6):
            at = (4 * yc + (z + 1) // 2) * CH
            if 1 <= y <= 4 and 1 <= z <= 4:
                value = grad[y - 1, z - 1]
            elif 1 <= y <= 4:
                value = kept[z // 5, y - 1].astype(f32)
            else:
                value = beside[y // 5, z].astype(f32)
            value = value + lifted[at : at + CH]
            mask = fine[y + 1, (z + 1) * CH : (z + 2) * CH, :].astype(f32) > 0
            fine_grid[y, z * CH : (z + 1) * CH, :] = jnp.where(mask, value, 0.0).astype(bf16)
    lin = block_diagonal(lin_ref[...].astype(f32).T.astype(bf16))
    for y in range(4):
        value = band_conv(bands[0], [fine_grid[y + a] for a in range(3)])
        value = value + dot(lin, rounded[4 * y : 4 * y + 4].reshape(4 * CH, span))
        base[y] = value.reshape(4, CH, span)
    finish(loads[8], *stores)


def swaps(blocks, axis):
    size_y, size_z = lax.axis_size("gy"), lax.axis_size("gz")
    results = []
    for start, block in enumerate(blocks):
        pairs = []
        for y in range(size_y):
            for z in range(size_z):
                step = 1 if ((y if axis == "gy" else z) - start) % 2 == 0 else -1
                to_y, to_z = y, z
                if axis == "gy":
                    to_y = (y + step) % size_y
                elif 0 <= z + step < size_z:
                    to_z = z + step
                else:
                    to_y = y ^ 1
                pairs.append((y * size_z + z, to_y * size_z + to_z))
        results.append(lax.ppermute(block, BOTH, pairs))
    return results


def exchange(block):
    return lax.all_to_all(block, BOTH, split_axis=0, concat_axis=0, tiled=True)


def shards(
    carbon_input_volume,
    cotangent,
    spec_weight,
    lin_weight,
    conv_fine,
    bias_fine,
    conv_coarse,
    bias_coarse,
):
    channels, rows_y, rows_z, span = carbon_input_volume.shape
    gy, gz = lax.axis_size("gy"), lax.axis_size("gz")
    devices = gy * gz
    cells = rows_y * rows_z
    local = MX // gy
    modes = (MY // gz) * MZ
    wide = local * CH
    scale = 1.0 / math.sqrt(span * cells * devices)
    there, back = mode_tables(gy, gz, rows_y, rows_z, scale)
    forward_x = jnp.asarray(x_tables(span, gy))
    inverse_table = jnp.asarray(x_back_table(span, gy, gz))

    limit = (14 << 20) + devices * (64 << 10)
    chunk = struct((devices, 2 * cells, wide), bf16)
    sent = pltpu.VMEM(chunk.shape, bf16)
    field = struct((rows_y, rows_z, CH, span))
    field_v = pltpu.VMEM(field.shape, f32)
    round_field = struct(field.shape, bf16)
    round_v = pltpu.VMEM(field.shape, bf16)
    raw = struct(carbon_input_volume.shape, bf16)
    raw_v = pltpu.VMEM(raw.shape, bf16)
    taps_v = pltpu.VMEM(conv_fine.shape, bf16)
    x_scratch = pltpu.VMEM((2 * gy * cells, wide), f32)
    wide_scratch = pltpu.VMEM((devices * 2 * cells, wide), f32)
    left_scratch = pltpu.VMEM((cells * CH, local * devices * 2), bf16)
    mode_field = struct((2 * modes, wide))
    mode_v = pltpu.VMEM(mode_field.shape, f32)
    rows = modes * CH
    packed = struct((rows, 2 * wide), bf16)
    bands_v = pltpu.VMEM((2, 12 * CH, 24 * CH), bf16)
    side = struct((rows_y, 3, CH, span), bf16)
    message = struct((6, CH, span), bf16)
    y_side = struct((3, 10 * CH, span), bf16)
    y_message = struct((12, CH, span), bf16)

    with jax.named_scope("arrive"):
        u, one, two, my_x = run(
            arrive_kernel,
            [(IN_HBM, carbon_input_volume), (IN_HBM, forward_x)],
            [
                (IN_VMEM, round_field),
                (IN_VMEM, side),
                (IN_VMEM, side),
                (IN_VMEM, struct(forward_x.shape, bf16)),
            ],
            limit,
            [raw_v],
            copies=2,
        )
    one, two = swaps((one, two), "gz")

    def spread(values, table, exact, *others):
        with jax.named_scope("spread"):
            return run(
                lambda *refs: spread_kernel(exact, local, gy, gz, *refs),
                [(IN_VMEM, array) for array in (values, table) + others],
                [(IN_HBM, chunk)] + [(IN_HBM, struct(x.shape, x.dtype)) for x in others],
                limit,
                [x_scratch, sent],
                copies=2 + len(others),
                micros=1.2,
            )

    received = exchange(spread(u, my_x, True)[0])

    with jax.named_scope("y_message"):
        own_one, own_two = run(
            y_message_kernel,
            [(IN_VMEM, u), (IN_VMEM, one), (IN_VMEM, two)],
            [(IN_HBM, y_side), (IN_HBM, y_side)],
            limit,
            [pltpu.VMEM((rows_y, 10 * CH, span), bf16)],
            copies=2,
        )
    one, two = swaps((own_one, own_two), "gy")

    with jax.named_scope("setup"):
        w_high, w_low, my_there, my_back, w_kept = run(
            lambda *refs: setup_kernel(local, *refs),
            [
                (IN_HBM, spec_weight.reshape(2, local, rows, CH)),
                (IN_HBM, there),
                (IN_HBM, back),
            ],
            [
                (IN_VMEM, packed),
                (IN_VMEM, packed),
                (IN_VMEM, struct(there.shape[1:], bf16)),
                (IN_VMEM, struct(back.shape[1:], bf16)),
                (IN_HBM, packed),
            ],
            limit + (10 << 20),
            [pltpu.VMEM((2, local, rows, CH), f32)],
            copies=10,
            micros=4.5,
        )

    with jax.named_scope("mix"):
        v, send = run(
            lambda *refs: mix_kernel(local, *refs),
            [
                (IN_VMEM, received),
                (IN_VMEM, my_there),
                (IN_VMEM, w_high),
                (IN_VMEM, w_low),
                (IN_VMEM, my_back),
            ],
            [(IN_HBM, mode_field), (IN_HBM, chunk)],
            limit,
            [mode_v, sent],
            copies=5,
            micros=3,
        )
    received = exchange(send)

    with jax.named_scope("forward_convs"):
        base, fine, coarse, cot, my_inverse, my_x = run(
            forward_conv_kernel,
            [
                (IN_HBM, own_one),
                (IN_HBM, own_two),
                (IN_HBM, one),
                (IN_HBM, two),
                (IN_VMEM, lin_weight),
                (IN_HBM, conv_fine),
                (IN_HBM, conv_coarse),
                (IN_VMEM, bias_fine[None]),
                (IN_VMEM, bias_coarse[None]),
                (IN_HBM, cotangent),
                (IN_HBM, inverse_table),
                (IN_HBM, forward_x),
            ],
            [
                (IN_VMEM, field),
                (IN_HBM, struct((8, 8 * CH, span), bf16)),
                (IN_VMEM, struct((2, 2, CH, span // 2), bf16)),
                (IN_VMEM, round_field),
                (IN_VMEM, struct(inverse_table.shape, bf16)),
                (IN_VMEM, struct(forward_x.shape, bf16)),
            ],
            limit,
            [
                pltpu.VMEM((10, 12 * CH, span), bf16),
                taps_v,
                taps_v,
                raw_v,
                bands_v,
                pltpu.VMEM((4, 8 * CH, span // 2), bf16),
                pltpu.VMEM((8, 8 * CH, span), bf16),
            ],
            copies=10,
            micros=7,
        )

    with jax.named_scope("middle"):
        activated, grad, grad_round, one, two = run(
            lambda *refs: middle_kernel(local, *refs),
            [
                (IN_VMEM, received),
                (IN_VMEM, my_inverse),
                (IN_VMEM, base),
                (IN_VMEM, cot),
                (IN_VMEM, coarse),
            ],
            [
                (IN_VMEM, round_field),
                (IN_VMEM, field),
                (IN_VMEM, struct((cells + 2, CH, span), bf16)),
                (IN_VMEM, message),
                (IN_VMEM, message),
            ],
            limit,
            [wide_scratch, left_scratch],
            micros=2,
        )
    one, two = swaps((one, two), "gz")
    send, grad, activated, grad_round = spread(grad, my_x, False, grad, activated, grad_round)
    received = exchange(send)

    with jax.named_scope("y_gradient"):
        kept_z, one, two = run(
            y_gradient_kernel,
            [(IN_HBM, grad_round), (IN_VMEM, one), (IN_VMEM, two)],
            [
                (IN_HBM, struct((2,) + message.shape, bf16)),
                (IN_VMEM, y_message),
                (IN_VMEM, y_message),
            ],
            limit,
            [
                pltpu.VMEM((cells + 2, CH, span), bf16),
                pltpu.VMEM((2,) + message.shape, bf16),
            ],
            copies=2,
            micros=20,
        )
    one, two = swaps((one, two), "gy")
    with jax.named_scope("turn"):
        predicted, my_there, my_w, my_back = run(
            turn_kernel,
            [
                (IN_HBM, activated),
                (IN_HBM, there),
                (IN_HBM, w_kept),
                (IN_HBM, back),
            ],
            [
                (IN_HBM, raw),
                (IN_VMEM, struct(there.shape[1:], bf16)),
                (IN_VMEM, packed),
                (IN_VMEM, struct(back.shape[1:], bf16)),
            ],
            limit,
            [round_v, raw_v],
            copies=5,
            micros=2,
        )

    with jax.named_scope("mix_adjoint"):
        d, send = run(
            lambda *refs: adjoint_kernel(local, *refs),
            [(IN_VMEM, received), (IN_VMEM, my_there), (IN_VMEM, my_w), (IN_VMEM, my_back)],
            [(IN_VMEM, mode_field), (IN_HBM, chunk)],
            limit,
            [sent],
            copies=4,
            micros=2,
        )
    received = exchange(send)

    with jax.named_scope("backward"):
        weight_grad, base, my_inverse = run(
            backward_kernel,
            [
                (IN_VMEM, d),
                (IN_VMEM, v),
                (IN_HBM, grad),
                (IN_HBM, grad_round),
                (IN_HBM, kept_z),
                (IN_HBM, one),
                (IN_HBM, two),
                (IN_HBM, fine),
                (IN_VMEM, lin_weight),
                (IN_HBM, conv_fine),
                (IN_HBM, conv_coarse),
                (IN_HBM, inverse_table),
            ],
            [
                (IN_HBM, struct((2, local, rows, CH))),
                (IN_VMEM, field),
                (IN_VMEM, struct(inverse_table.shape, bf16)),
            ],
            limit + (10 << 20),
            [
                pltpu.VMEM((2, local, rows, CH), f32),
                field_v,
                pltpu.VMEM((cells + 2, CH, span), bf16),
                pltpu.VMEM((2,) + message.shape, bf16),
                pltpu.VMEM((2,) + y_message.shape, bf16),
                pltpu.VMEM((8, 8 * CH, span), bf16),
                taps_v,
                taps_v,
                bands_v,
                pltpu.VMEM((6, 8 * CH, span // 2), bf16),
                pltpu.VMEM((6, 8 * CH, span), bf16),
            ],
            copies=9 + local,
            micros=6,
        )
    weight_grad = weight_grad.reshape(spec_weight.shape)

    with jax.named_scope("last"):
        (sensitivity,) = run(
            lambda *refs: last_kernel(local, *refs),
            [(IN_VMEM, received), (IN_VMEM, my_inverse), (IN_VMEM, base)],
            [(IN_HBM, raw)],
            limit,
            [raw_v, wide_scratch, left_scratch],
            copies=1,
            micros=2,
        )
    return (predicted, sensitivity, weight_grad)


def solution(mesh):
    field = P(None, "gy", "gz", None)
    modes = P(None, "gy", "gz", None, None, None)
    return jax.shard_map(
        shards,
        mesh=mesh,
        in_specs=(field, field, modes, P(), P(), P(), P(), P()),
        out_specs=(field, field, modes),
        check_vma=False,
    )
```

```python
import math

import jax
import jax.numpy as jnp
import ml_dtypes
import numpy as np
from jax import lax
from jax.experimental import pallas as pl
from jax.experimental.pallas import tpu as pltpu
from jax.sharding import PartitionSpec as P

MX = 32
MY = 32
MZ = 8
CH = 32
BOTH = ("gy", "gz")

f32 = jnp.float32
bf16 = jnp.bfloat16
root_coef = math.sqrt(2.0 / math.pi)
NN = (((1,), (0,)), ((), ()))
NT = (((1,), (1,)), ((), ()))
TN = (((0,), (0,)), ((), ()))


def dot(a, b, form=NN):
    return lax.dot_general(a, b, form, preferred_element_type=f32)


def halves(value):
    high = value.astype(bf16)
    return high, (value - high.astype(f32)).astype(bf16)


def iota(shape, dim):
    return lax.broadcasted_iota(jnp.int32, shape, dim)


IN_VMEM = pl.BlockSpec(memory_space=pltpu.VMEM)
IN_HBM = pl.BlockSpec(memory_space=pltpu.HBM)


def struct(shape, kind=f32):
    return jax.ShapeDtypeStruct(shape, kind)


def run(kernel, ins, outs, limit, scratch=(), micros=1.0, copies=0, **grid):
    scratch = list(scratch)
    if copies:
        scratch.append(pltpu.SemaphoreType.DMA((copies,)))
    held = {id(IN_HBM): pltpu.HBM, id(IN_VMEM): pltpu.VMEM}

    def placed(spec, array):
        if id(spec) in held:
            return pltpu.with_memory_space_constraint(array, held[id(spec)])
        return array

    def shaped(spec, shape):
        if id(spec) in held:
            return held[id(spec)](shape.shape, shape.dtype)
        return shape

    return pl.pallas_call(
        kernel,
        in_specs=[spec for spec, _ in ins],
        out_specs=[spec for spec, _ in outs],
        out_shape=[shaped(spec, shape) for spec, shape in outs],
        scratch_shapes=scratch,
        compiler_params=pltpu.CompilerParams(vmem_limit_bytes=limit),
        cost_estimate=pl.CostEstimate(
            flops=int(micros * 1.1e9), bytes_accessed=1 << 16, transcendentals=0
        ),
        **grid,
    )(*[placed(spec, array) for spec, array in ins])


def begin(sem, first, *pairs):
    copies = [
        pltpu.make_async_copy(source, target, sem.at[first + i])
        for i, (source, target) in enumerate(pairs)
    ]
    for copy in copies:
        copy.start()
    return copies


def finish(*copies):
    for copy in copies:
        copy.wait()


def kept(count, length):
    position = np.arange(count)
    return np.where(position < count // 2, position, length - count + position)


def split_np(table):
    high = table.astype(ml_dtypes.bfloat16)
    return high, (table - high.astype(np.float64)).astype(ml_dtypes.bfloat16)


def x_tables(cells_x, blocks):
    local = MX // blocks
    freqs = kept(MX, cells_x).reshape(blocks, local).T
    angles = 2.0 * np.pi * ((freqs[:, :, None] * np.arange(cells_x)) % cells_x) / cells_x
    table = np.stack([np.cos(angles), -np.sin(angles)], axis=2).reshape(2 * MX, cells_x)
    return np.concatenate(split_np(table), axis=0)


def x_back_table(cells_x, gy, gz):
    local = MX // gy
    freqs = kept(MX, cells_x).reshape(gy, local).T
    angles = 2.0 * np.pi * ((freqs[:, :, None] * np.arange(cells_x)) % cells_x) / cells_x
    table = np.stack([np.cos(angles), -np.sin(angles)], axis=2)
    table = np.broadcast_to(table[:, :, None], (local, gy, gz, 2, cells_x))
    return np.concatenate(split_np(table.reshape(-1, cells_x)), axis=0)


def yz_angles(xp, freqs_y, gy, gz, rows_y, rows_z):
    span_y, span_z = gy * rows_y, gz * rows_z
    phase_y = (freqs_y[:, None] * xp.arange(span_y)[None]) % span_y
    phase_z = (xp.arange(MZ)[:, None] * xp.arange(span_z)[None]) % span_z
    phase_y = phase_y.reshape(-1, 1, gy, 1, rows_y, 1)
    phase_z = phase_z.reshape(1, MZ, 1, gz, 1, rows_z)
    turn = (phase_y * span_z + phase_z * span_y) % (span_y * span_z)
    return turn.reshape(turn.shape[0] * MZ, gy * gz, rows_y * rows_z)


def yz_table(xp, freqs_y, gy, gz, rows_y, rows_z):
    cells = gy * gz * rows_y * rows_z
    turn = yz_angles(xp, freqs_y, gy, gz, rows_y, rows_z)
    angles = 2.0 * math.pi / cells * turn
    cosine, sine = xp.cos(angles), xp.sin(angles)
    table = xp.stack([xp.stack([cosine, sine], 2), xp.stack([-sine, cosine], 2)], 0)
    return table.reshape(2 * turn.shape[0], -1)


def mode_tables(gy, gz, rows_y, rows_z, scale):
    local = MY // gz
    cells = gy * gz * rows_y * rows_z
    freqs = kept(MY, gy * rows_y).reshape(gz, local)
    if gz * 2 * local * MZ * 2 * cells <= 1 << 20:
        there, back = [], []
        for block in range(gz):
            high, low = split_np(scale * yz_table(np, freqs[block], gy, gz, rows_y, rows_z))
            there.append(np.concatenate([high, low], 0))
            back.append(np.concatenate([high.T, low.T], 1))
        return jnp.asarray(np.stack(there)), jnp.asarray(np.stack(back))
    where = lax.axis_index("gz")
    mine = lax.dynamic_index_in_dim(jnp.asarray(freqs, jnp.int32), where, keepdims=False)
    high, low = halves(scale * yz_table(jnp, mine, gy, gz, rows_y, rows_z).astype(f32))
    return jnp.concatenate([high, low], 0)[None], jnp.concatenate([high.T, low.T], 1)[None]


def put_x_modes(product, local, blocks, copies, cells, scratch, sent, send_ref, sem, first):
    rows = 2 * blocks
    half = blocks // 2
    moves = []
    for start in (0, half):
        at = 2 * start * cells
        for cell in range(cells):
            piece = product[:, cell * CH : (cell + 1) * CH]
            parts = [piece[k * rows + 2 * start : k * rows + 2 * start + blocks] for k in range(local)]
            scratch[pl.ds(at + cell, blocks, stride=cells), :] = jnp.concatenate(parts, axis=1)
        for block in range(start, start + half):
            value = scratch[block * 2 * cells : (block + 1) * 2 * cells].astype(bf16)
            for copy in range(copies):
                sent[block * copies + copy] = value
        part = pl.ds(start * copies, half * copies)
        moves += begin(sem, first + len(moves), (sent.at[part], send_ref.at[part]))
    return moves


def odd(axis):
    return lax.axis_index(axis) & 1


def first(axis):
    return lax.axis_index(axis) == 0


def last(axis):
    return lax.axis_index(axis) == lax.axis_size(axis) - 1


def arrive_kernel(raw_ref, table_ref, u_ref, one_ref, two_ref, my_table_ref, raw, sem):
    loads = begin(sem, 0, (raw_ref, raw), (table_ref, my_table_ref))
    finish(*loads)
    u = jnp.transpose(raw[...], (1, 2, 0, 3))
    u_ref[...] = u
    side = odd("gz")
    one_ref[...] = u_ref[:, pl.ds(1 - side, 3)]
    two_ref[...] = u_ref[:, pl.ds(side, 3)]


def spread_kernel(
    exact, local, blocks, copies, u_ref, table, *refs
):
    *refs, scratch, sent, sem = refs
    count = len(refs) // 2
    stores = begin(sem, 2, *zip(refs[:count], refs[count + 1 :]))
    send_ref = refs[count]
    cells = u_ref.shape[0] * u_ref.shape[1]
    u = u_ref[...].reshape(cells * CH, -1)
    if exact:
        both = dot(table[...], u, NT)
        product = both[: 2 * MX] + both[2 * MX :]
    else:
        high, low = halves(u)
        both = dot(table[...], high, NT)
        product = both[: 2 * MX] + both[2 * MX :] + dot(table[: 2 * MX], low, NT)
    moves = put_x_modes(product, local, blocks, copies, cells, scratch, sent, send_ref, sem, 0)
    finish(*moves, *stores)


def pick(tables_ref):
    if tables_ref.shape[0] == 1:
        return tables_ref.at[0]
    return tables_ref.at[lax.axis_index("gz")]


def mode_values(rec_ref, there, rows):
    both = dot(there[...], rec_ref[...].reshape(-1, rec_ref.shape[2]))
    return both[:rows] + both[rows:]


def put_back(values, back_ref, sent, send_ref, sem, first):
    high, low = halves(values)
    twice = jnp.concatenate([high, high], 0)
    rows = values.shape[0]
    devices, depth, wide = sent.shape
    part = devices // 4
    moves = []
    for step in range(4):
        at = slice(step * part * depth, (step + 1) * part * depth)
        result = dot(back_ref[at], twice) + dot(back_ref[at, :rows], low)
        sent[step * part : (step + 1) * part] = result.astype(bf16).reshape(part, depth, wide)
        span = pl.ds(step * part, part)
        moves += begin(sem, first + step, (sent.at[span], send_ref.at[span]))
    finish(*moves)


def kz_weight(shape):
    return jnp.where(iota(shape, 0) % MZ == 0, 1.0, 2.0).astype(f32)


def same_mode(rows, lanes):
    return (iota((rows, lanes), 0) % MZ) == ((iota((rows, lanes), 1) // CH) % MZ)


def mix_kernel(
    local,
    rec_ref,
    there_ref,
    high_ref,
    low_ref,
    back_ref,
    v_ref,
    kept_w_ref,
    send_ref,
    kept_v,
    sent,
    sem,
):
    store_w = begin(sem, 5, (high_ref, kept_w_ref))
    rows = there_ref.shape[0] // 2
    modes = rows // 2
    wide = local * CH
    v = mode_values(rec_ref, there_ref, rows)
    kept_v[...] = v
    store = begin(sem, 0, (kept_v, v_ref))
    real, imag = v[:modes], v[modes:]
    pair = (
        jnp.concatenate([real, -imag], 1),
        jnp.concatenate([imag, real], 1),
    )
    lane_k = (iota((MZ, 2 * wide), 1) // CH) % local
    size = MZ * CH
    diag = same_mode(2 * MZ * local, size)
    placed = [[[None] * (modes // MZ) for _ in range(local)] for _ in range(2)]
    for g in range(modes // MZ):
        pieces = []
        for k in range(local):
            for part in range(2):
                piece = pair[part][g * MZ : (g + 1) * MZ]
                pieces.append(jnp.where(lane_k == k, piece, 0.0))
        left_high, left_low = halves(jnp.concatenate(pieces, 0))
        w_high = high_ref[g * size : (g + 1) * size]
        w_low = low_ref[g * size : (g + 1) * size]
        count = left_high.shape[0]
        both = dot(jnp.concatenate([left_high, left_low], 0), w_high, NT)
        value = both[:count] + both[count:] + dot(left_high, w_low, NT)
        value = jnp.where(diag, value, 0.0)
        for k in range(local):
            for part in range(2):
                at = (2 * k + part) * MZ
                placed[part][k][g] = value[at : at + MZ]
    columns = [jnp.concatenate(placed[0][k] + placed[1][k], 0) for k in range(local)]
    all_values = jnp.concatenate(columns, 1)
    shape = (local * size, wide)
    fold = (iota(shape, 0) // size == iota(shape, 1) // CH) & (
        iota(shape, 0) % CH == iota(shape, 1) % CH
    )
    fold = fold.astype(bf16)
    high, low = halves(all_values)
    mixed = dot(high, fold) + dot(low, fold)
    put_back(mixed * kz_weight(mixed.shape), back_ref, sent, send_ref, sem, 1)
    finish(*store, *store_w)


def adjoint_kernel(
    local,
    rec_ref,
    there_ref,
    high_ref,
    back_ref,
    rep_ref,
    d_ref,
    send_ref,
    sent,
    sem,
):
    rows = there_ref.shape[0] // 2
    modes = rows // 2
    wide = local * CH
    size = MZ * CH
    d = mode_values(rec_ref, there_ref, rows)
    d = d * kz_weight(d.shape)
    d_ref[...] = d
    high, low = halves(d)
    spread = dot(high, rep_ref[...]) + dot(low, rep_ref[...])
    spread = jnp.where(same_mode(rows, local * size), spread, 0.0)
    lane_k = (iota((2 * MZ, 2 * wide), 1) // CH) % local
    parts = ([], [])
    for g in range(modes // MZ):
        pieces = []
        for k in range(local):
            for part in range(2):
                at = part * modes + g * MZ
                pieces.append(spread[at : at + MZ, k * size : (k + 1) * size])
        left_high, left_low = halves(jnp.concatenate(pieces, 0))
        count = left_high.shape[0]
        both = dot(
            jnp.concatenate([left_high, left_low], 0), high_ref[g * size : (g + 1) * size]
        )
        value = both[:count] + both[count:]
        total = None
        for k in range(local):
            piece = jnp.where(lane_k == k, value[2 * k * MZ : 2 * (k + 1) * MZ], 0.0)
            total = piece if total is None else total + piece
        parts[0].append(total[:MZ])
        parts[1].append(total[MZ:])
    real = jnp.concatenate(parts[0], 0)
    imag = jnp.concatenate(parts[1], 0)
    value = jnp.concatenate(
        [real[:, :wide] + imag[:, wide:], imag[:, :wide] - real[:, wide:]], 0
    )
    put_back(value, back_ref, sent, send_ref, sem, 0)


def setup_kernel(
    local,
    w_ref,
    there_ref,
    back_ref,
    high_ref,
    low_ref,
    my_there_ref,
    my_back_ref,
    w,
    sem,
):
    parts = 8
    rows = w.shape[2] // parts
    spans = [pl.ds(step * rows, rows) for step in range(parts)]
    loads = begin(sem, 0, *[(w_ref.at[:, :, span], w.at[:, :, span]) for span in spans])
    tables = begin(
        sem, parts, (pick(there_ref), my_there_ref), (pick(back_ref), my_back_ref)
    )
    for step in range(parts):
        at = slice(step * rows, (step + 1) * rows)
        finish(loads[step])
        pieces = [w[part, k, at] for part in range(2) for k in range(local)]
        high_ref[at], low_ref[at] = halves(jnp.concatenate(pieces, 1))
    finish(*tables)


def put_weight_grad(d_ref, v_ref, out, out_ref, sem, first):
    rows, wide = d_ref.shape
    modes = rows // 2
    size = MZ * CH
    keep = same_mode(rows, size)
    d_halves = halves(d_ref[...])
    v_halves = halves(v_ref[...])
    stores = []
    for k in range(wide // CH):
        shape = (wide, size)
        rep = (iota(shape, 0) == k * CH + iota(shape, 1) % CH).astype(bf16)
        d_high, d_low = [jnp.where(keep, dot(value, rep), 0.0) for value in d_halves]
        at = slice(k * CH, (k + 1) * CH)
        v_high, v_low = [value[:, at].astype(f32) for value in v_halves]
        for g in range(modes // MZ):
            real = slice(g * MZ, (g + 1) * MZ)
            imag = slice(modes + g * MZ, modes + (g + 1) * MZ)
            left = jnp.concatenate(
                [d_high[real], d_high[imag], d_low[real], d_low[imag], d_high[real], d_high[imag]],
                0,
            ).astype(bf16)
            for part in range(2):
                rights = []
                for v in (v_high, v_high, v_low):
                    rights += [v[real], v[imag]] if part == 0 else [-v[imag], v[real]]
                right = jnp.concatenate(rights, 0).astype(bf16)
                out[part, k, g * size : (g + 1) * size, :] = dot(left, right, TN)
        stores += begin(sem, first + k, (out.at[:, k], out_ref.at[:, k]))
    return stores


def widen(rec_ref, wide):
    wide[...] = rec_ref[...].reshape(-1, rec_ref.shape[2]).astype(f32)


def inverse_x(wide, table, local, cells, part, left):
    rows = wide.shape[0] // cells
    for cell in part:
        turned = wide[pl.ds(cell, rows, stride=cells), :].T.astype(bf16)
        for k in range(local):
            left[cell * CH : (cell + 1) * CH, k * rows : (k + 1) * rows] = turned[
                k * CH : (k + 1) * CH
            ]
    depth = local * rows
    value = left[part.start * CH : part.stop * CH]
    return dot(value, table[:depth]) + dot(value, table[depth:])


def gelu_pair(pre_act):
    cube_term = pre_act * pre_act * pre_act
    tanh_result = jnp.tanh(root_coef * (pre_act + 0.044715 * cube_term))
    activated_output = 0.5 * pre_act * (1.0 + tanh_result)
    gelu_slope = 0.5 * (1.0 + tanh_result) + 0.5 * pre_act * (
        1.0 - tanh_result * tanh_result
    ) * root_coef * (1.0 + 3.0 * 0.044715 * pre_act * pre_act)
    return (activated_output, gelu_slope)


def middle_kernel(
    local,
    rec_ref,
    back_ref,
    base_ref,
    cot_ref,
    coarse_ref,
    out_ref,
    grad_ref,
    rounded,
    one_ref,
    two_ref,
    wide,
    left,
):
    rows_y, rows_z, _, span = base_ref.shape
    cells = rows_y * rows_z
    widen(rec_ref, wide)
    pre_act = inverse_x(wide, back_ref, local, cells, range(cells), left)
    pre_act = pre_act + base_ref[...].reshape(pre_act.shape)
    activated, slope = gelu_pair(pre_act)
    out_ref[...] = activated.astype(bf16).reshape(out_ref.shape)
    value = cot_ref[...].astype(f32).reshape(pre_act.shape) * slope
    grad_ref[...] = value.reshape(grad_ref.shape)
    rounded[:cells] = value.astype(bf16).reshape(cells, CH, span)
    side = odd("gz")
    for y in range(rows_y):
        one_ref[y] = rounded[rows_z * y + (rows_z - 1) * (1 - side)]
        two_ref[y] = rounded[rows_z * y + (rows_z - 1) * side]
    pool = pool_matrix(span)
    for yc in range(2):
        sums = []
        for zc in range(2):
            y, z = 2 * yc, 2 * zc
            sums.append(
                grad_ref[y, z] + grad_ref[y, z + 1] + grad_ref[y + 1, z] + grad_ref[y + 1, z + 1]
            )
        total_high, total_low = halves(jnp.concatenate(sums, 0))
        total = dot(total_high, pool) + dot(total_low, pool)
        pieces = []
        for zc in range(2):
            piece = total[zc * CH : (zc + 1) * CH]
            pieces.append(jnp.where(coarse_ref[yc, zc].astype(f32) > 0, piece, 0.0))
        piece = jnp.concatenate(pieces, 1).astype(bf16)
        rounded[cells + yc] = piece
        one_ref[rows_y + yc] = piece
        two_ref[rows_y + yc] = piece


def last_kernel(local, rec_ref, back_ref, base_ref, out_ref, out, wide, left, sem):
    rows_y, rows_z, _, span = base_ref.shape
    cells = rows_y * rows_z
    widen(rec_ref, wide)
    moves = []
    for y in range(0, rows_y, 2):
        part = range(y * rows_z, (y + 2) * rows_z)
        value = inverse_x(wide, back_ref, local, cells, part, left)
        value = value.reshape(2, rows_z, CH, span) + base_ref[y : y + 2]
        out[:, y : y + 2] = jnp.transpose(value.astype(bf16), (2, 0, 1, 3))
        at = pl.ds(y, 2)
        moves += begin(sem, y // 2, (out.at[:, at], out_ref.at[:, at]))
    finish(*moves)


def turn_kernel(
    value_ref,
    there_ref,
    w_ref,
    back_ref,
    out_ref,
    my_there_ref,
    my_w_ref,
    my_back_ref,
    rep_ref,
    value,
    out,
    sem,
):
    loads = begin(
        sem,
        0,
        (value_ref, value),
        (pick(there_ref), my_there_ref),
        (w_ref, my_w_ref),
        (pick(back_ref), my_back_ref),
    )
    shape = rep_ref.shape
    size = MZ * CH
    rep = (iota(shape, 1) // size == iota(shape, 0) // CH) & (
        iota(shape, 1) % CH == iota(shape, 0) % CH
    )
    rep_ref[...] = rep.astype(bf16)
    finish(loads[0])
    out[...] = jnp.transpose(value[...], (2, 0, 1, 3))
    finish(*begin(sem, 4, (out, out_ref)), *loads[1:])


def write_bands(adjoint, k_ref, out, index):
    for a in range(3):
        for e in range(3):
            taps = []
            for b in range(3):
                if adjoint:
                    tap = k_ref[9 * (2 - a) + 3 * (2 - b) + 2 - e].astype(f32).T
                else:
                    tap = k_ref[9 * a + 3 * b + e].astype(f32)
                taps.append(tap)
            taps = jnp.concatenate(taps, 1)
            for z in range(4):
                pieces = [taps, jnp.zeros((CH, (5 - z) * CH), f32)]
                if z > 0:
                    pieces.insert(0, jnp.zeros((CH, z * CH), f32))
                row = jnp.concatenate(pieces, 1)
                at = (e * 4 + z) * CH
                out[index, at : at + CH, a * 8 * CH : (a + 1) * 8 * CH] = row.astype(bf16)


def x_sum(low, same, high):
    span = same.shape[1]
    lane = iota(same.shape, 1)
    before = jnp.where(lane == 0, 0.0, pltpu.roll(low, 1, axis=1))
    after = jnp.where(lane == span - 1, 0.0, pltpu.roll(high, span - 1, axis=1))
    return same + before + after


def band_conv(bands, planes):
    value = dot(bands, jnp.concatenate(planes, 0))
    size = 4 * CH
    return x_sum(value[:size], value[size : 2 * size], value[2 * size :])


def column(row_ref, copies):
    eye = iota((CH, CH), 0) == iota((CH, CH), 1)
    value = jnp.sum(jnp.where(eye, row_ref[...], 0.0), axis=1, keepdims=True)
    return jnp.concatenate([value] * copies, 0)


def block_diagonal(matrix):
    shape = (4 * CH, 4 * CH)
    wide = jnp.concatenate([matrix.astype(f32)] * 4, 1)
    tiled = jnp.concatenate([wide] * 4, 0)
    return jnp.where(iota(shape, 0) // CH == iota(shape, 1) // CH, tiled, 0.0).astype(bf16)


def pool_matrix(span):
    shape = (span, span // 2)
    return (iota(shape, 0) // 2 == iota(shape, 1)).astype(bf16)


def up_matrix(span):
    shape = (span // 2, span)
    return (iota(shape, 1) // 2 == iota(shape, 0)).astype(bf16)


def y_message_kernel(u_ref, z_one_ref, z_two_ref, one_ref, two_ref, rows, sem):
    side = odd("gz")
    for y in range(4):
        for z in range(3):
            at = pl.multiple_of((7 * (1 - side) + z) * CH, CH)
            rows[y, pl.ds(at, CH)] = z_one_ref[y, z]
            at = pl.multiple_of((7 * side + z) * CH, CH)
            rows[y, pl.ds(at, CH)] = z_two_ref[y, z]
        for z in range(4):
            rows[y, (z + 3) * CH : (z + 4) * CH] = u_ref[y, z]
    blank = jnp.zeros((4, 3 * CH, rows.shape[2]), bf16)

    @pl.when(first("gz"))
    def low_end():
        rows[:, : 3 * CH] = blank

    @pl.when(last("gz"))
    def high_end():
        rows[:, 7 * CH :] = blank

    side = odd("gy")
    finish(
        *begin(
            sem, 0, (rows.at[pl.ds(1 - side, 3)], one_ref), (rows.at[pl.ds(side, 3)], two_ref)
        )
    )


def forward_conv_kernel(
    own_one_ref,
    own_two_ref,
    y_one_ref,
    y_two_ref,
    lin_ref,
    taps_fine_ref,
    taps_coarse_ref,
    bias_fine_ref,
    bias_coarse_ref,
    cot_ref,
    table_ref,
    x_ref,
    base,
    fine_ref,
    coarse,
    my_cot_ref,
    my_table_ref,
    my_x_ref,
    grid,
    taps_fine,
    taps_coarse,
    raw,
    bands,
    pooled,
    fine,
    sem,
):
    span = grid.shape[2]
    inner = pl.ds(0, 10 * CH)
    side = odd("gy")
    loads = begin(
        sem,
        0,
        (taps_fine_ref, taps_fine),
        (own_one_ref, grid.at[pl.ds(4 - side, 3), inner]),
        (own_two_ref.at[pl.ds(2 * side, 1)], grid.at[pl.ds(3 + 3 * side, 1), inner]),
        (y_one_ref, grid.at[pl.ds(7 * (1 - side), 3), inner]),
        (y_two_ref, grid.at[pl.ds(7 * side, 3), inner]),
        (taps_coarse_ref, taps_coarse),
        (cot_ref, raw),
        (table_ref, my_table_ref),
        (x_ref, my_x_ref),
    )
    edges = [jnp.logical_not(end(axis)) for axis in ("gy", "gz") for end in (first, last)]
    grid[:, 10 * CH :, :] = jnp.zeros((10, 2 * CH, span), bf16)
    pooled[:, 4 * CH :, :] = jnp.zeros((4, 4 * CH, span // 2), bf16)
    bias = column(bias_fine_ref, 4)
    half = 4 * CH
    row_z = iota((half, span), 0) // CH
    finish(loads[0])
    write_bands(False, taps_fine, bands, 0)
    finish(*loads[1:3])
    for y in (3, 4, 2, 1, 0, 5, 6, 7):
        if y == 2:
            finish(loads[3], loads[4])

            @pl.when(first("gy"))
            def low_end():
                grid[:3] = jnp.zeros((3, 12 * CH, span), bf16)

            @pl.when(last("gy"))
            def high_end():
                grid[7:] = jnp.zeros((3, 12 * CH, span), bf16)

        y_in = None
        if y < 2:
            y_in = edges[0]
        elif y >= 6:
            y_in = edges[1]
        for h in range(2):
            at = h * half
            value = band_conv(bands[0], [grid[y + a, at : at + 8 * CH, :] for a in range(3)])
            value = jnp.maximum(value + bias, 0.0)
            inside = (row_z >= 2) | edges[2] if h == 0 else (row_z < 2) | edges[3]
            if y_in is not None:
                inside = inside & y_in
            fine[y, at : at + half, :] = jnp.where(inside, value, 0.0).astype(bf16)
    (store,) = begin(sem, 9, (fine, fine_ref))
    sums = []
    for yc in range(4):
        both = fine[2 * yc].astype(f32) + fine[2 * yc + 1].astype(f32)
        for zc in range(4):
            at = 2 * zc * CH
            sums.append(both[at : at + CH] + both[at + CH : at + 2 * CH])
    pool = pool_matrix(span)
    high, low = halves(jnp.concatenate(sums, 0))
    pools = (0.125 * (dot(high, pool) + dot(low, pool))).astype(bf16)
    pooled[:, : 4 * CH, :] = pools.reshape(4, 4 * CH, span // 2)
    bias = column(bias_coarse_ref, 4)
    finish(loads[5])
    write_bands(False, taps_coarse, bands, 1)
    planes = [jnp.concatenate([pooled[a], pooled[a + 1]], 1) for a in range(3)]
    value = dot(bands[1], jnp.concatenate(planes, 0))
    parts = [value[e * half : (e + 1) * half] for e in range(3)]
    for yc in range(2):
        at = slice(yc * span // 2, (yc + 1) * span // 2)
        value = x_sum(*[part[:, at] for part in parts])
        value = jnp.maximum(value + bias, 0.0).astype(bf16)
        coarse[yc] = value[: 2 * CH].reshape(2, CH, span // 2)
    lifted = dot(coarse[...].reshape(half, span // 2), up_matrix(span))
    lin = block_diagonal(lin_ref[...])
    for y in range(4):
        total = dot(lin, grid[y + 3, 3 * CH : 7 * CH, :])
        total = total + fine[y + 2, 2 * CH : 6 * CH, :].astype(f32)
        for z in range(4):
            at = (y // 2 * 2 + z // 2) * CH
            base[y, z] = total[z * CH : (z + 1) * CH] + lifted[at : at + CH]
    finish(loads[6])
    my_cot_ref[...] = jnp.transpose(raw[...], (1, 2, 0, 3))
    finish(store, *loads[7:])


def y_gradient_kernel(
    round_ref, z_one_ref, z_two_ref, kept_ref, one_ref, two_ref, own, halo, sem
):
    (load,) = begin(sem, 0, (round_ref, own))
    side = odd("gz")
    halo[1 - side] = z_one_ref[...]
    halo[side] = z_two_ref[...]

    @pl.when(first("gz"))
    def low_end():
        halo[0] = jnp.zeros(halo.shape[1:], bf16)

    @pl.when(last("gz"))
    def high_end():
        halo[1] = jnp.zeros(halo.shape[1:], bf16)

    (store,) = begin(sem, 1, (halo, kept_ref))
    finish(load)
    side = odd("gy")
    for out_ref, y in ((one_ref, 3 * (1 - side)), (two_ref, 3 * side)):
        out_ref[0] = halo[0, y]
        out_ref[1:5] = own[pl.ds(4 * y, 4)]
        out_ref[5] = halo[1, y]
        for yc in range(2):
            out_ref[6 + 3 * yc] = halo[0, 4 + yc]
            out_ref[7 + 3 * yc] = own[16 + yc]
            out_ref[8 + 3 * yc] = halo[1, 4 + yc]
    finish(store)


def backward_kernel(
    d_ref,
    v_ref,
    grad_ref,
    round_ref,
    kept_ref,
    y_one_ref,
    y_two_ref,
    fine_ref,
    lin_ref,
    taps_fine_ref,
    taps_coarse_ref,
    table_ref,
    weight_ref,
    base,
    my_table_ref,
    weights,
    grad,
    rounded,
    kept,
    beside,
    fine,
    taps_fine,
    taps_coarse,
    bands,
    coarse_grid,
    fine_grid,
    sem,
):
    side = odd("gy")
    loads = begin(
        sem,
        0,
        (taps_coarse_ref, taps_coarse),
        (round_ref, rounded),
        (kept_ref, kept),
        (y_one_ref, beside.at[1 - side]),
        (y_two_ref, beside.at[side]),
        (grad_ref, grad),
        (fine_ref, fine),
        (taps_fine_ref, taps_fine),
        (table_ref, my_table_ref),
    )
    stores = put_weight_grad(d_ref, v_ref, weights, weight_ref, sem, 9)
    finish(loads[0], loads[7])
    write_bands(True, taps_coarse, bands, 1)
    write_bands(True, taps_fine, bands, 0)
    span = grad.shape[3]
    half = span // 2
    coarse_grid[:, 6 * CH :, :] = jnp.zeros((6, 2 * CH, half), bf16)
    fine_grid[:, 6 * CH :, :] = jnp.zeros((6, 2 * CH, span), bf16)

    def place(yc, pair, value):
        for zc in range(2):
            at = (2 * pair + zc) * CH
            coarse_grid[yc, at : at + CH, :] = value[:, zc * half : (zc + 1) * half]

    finish(*loads[1:5])

    @pl.when(first("gy"))
    def low_end():
        beside[0] = jnp.zeros(beside.shape[1:], bf16)

    @pl.when(last("gy"))
    def high_end():
        beside[1] = jnp.zeros(beside.shape[1:], bf16)

    for yc in range(2):
        place(2 + yc, 0, kept[0, 4 + yc])
        place(2 + yc, 1, rounded[16 + yc])
        place(2 + yc, 2, kept[1, 4 + yc])
        for pair in range(3):
            place(yc, pair, beside[0, 6 + 3 * yc + pair])
            place(4 + yc, pair, beside[1, 6 + 3 * yc + pair])
    pooled = [
        0.125 * band_conv(bands[1], [coarse_grid[yc + a] for a in range(3)]) for yc in range(4)
    ]
    high, low = halves(jnp.concatenate(pooled, 0))
    up = up_matrix(span)
    lifted = dot(high, up) + dot(low, up)
    finish(*loads[5:7])
    for y in range(6):
        yc = (y + 1) // 2
        for z in range(6):
            at = (4 * yc + (z + 1) // 2) * CH
            if 1 <= y <= 4 and 1 <= z <= 4:
                value = grad[y - 1, z - 1]
            elif 1 <= y <= 4:
                value = kept[z // 5, y - 1].astype(f32)
            else:
                value = beside[y // 5, z].astype(f32)
            value = value + lifted[at : at + CH]
            mask = fine[y + 1, (z + 1) * CH : (z + 2) * CH, :].astype(f32) > 0
            fine_grid[y, z * CH : (z + 1) * CH, :] = jnp.where(mask, value, 0.0).astype(bf16)
    lin = block_diagonal(lin_ref[...].astype(f32).T.astype(bf16))
    for y in range(4):
        value = band_conv(bands[0], [fine_grid[y + a] for a in range(3)])
        value = value + dot(lin, rounded[4 * y : 4 * y + 4].reshape(4 * CH, span))
        base[y] = value.reshape(4, CH, span)
    finish(loads[8], *stores)


def swaps(blocks, axis):
    size_y, size_z = lax.axis_size("gy"), lax.axis_size("gz")
    results = []
    for start, block in enumerate(blocks):
        pairs = []
        for y in range(size_y):
            for z in range(size_z):
                step = 1 if ((y if axis == "gy" else z) - start) % 2 == 0 else -1
                to_y, to_z = y, z
                if axis == "gy":
                    to_y = (y + step) % size_y
                elif 0 <= z + step < size_z:
                    to_z = z + step
                else:
                    to_y = y ^ 1
                pairs.append((y * size_z + z, to_y * size_z + to_z))
        results.append(lax.ppermute(block, BOTH, pairs))
    return results


def exchange(block):
    return lax.all_to_all(block, BOTH, split_axis=0, concat_axis=0, tiled=True)


def shards(
    carbon_input_volume,
    cotangent,
    spec_weight,
    lin_weight,
    conv_fine,
    bias_fine,
    conv_coarse,
    bias_coarse,
):
    channels, rows_y, rows_z, span = carbon_input_volume.shape
    gy, gz = lax.axis_size("gy"), lax.axis_size("gz")
    devices = gy * gz
    cells = rows_y * rows_z
    local = MX // gy
    modes = (MY // gz) * MZ
    wide = local * CH
    scale = 1.0 / math.sqrt(span * cells * devices)
    there, back = mode_tables(gy, gz, rows_y, rows_z, scale)
    forward_x = jnp.asarray(x_tables(span, gy))
    inverse_table = jnp.asarray(x_back_table(span, gy, gz))

    limit = (14 << 20) + devices * (64 << 10)
    chunk = struct((devices, 2 * cells, wide), bf16)
    sent = pltpu.VMEM(chunk.shape, bf16)
    field = struct((rows_y, rows_z, CH, span))
    field_v = pltpu.VMEM(field.shape, f32)
    round_field = struct(field.shape, bf16)
    round_v = pltpu.VMEM(field.shape, bf16)
    raw = struct(carbon_input_volume.shape, bf16)
    raw_v = pltpu.VMEM(raw.shape, bf16)
    taps_v = pltpu.VMEM(conv_fine.shape, bf16)
    x_scratch = pltpu.VMEM((2 * gy * cells, wide), f32)
    wide_scratch = pltpu.VMEM((devices * 2 * cells, wide), f32)
    left_scratch = pltpu.VMEM((cells * CH, local * devices * 2), bf16)
    mode_field = struct((2 * modes, wide))
    mode_v = pltpu.VMEM(mode_field.shape, f32)
    rows = modes * CH
    packed = struct((rows, 2 * wide), bf16)
    bands_v = pltpu.VMEM((2, 12 * CH, 24 * CH), bf16)
    side = struct((rows_y, 3, CH, span), bf16)
    message = struct((6, CH, span), bf16)
    y_side = struct((3, 10 * CH, span), bf16)
    y_message = struct((12, CH, span), bf16)

    with jax.named_scope("arrive"):
        u, one, two, my_x = run(
            arrive_kernel,
            [(IN_HBM, carbon_input_volume), (IN_HBM, forward_x)],
            [
                (IN_VMEM, round_field),
                (IN_VMEM, side),
                (IN_VMEM, side),
                (IN_VMEM, struct(forward_x.shape, bf16)),
            ],
            limit,
            [raw_v],
            copies=2,
        )
    one, two = swaps((one, two), "gz")

    def spread(values, table, exact, *others):
        with jax.named_scope("spread"):
            return run(
                lambda *refs: spread_kernel(exact, local, gy, gz, *refs),
                [(IN_VMEM, array) for array in (values, table) + others],
                [(IN_HBM, chunk)] + [(IN_HBM, struct(x.shape, x.dtype)) for x in others],
                limit,
                [x_scratch, sent],
                copies=2 + len(others),
                micros=1.2,
            )

    received = exchange(spread(u, my_x, True)[0])

    with jax.named_scope("y_message"):
        own_one, own_two = run(
            y_message_kernel,
            [(IN_VMEM, u), (IN_VMEM, one), (IN_VMEM, two)],
            [(IN_HBM, y_side), (IN_HBM, y_side)],
            limit,
            [pltpu.VMEM((rows_y, 10 * CH, span), bf16)],
            copies=2,
        )
    one, two = swaps((own_one, own_two), "gy")

    with jax.named_scope("setup"):
        w_high, w_low, my_there, my_back = run(
            lambda *refs: setup_kernel(local, *refs),
            [
                (IN_HBM, spec_weight.reshape(2, local, rows, CH)),
                (IN_HBM, there),
                (IN_HBM, back),
            ],
            [
                (IN_VMEM, packed),
                (IN_VMEM, packed),
                (IN_VMEM, struct(there.shape[1:], bf16)),
                (IN_VMEM, struct(back.shape[1:], bf16)),
            ],
            limit + (10 << 20),
            [pltpu.VMEM((2, local, rows, CH), f32)],
            copies=10,
            micros=4.5,
        )

    with jax.named_scope("mix"):
        v, w_kept, send = run(
            lambda *refs: mix_kernel(local, *refs),
            [
                (IN_VMEM, received),
                (IN_VMEM, my_there),
                (IN_VMEM, w_high),
                (IN_VMEM, w_low),
                (IN_VMEM, my_back),
            ],
            [(IN_HBM, mode_field), (IN_HBM, packed), (IN_HBM, chunk)],
            limit,
            [mode_v, sent],
            copies=6,
            micros=3,
        )
    received = exchange(send)

    with jax.named_scope("forward_convs"):
        base, fine, coarse, cot, my_inverse, my_x = run(
            forward_conv_kernel,
            [
                (IN_HBM, own_one),
                (IN_HBM, own_two),
                (IN_HBM, one),
                (IN_HBM, two),
                (IN_VMEM, lin_weight),
                (IN_HBM, conv_fine),
                (IN_HBM, conv_coarse),
                (IN_VMEM, bias_fine[None]),
                (IN_VMEM, bias_coarse[None]),
                (IN_HBM, cotangent),
                (IN_HBM, inverse_table),
                (IN_HBM, forward_x),
            ],
            [
                (IN_VMEM, field),
                (IN_HBM, struct((8, 8 * CH, span), bf16)),
                (IN_VMEM, struct((2, 2, CH, span // 2), bf16)),
                (IN_VMEM, round_field),
                (IN_VMEM, struct(inverse_table.shape, bf16)),
                (IN_VMEM, struct(forward_x.shape, bf16)),
            ],
            limit,
            [
                pltpu.VMEM((10, 12 * CH, span), bf16),
                taps_v,
                taps_v,
                raw_v,
                bands_v,
                pltpu.VMEM((4, 8 * CH, span // 2), bf16),
                pltpu.VMEM((8, 8 * CH, span), bf16),
            ],
            copies=10,
            micros=7,
        )

    with jax.named_scope("middle"):
        activated, grad, grad_round, one, two = run(
            lambda *refs: middle_kernel(local, *refs),
            [
                (IN_VMEM, received),
                (IN_VMEM, my_inverse),
                (IN_VMEM, base),
                (IN_VMEM, cot),
                (IN_VMEM, coarse),
            ],
            [
                (IN_VMEM, round_field),
                (IN_VMEM, field),
                (IN_VMEM, struct((cells + 2, CH, span), bf16)),
                (IN_VMEM, message),
                (IN_VMEM, message),
            ],
            limit,
            [wide_scratch, left_scratch],
            micros=2,
        )
    one, two = swaps((one, two), "gz")
    send, grad, activated, grad_round = spread(grad, my_x, False, grad, activated, grad_round)
    received = exchange(send)

    with jax.named_scope("y_gradient"):
        kept_z, one, two = run(
            y_gradient_kernel,
            [(IN_HBM, grad_round), (IN_VMEM, one), (IN_VMEM, two)],
            [
                (IN_HBM, struct((2,) + message.shape, bf16)),
                (IN_VMEM, y_message),
                (IN_VMEM, y_message),
            ],
            limit,
            [
                pltpu.VMEM((cells + 2, CH, span), bf16),
                pltpu.VMEM((2,) + message.shape, bf16),
            ],
            copies=2,
            micros=20,
        )
    one, two = swaps((one, two), "gy")
    with jax.named_scope("turn"):
        predicted, my_there, my_w, my_back, rep = run(
            turn_kernel,
            [
                (IN_HBM, activated),
                (IN_HBM, there),
                (IN_HBM, w_kept),
                (IN_HBM, back),
            ],
            [
                (IN_HBM, raw),
                (IN_VMEM, struct(there.shape[1:], bf16)),
                (IN_VMEM, packed),
                (IN_VMEM, struct(back.shape[1:], bf16)),
                (IN_VMEM, struct((wide, local * MZ * CH), bf16)),
            ],
            limit,
            [round_v, raw_v],
            copies=5,
            micros=2,
        )

    with jax.named_scope("mix_adjoint"):
        d, send = run(
            lambda *refs: adjoint_kernel(local, *refs),
            [(IN_VMEM, array) for array in (received, my_there, my_w, my_back, rep)],
            [(IN_VMEM, mode_field), (IN_HBM, chunk)],
            limit,
            [sent],
            copies=4,
            micros=2,
        )
    received = exchange(send)

    with jax.named_scope("backward"):
        weight_grad, base, my_inverse = run(
            backward_kernel,
            [
                (IN_VMEM, d),
                (IN_VMEM, v),
                (IN_HBM, grad),
                (IN_HBM, grad_round),
                (IN_HBM, kept_z),
                (IN_HBM, one),
                (IN_HBM, two),
                (IN_HBM, fine),
                (IN_VMEM, lin_weight),
                (IN_HBM, conv_fine),
                (IN_HBM, conv_coarse),
                (IN_HBM, inverse_table),
            ],
            [
                (IN_HBM, struct((2, local, rows, CH))),
                (IN_VMEM, field),
                (IN_VMEM, struct(inverse_table.shape, bf16)),
            ],
            limit + (10 << 20),
            [
                pltpu.VMEM((2, local, rows, CH), f32),
                field_v,
                pltpu.VMEM((cells + 2, CH, span), bf16),
                pltpu.VMEM((2,) + message.shape, bf16),
                pltpu.VMEM((2,) + y_message.shape, bf16),
                pltpu.VMEM((8, 8 * CH, span), bf16),
                taps_v,
                taps_v,
                bands_v,
                pltpu.VMEM((6, 8 * CH, span // 2), bf16),
                pltpu.VMEM((6, 8 * CH, span), bf16),
            ],
            copies=9 + local,
            micros=6,
        )
    weight_grad = weight_grad.reshape(spec_weight.shape)

    with jax.named_scope("last"):
        (sensitivity,) = run(
            lambda *refs: last_kernel(local, *refs),
            [(IN_VMEM, received), (IN_VMEM, my_inverse), (IN_VMEM, base)],
            [(IN_HBM, raw)],
            limit,
            [raw_v, wide_scratch, left_scratch],
            copies=2,
            micros=2,
        )
    return (predicted, sensitivity, weight_grad)


def solution(mesh):
    field = P(None, "gy", "gz", None)
    modes = P(None, "gy", "gz", None, None, None)
    return jax.shard_map(
        shards,
        mesh=mesh,
        in_specs=(field, field, modes, P(), P(), P(), P(), P()),
        out_specs=(field, field, modes),
        check_vma=False,
    )
```

```python
import math

import jax
import jax.numpy as jnp
import ml_dtypes
import numpy as np
from jax import lax
from jax.experimental import pallas as pl
from jax.experimental.pallas import tpu as pltpu
from jax.sharding import PartitionSpec as P

MX = 32
MY = 32
MZ = 8
CH = 32
BOTH = ("gy", "gz")

f32 = jnp.float32
bf16 = jnp.bfloat16
root_coef = math.sqrt(2.0 / math.pi)
NN = (((1,), (0,)), ((), ()))
NT = (((1,), (1,)), ((), ()))
TN = (((0,), (0,)), ((), ()))


def dot(a, b, form=NN):
    return lax.dot_general(a, b, form, preferred_element_type=f32)


def halves(value):
    high = value.astype(bf16)
    return high, (value - high.astype(f32)).astype(bf16)


def iota(shape, dim):
    return lax.broadcasted_iota(jnp.int32, shape, dim)


IN_VMEM = pl.BlockSpec(memory_space=pltpu.VMEM)
IN_HBM = pl.BlockSpec(memory_space=pltpu.HBM)


def struct(shape, kind=f32):
    return jax.ShapeDtypeStruct(shape, kind)


def run(kernel, ins, outs, limit, scratch=(), micros=1.0, copies=0, **grid):
    scratch = list(scratch)
    if copies:
        scratch.append(pltpu.SemaphoreType.DMA((copies,)))
    held = {id(IN_HBM): pltpu.HBM, id(IN_VMEM): pltpu.VMEM}

    def placed(spec, array):
        if id(spec) in held:
            return pltpu.with_memory_space_constraint(array, held[id(spec)])
        return array

    def shaped(spec, shape):
        if id(spec) in held:
            return held[id(spec)](shape.shape, shape.dtype)
        return shape

    return pl.pallas_call(
        kernel,
        in_specs=[spec for spec, _ in ins],
        out_specs=[spec for spec, _ in outs],
        out_shape=[shaped(spec, shape) for spec, shape in outs],
        scratch_shapes=scratch,
        compiler_params=pltpu.CompilerParams(vmem_limit_bytes=limit),
        cost_estimate=pl.CostEstimate(
            flops=int(micros * 1.1e9), bytes_accessed=1 << 16, transcendentals=0
        ),
        **grid,
    )(*[placed(spec, array) for spec, array in ins])


def begin(sem, first, *pairs):
    copies = [
        pltpu.make_async_copy(source, target, sem.at[first + i])
        for i, (source, target) in enumerate(pairs)
    ]
    for copy in copies:
        copy.start()
    return copies


def finish(*copies):
    for copy in copies:
        copy.wait()


def kept(count, length):
    position = np.arange(count)
    return np.where(position < count // 2, position, length - count + position)


def split_np(table):
    high = table.astype(ml_dtypes.bfloat16)
    return high, (table - high.astype(np.float64)).astype(ml_dtypes.bfloat16)


def x_tables(cells_x, blocks):
    local = MX // blocks
    freqs = kept(MX, cells_x).reshape(blocks, local).T
    angles = 2.0 * np.pi * ((freqs[:, :, None] * np.arange(cells_x)) % cells_x) / cells_x
    table = np.stack([np.cos(angles), -np.sin(angles)], axis=2).reshape(2 * MX, cells_x)
    return np.concatenate(split_np(table), axis=0)


def x_back_table(cells_x, gy, gz):
    local = MX // gy
    freqs = kept(MX, cells_x).reshape(gy, local).T
    angles = 2.0 * np.pi * ((freqs[:, :, None] * np.arange(cells_x)) % cells_x) / cells_x
    table = np.stack([np.cos(angles), -np.sin(angles)], axis=2)
    table = np.broadcast_to(table[:, :, None], (local, gy, gz, 2, cells_x))
    return np.concatenate(split_np(table.reshape(-1, cells_x)), axis=0)


def yz_angles(xp, freqs_y, gy, gz, rows_y, rows_z):
    span_y, span_z = gy * rows_y, gz * rows_z
    phase_y = (freqs_y[:, None] * xp.arange(span_y)[None]) % span_y
    phase_z = (xp.arange(MZ)[:, None] * xp.arange(span_z)[None]) % span_z
    phase_y = phase_y.reshape(-1, 1, gy, 1, rows_y, 1)
    phase_z = phase_z.reshape(1, MZ, 1, gz, 1, rows_z)
    turn = (phase_y * span_z + phase_z * span_y) % (span_y * span_z)
    return turn.reshape(turn.shape[0] * MZ, gy * gz, rows_y * rows_z)


def yz_table(xp, freqs_y, gy, gz, rows_y, rows_z):
    cells = gy * gz * rows_y * rows_z
    turn = yz_angles(xp, freqs_y, gy, gz, rows_y, rows_z)
    angles = 2.0 * math.pi / cells * turn
    cosine, sine = xp.cos(angles), xp.sin(angles)
    table = xp.stack([xp.stack([cosine, sine], 2), xp.stack([-sine, cosine], 2)], 0)
    return table.reshape(2 * turn.shape[0], -1)


def mode_tables(gy, gz, rows_y, rows_z, scale):
    local = MY // gz
    cells = gy * gz * rows_y * rows_z
    freqs = kept(MY, gy * rows_y).reshape(gz, local)
    if gz * 2 * local * MZ * 2 * cells <= 1 << 20:
        there, back = [], []
        for block in range(gz):
            high, low = split_np(scale * yz_table(np, freqs[block], gy, gz, rows_y, rows_z))
            there.append(np.concatenate([high, low], 0))
            back.append(np.concatenate([high.T, low.T], 1))
        return jnp.asarray(np.stack(there)), jnp.asarray(np.stack(back))
    where = lax.axis_index("gz")
    mine = lax.dynamic_index_in_dim(jnp.asarray(freqs, jnp.int32), where, keepdims=False)
    high, low = halves(scale * yz_table(jnp, mine, gy, gz, rows_y, rows_z).astype(f32))
    return jnp.concatenate([high, low], 0)[None], jnp.concatenate([high.T, low.T], 1)[None]


def put_x_modes(product, local, blocks, copies, cells, scratch, sent, send_ref, sem, first):
    rows = 2 * blocks
    half = blocks // 2
    moves = []
    for start in (0, half):
        at = 2 * start * cells
        for cell in range(cells):
            piece = product[:, cell * CH : (cell + 1) * CH]
            parts = [piece[k * rows + 2 * start : k * rows + 2 * start + blocks] for k in range(local)]
            scratch[pl.ds(at + cell, blocks, stride=cells), :] = jnp.concatenate(parts, axis=1)
        for block in range(start, start + half):
            value = scratch[block * 2 * cells : (block + 1) * 2 * cells].astype(bf16)
            for copy in range(copies):
                sent[block * copies + copy] = value
        part = pl.ds(start * copies, half * copies)
        moves += begin(sem, first + len(moves), (sent.at[part], send_ref.at[part]))
    return moves


def odd(axis):
    return lax.axis_index(axis) & 1


def first(axis):
    return lax.axis_index(axis) == 0


def last(axis):
    return lax.axis_index(axis) == lax.axis_size(axis) - 1


def arrive_kernel(raw_ref, table_ref, u_ref, one_ref, two_ref, my_table_ref, raw, sem):
    loads = begin(sem, 0, (raw_ref, raw), (table_ref, my_table_ref))
    finish(*loads)
    u = jnp.transpose(raw[...], (1, 2, 0, 3))
    u_ref[...] = u
    side = odd("gz")
    one_ref[...] = u_ref[:, pl.ds(1 - side, 3)]
    two_ref[...] = u_ref[:, pl.ds(side, 3)]


def spread_kernel(
    exact, local, blocks, copies, u_ref, table, *refs
):
    *refs, scratch, sent, sem = refs
    count = len(refs) // 2
    stores = begin(sem, 2, *zip(refs[:count], refs[count + 1 :]))
    send_ref = refs[count]
    cells = u_ref.shape[0] * u_ref.shape[1]
    u = u_ref[...].reshape(cells * CH, -1)
    if exact:
        both = dot(table[...], u, NT)
        product = both[: 2 * MX] + both[2 * MX :]
    else:
        high, low = halves(u)
        both = dot(table[...], high, NT)
        product = both[: 2 * MX] + both[2 * MX :] + dot(table[: 2 * MX], low, NT)
    moves = put_x_modes(product, local, blocks, copies, cells, scratch, sent, send_ref, sem, 0)
    finish(*moves, *stores)


def pick(tables_ref):
    if tables_ref.shape[0] == 1:
        return tables_ref.at[0]
    return tables_ref.at[lax.axis_index("gz")]


def mode_values(rec_ref, there, rows):
    both = dot(there[...], rec_ref[...].reshape(-1, rec_ref.shape[2]))
    return both[:rows] + both[rows:]


def put_back(values, back_ref, sent, send_ref, sem, first):
    high, low = halves(values)
    twice = jnp.concatenate([high, high], 0)
    rows = values.shape[0]
    devices, depth, wide = sent.shape
    part = devices // 4
    moves = []
    for step in range(4):
        at = slice(step * part * depth, (step + 1) * part * depth)
        result = dot(back_ref[at], twice) + dot(back_ref[at, :rows], low)
        sent[step * part : (step + 1) * part] = result.astype(bf16).reshape(part, depth, wide)
        span = pl.ds(step * part, part)
        moves += begin(sem, first + step, (sent.at[span], send_ref.at[span]))
    finish(*moves)


def kz_weight(shape):
    return jnp.where(iota(shape, 0) % MZ == 0, 1.0, 2.0).astype(f32)


def same_mode(rows, lanes):
    return (iota((rows, lanes), 0) % MZ) == ((iota((rows, lanes), 1) // CH) % MZ)


def mix_kernel(
    local,
    rec_ref,
    there_ref,
    high_ref,
    low_ref,
    back_ref,
    v_ref,
    kept_w_ref,
    send_ref,
    kept_v,
    sent,
    sem,
):
    store_w = begin(sem, 5, (high_ref, kept_w_ref))
    rows = there_ref.shape[0] // 2
    modes = rows // 2
    wide = local * CH
    v = mode_values(rec_ref, there_ref, rows)
    kept_v[...] = v
    store = begin(sem, 0, (kept_v, v_ref))
    real, imag = v[:modes], v[modes:]
    pair = (
        jnp.concatenate([real, -imag], 1),
        jnp.concatenate([imag, real], 1),
    )
    lane_k = (iota((MZ, 2 * wide), 1) // CH) % local
    size = MZ * CH
    diag = same_mode(2 * MZ * local, size)
    placed = [[[None] * (modes // MZ) for _ in range(local)] for _ in range(2)]
    for g in range(modes // MZ):
        pieces = []
        for k in range(local):
            for part in range(2):
                piece = pair[part][g * MZ : (g + 1) * MZ]
                pieces.append(jnp.where(lane_k == k, piece, 0.0))
        left_high, left_low = halves(jnp.concatenate(pieces, 0))
        w_high = high_ref[g]
        w_low = low_ref[g]
        count = left_high.shape[0]
        both = dot(jnp.concatenate([left_high, left_low], 0), w_high)
        value = both[:count] + both[count:] + dot(left_high, w_low)
        value = jnp.where(diag, value, 0.0)
        for k in range(local):
            for part in range(2):
                at = (2 * k + part) * MZ
                placed[part][k][g] = value[at : at + MZ]
    columns = [jnp.concatenate(placed[0][k] + placed[1][k], 0) for k in range(local)]
    all_values = jnp.concatenate(columns, 1)
    shape = (local * size, wide)
    fold = (iota(shape, 0) // size == iota(shape, 1) // CH) & (
        iota(shape, 0) % CH == iota(shape, 1) % CH
    )
    fold = fold.astype(bf16)
    high, low = halves(all_values)
    mixed = dot(high, fold) + dot(low, fold)
    put_back(mixed * kz_weight(mixed.shape), back_ref, sent, send_ref, sem, 1)
    finish(*store, *store_w)


def adjoint_kernel(
    local,
    rec_ref,
    there_ref,
    high_ref,
    back_ref,
    rep_ref,
    d_ref,
    send_ref,
    sent,
    sem,
):
    rows = there_ref.shape[0] // 2
    modes = rows // 2
    wide = local * CH
    size = MZ * CH
    d = mode_values(rec_ref, there_ref, rows)
    d = d * kz_weight(d.shape)
    d_ref[...] = d
    high, low = halves(d)
    spread = dot(high, rep_ref[...]) + dot(low, rep_ref[...])
    spread = jnp.where(same_mode(rows, local * size), spread, 0.0)
    lane_k = (iota((2 * MZ, 2 * wide), 1) // CH) % local
    parts = ([], [])
    for g in range(modes // MZ):
        pieces = []
        for k in range(local):
            for part in range(2):
                at = part * modes + g * MZ
                pieces.append(spread[at : at + MZ, k * size : (k + 1) * size])
        left_high, left_low = halves(jnp.concatenate(pieces, 0))
        count = left_high.shape[0]
        both = dot(
            jnp.concatenate([left_high, left_low], 0), high_ref[g * size : (g + 1) * size]
        )
        value = both[:count] + both[count:]
        total = None
        for k in range(local):
            piece = jnp.where(lane_k == k, value[2 * k * MZ : 2 * (k + 1) * MZ], 0.0)
            total = piece if total is None else total + piece
        parts[0].append(total[:MZ])
        parts[1].append(total[MZ:])
    real = jnp.concatenate(parts[0], 0)
    imag = jnp.concatenate(parts[1], 0)
    value = jnp.concatenate(
        [real[:, :wide] + imag[:, wide:], imag[:, :wide] - real[:, wide:]], 0
    )
    put_back(value, back_ref, sent, send_ref, sem, 0)


def setup_kernel(
    local,
    w_ref,
    there_ref,
    back_ref,
    high_ref,
    low_ref,
    my_there_ref,
    my_back_ref,
    w,
    sem,
):
    parts = high_ref.shape[0]
    rows = w.shape[2] // parts
    spans = [pl.ds(step * rows, rows) for step in range(parts)]
    loads = begin(sem, 0, *[(w_ref.at[:, :, span], w.at[:, :, span]) for span in spans])
    tables = begin(
        sem, parts, (pick(there_ref), my_there_ref), (pick(back_ref), my_back_ref)
    )
    for step in range(parts):
        at = slice(step * rows, (step + 1) * rows)
        finish(loads[step])
        pieces = [w[part, k, at] for part in range(2) for k in range(local)]
        high_ref[step], low_ref[step] = halves(jnp.concatenate(pieces, 1).T)
    finish(*tables)


def put_weight_grad(d_ref, v_ref, out, out_ref, sem, first):
    rows, wide = d_ref.shape
    modes = rows // 2
    size = MZ * CH
    keep = same_mode(rows, size)
    d_halves = halves(d_ref[...])
    v_halves = halves(v_ref[...])
    stores = []
    for k in range(wide // CH):
        shape = (wide, size)
        rep = (iota(shape, 0) == k * CH + iota(shape, 1) % CH).astype(bf16)
        d_high, d_low = [jnp.where(keep, dot(value, rep), 0.0) for value in d_halves]
        at = slice(k * CH, (k + 1) * CH)
        v_high, v_low = [value[:, at].astype(f32) for value in v_halves]
        for g in range(modes // MZ):
            real = slice(g * MZ, (g + 1) * MZ)
            imag = slice(modes + g * MZ, modes + (g + 1) * MZ)
            left = jnp.concatenate(
                [d_high[real], d_high[imag], d_low[real], d_low[imag], d_high[real], d_high[imag]],
                0,
            ).astype(bf16)
            for part in range(2):
                rights = []
                for v in (v_high, v_high, v_low):
                    rights += [v[real], v[imag]] if part == 0 else [-v[imag], v[real]]
                right = jnp.concatenate(rights, 0).astype(bf16)
                out[part, k, g * size : (g + 1) * size, :] = dot(left, right, TN)
        stores += begin(sem, first + k, (out.at[:, k], out_ref.at[:, k]))
    return stores


def widen(rec_ref, wide):
    wide[...] = rec_ref[...].reshape(-1, rec_ref.shape[2]).astype(f32)


def inverse_x(wide, table, local, cells, part, left):
    rows = wide.shape[0] // cells
    for cell in part:
        turned = wide[pl.ds(cell, rows, stride=cells), :].T.astype(bf16)
        for k in range(local):
            left[cell * CH : (cell + 1) * CH, k * rows : (k + 1) * rows] = turned[
                k * CH : (k + 1) * CH
            ]
    depth = local * rows
    value = left[part.start * CH : part.stop * CH]
    return dot(value, table[:depth]) + dot(value, table[depth:])


def gelu_pair(pre_act):
    cube_term = pre_act * pre_act * pre_act
    tanh_result = jnp.tanh(root_coef * (pre_act + 0.044715 * cube_term))
    activated_output = 0.5 * pre_act * (1.0 + tanh_result)
    gelu_slope = 0.5 * (1.0 + tanh_result) + 0.5 * pre_act * (
        1.0 - tanh_result * tanh_result
    ) * root_coef * (1.0 + 3.0 * 0.044715 * pre_act * pre_act)
    return (activated_output, gelu_slope)


def middle_kernel(
    local,
    rec_ref,
    back_ref,
    base_ref,
    cot_ref,
    coarse_ref,
    out_ref,
    grad_ref,
    rounded,
    one_ref,
    two_ref,
    wide,
    left,
):
    rows_y, rows_z, _, span = base_ref.shape
    cells = rows_y * rows_z
    widen(rec_ref, wide)
    pre_act = inverse_x(wide, back_ref, local, cells, range(cells), left)
    pre_act = pre_act + base_ref[...].reshape(pre_act.shape)
    activated, slope = gelu_pair(pre_act)
    out_ref[...] = activated.astype(bf16).reshape(out_ref.shape)
    value = cot_ref[...].astype(f32).reshape(pre_act.shape) * slope
    grad_ref[...] = value.reshape(grad_ref.shape)
    rounded[:cells] = value.astype(bf16).reshape(cells, CH, span)
    side = odd("gz")
    for y in range(rows_y):
        one_ref[y] = rounded[rows_z * y + (rows_z - 1) * (1 - side)]
        two_ref[y] = rounded[rows_z * y + (rows_z - 1) * side]
    pool = pool_matrix(span)
    for yc in range(2):
        sums = []
        for zc in range(2):
            y, z = 2 * yc, 2 * zc
            sums.append(
                grad_ref[y, z] + grad_ref[y, z + 1] + grad_ref[y + 1, z] + grad_ref[y + 1, z + 1]
            )
        total_high, total_low = halves(jnp.concatenate(sums, 0))
        total = dot(total_high, pool) + dot(total_low, pool)
        pieces = []
        for zc in range(2):
            piece = total[zc * CH : (zc + 1) * CH]
            pieces.append(jnp.where(coarse_ref[yc, zc].astype(f32) > 0, piece, 0.0))
        piece = jnp.concatenate(pieces, 1).astype(bf16)
        rounded[cells + yc] = piece
        one_ref[rows_y + yc] = piece
        two_ref[rows_y + yc] = piece


def last_kernel(local, rec_ref, back_ref, base_ref, out_ref, out, wide, left, sem):
    rows_y, rows_z, _, span = base_ref.shape
    cells = rows_y * rows_z
    widen(rec_ref, wide)
    moves = []
    for y in range(0, rows_y, 2):
        part = range(y * rows_z, (y + 2) * rows_z)
        value = inverse_x(wide, back_ref, local, cells, part, left)
        value = value.reshape(2, rows_z, CH, span) + base_ref[y : y + 2]
        out[:, y : y + 2] = jnp.transpose(value.astype(bf16), (2, 0, 1, 3))
        at = pl.ds(y, 2)
        moves += begin(sem, y // 2, (out.at[:, at], out_ref.at[:, at]))
    finish(*moves)


def turn_kernel(
    value_ref,
    there_ref,
    w_ref,
    back_ref,
    out_ref,
    my_there_ref,
    my_w_ref,
    my_back_ref,
    rep_ref,
    value,
    out,
    packed,
    sem,
):
    loads = begin(
        sem,
        0,
        (value_ref, value),
        (pick(there_ref), my_there_ref),
        (w_ref, packed),
        (pick(back_ref), my_back_ref),
    )
    shape = rep_ref.shape
    size = MZ * CH
    rep = (iota(shape, 1) // size == iota(shape, 0) // CH) & (
        iota(shape, 1) % CH == iota(shape, 0) % CH
    )
    rep_ref[...] = rep.astype(bf16)
    finish(loads[0])
    out[...] = jnp.transpose(value[...], (2, 0, 1, 3))
    store = begin(sem, 4, (out, out_ref))
    finish(*loads[1:])
    for g in range(packed.shape[0]):
        my_w_ref[g * size : (g + 1) * size] = packed[g].astype(f32).T.astype(bf16)
    finish(*store)


def write_bands(adjoint, k_ref, out, index):
    for a in range(3):
        for e in range(3):
            taps = []
            for b in range(3):
                if adjoint:
                    tap = k_ref[9 * (2 - a) + 3 * (2 - b) + 2 - e].astype(f32).T
                else:
                    tap = k_ref[9 * a + 3 * b + e].astype(f32)
                taps.append(tap)
            taps = jnp.concatenate(taps, 1)
            for z in range(4):
                pieces = [taps, jnp.zeros((CH, (5 - z) * CH), f32)]
                if z > 0:
                    pieces.insert(0, jnp.zeros((CH, z * CH), f32))
                row = jnp.concatenate(pieces, 1)
                at = (e * 4 + z) * CH
                out[index, at : at + CH, a * 8 * CH : (a + 1) * 8 * CH] = row.astype(bf16)


def x_sum(low, same, high):
    span = same.shape[1]
    lane = iota(same.shape, 1)
    before = jnp.where(lane == 0, 0.0, pltpu.roll(low, 1, axis=1))
    after = jnp.where(lane == span - 1, 0.0, pltpu.roll(high, span - 1, axis=1))
    return same + before + after


def band_conv(bands, planes):
    value = dot(bands, jnp.concatenate(planes, 0))
    size = 4 * CH
    return x_sum(value[:size], value[size : 2 * size], value[2 * size :])


def column(row_ref, copies):
    eye = iota((CH, CH), 0) == iota((CH, CH), 1)
    value = jnp.sum(jnp.where(eye, row_ref[...], 0.0), axis=1, keepdims=True)
    return jnp.concatenate([value] * copies, 0)


def block_diagonal(matrix):
    shape = (4 * CH, 4 * CH)
    wide = jnp.concatenate([matrix.astype(f32)] * 4, 1)
    tiled = jnp.concatenate([wide] * 4, 0)
    return jnp.where(iota(shape, 0) // CH == iota(shape, 1) // CH, tiled, 0.0).astype(bf16)


def pool_matrix(span):
    shape = (span, span // 2)
    return (iota(shape, 0) // 2 == iota(shape, 1)).astype(bf16)


def up_matrix(span):
    shape = (span // 2, span)
    return (iota(shape, 1) // 2 == iota(shape, 0)).astype(bf16)


def y_message_kernel(u_ref, z_one_ref, z_two_ref, one_ref, two_ref, rows, sem):
    side = odd("gz")
    for y in range(4):
        for z in range(3):
            at = pl.multiple_of((7 * (1 - side) + z) * CH, CH)
            rows[y, pl.ds(at, CH)] = z_one_ref[y, z]
            at = pl.multiple_of((7 * side + z) * CH, CH)
            rows[y, pl.ds(at, CH)] = z_two_ref[y, z]
        for z in range(4):
            rows[y, (z + 3) * CH : (z + 4) * CH] = u_ref[y, z]
    blank = jnp.zeros((4, 3 * CH, rows.shape[2]), bf16)

    @pl.when(first("gz"))
    def low_end():
        rows[:, : 3 * CH] = blank

    @pl.when(last("gz"))
    def high_end():
        rows[:, 7 * CH :] = blank

    side = odd("gy")
    finish(
        *begin(
            sem, 0, (rows.at[pl.ds(1 - side, 3)], one_ref), (rows.at[pl.ds(side, 3)], two_ref)
        )
    )


def forward_conv_kernel(
    own_one_ref,
    own_two_ref,
    y_one_ref,
    y_two_ref,
    lin_ref,
    taps_fine_ref,
    taps_coarse_ref,
    bias_fine_ref,
    bias_coarse_ref,
    cot_ref,
    table_ref,
    x_ref,
    base,
    fine_ref,
    coarse,
    my_cot_ref,
    my_table_ref,
    my_x_ref,
    grid,
    taps_fine,
    taps_coarse,
    raw,
    bands,
    pooled,
    fine,
    sem,
):
    span = grid.shape[2]
    inner = pl.ds(0, 10 * CH)
    side = odd("gy")
    loads = begin(
        sem,
        0,
        (taps_fine_ref, taps_fine),
        (own_one_ref, grid.at[pl.ds(4 - side, 3), inner]),
        (own_two_ref.at[pl.ds(2 * side, 1)], grid.at[pl.ds(3 + 3 * side, 1), inner]),
        (y_one_ref, grid.at[pl.ds(7 * (1 - side), 3), inner]),
        (y_two_ref, grid.at[pl.ds(7 * side, 3), inner]),
        (taps_coarse_ref, taps_coarse),
        (cot_ref, raw),
        (table_ref, my_table_ref),
        (x_ref, my_x_ref),
    )
    edges = [jnp.logical_not(end(axis)) for axis in ("gy", "gz") for end in (first, last)]
    grid[:, 10 * CH :, :] = jnp.zeros((10, 2 * CH, span), bf16)
    pooled[:, 4 * CH :, :] = jnp.zeros((4, 4 * CH, span // 2), bf16)
    bias = column(bias_fine_ref, 4)
    half = 4 * CH
    row_z = iota((half, span), 0) // CH
    finish(loads[0])
    write_bands(False, taps_fine, bands, 0)
    finish(*loads[1:3])
    for y in (3, 4, 2, 1, 0, 5, 6, 7):
        if y == 2:
            finish(loads[3], loads[4])

            @pl.when(first("gy"))
            def low_end():
                grid[:3] = jnp.zeros((3, 12 * CH, span), bf16)

            @pl.when(last("gy"))
            def high_end():
                grid[7:] = jnp.zeros((3, 12 * CH, span), bf16)

        y_in = None
        if y < 2:
            y_in = edges[0]
        elif y >= 6:
            y_in = edges[1]
        for h in range(2):
            at = h * half
            value = band_conv(bands[0], [grid[y + a, at : at + 8 * CH, :] for a in range(3)])
            value = jnp.maximum(value + bias, 0.0)
            inside = (row_z >= 2) | edges[2] if h == 0 else (row_z < 2) | edges[3]
            if y_in is not None:
                inside = inside & y_in
            fine[y, at : at + half, :] = jnp.where(inside, value, 0.0).astype(bf16)
    (store,) = begin(sem, 9, (fine, fine_ref))
    sums = []
    for yc in range(4):
        both = fine[2 * yc].astype(f32) + fine[2 * yc + 1].astype(f32)
        for zc in range(4):
            at = 2 * zc * CH
            sums.append(both[at : at + CH] + both[at + CH : at + 2 * CH])
    pool = pool_matrix(span)
    high, low = halves(jnp.concatenate(sums, 0))
    pools = (0.125 * (dot(high, pool) + dot(low, pool))).astype(bf16)
    pooled[:, : 4 * CH, :] = pools.reshape(4, 4 * CH, span // 2)
    bias = column(bias_coarse_ref, 4)
    finish(loads[5])
    write_bands(False, taps_coarse, bands, 1)
    planes = [jnp.concatenate([pooled[a], pooled[a + 1]], 1) for a in range(3)]
    value = dot(bands[1], jnp.concatenate(planes, 0))
    parts = [value[e * half : (e + 1) * half] for e in range(3)]
    for yc in range(2):
        at = slice(yc * span // 2, (yc + 1) * span // 2)
        value = x_sum(*[part[:, at] for part in parts])
        value = jnp.maximum(value + bias, 0.0).astype(bf16)
        coarse[yc] = value[: 2 * CH].reshape(2, CH, span // 2)
    lifted = dot(coarse[...].reshape(half, span // 2), up_matrix(span))
    lin = block_diagonal(lin_ref[...])
    for y in range(4):
        total = dot(lin, grid[y + 3, 3 * CH : 7 * CH, :])
        total = total + fine[y + 2, 2 * CH : 6 * CH, :].astype(f32)
        for z in range(4):
            at = (y // 2 * 2 + z // 2) * CH
            base[y, z] = total[z * CH : (z + 1) * CH] + lifted[at : at + CH]
    finish(loads[6])
    my_cot_ref[...] = jnp.transpose(raw[...], (1, 2, 0, 3))
    finish(store, *loads[7:])


def y_gradient_kernel(
    round_ref, z_one_ref, z_two_ref, kept_ref, one_ref, two_ref, own, halo, sem
):
    (load,) = begin(sem, 0, (round_ref, own))
    side = odd("gz")
    halo[1 - side] = z_one_ref[...]
    halo[side] = z_two_ref[...]

    @pl.when(first("gz"))
    def low_end():
        halo[0] = jnp.zeros(halo.shape[1:], bf16)

    @pl.when(last("gz"))
    def high_end():
        halo[1] = jnp.zeros(halo.shape[1:], bf16)

    (store,) = begin(sem, 1, (halo, kept_ref))
    finish(load)
    side = odd("gy")
    for out_ref, y in ((one_ref, 3 * (1 - side)), (two_ref, 3 * side)):
        out_ref[0] = halo[0, y]
        out_ref[1:5] = own[pl.ds(4 * y, 4)]
        out_ref[5] = halo[1, y]
        for yc in range(2):
            out_ref[6 + 3 * yc] = halo[0, 4 + yc]
            out_ref[7 + 3 * yc] = own[16 + yc]
            out_ref[8 + 3 * yc] = halo[1, 4 + yc]
    finish(store)


def backward_kernel(
    d_ref,
    v_ref,
    grad_ref,
    round_ref,
    kept_ref,
    y_one_ref,
    y_two_ref,
    fine_ref,
    lin_ref,
    taps_fine_ref,
    taps_coarse_ref,
    table_ref,
    weight_ref,
    base,
    my_table_ref,
    weights,
    grad,
    rounded,
    kept,
    beside,
    fine,
    taps_fine,
    taps_coarse,
    bands,
    coarse_grid,
    fine_grid,
    sem,
):
    side = odd("gy")
    loads = begin(
        sem,
        0,
        (taps_coarse_ref, taps_coarse),
        (round_ref, rounded),
        (kept_ref, kept),
        (y_one_ref, beside.at[1 - side]),
        (y_two_ref, beside.at[side]),
        (grad_ref, grad),
        (fine_ref, fine),
        (taps_fine_ref, taps_fine),
        (table_ref, my_table_ref),
    )
    stores = put_weight_grad(d_ref, v_ref, weights, weight_ref, sem, 9)
    finish(loads[0], loads[7])
    write_bands(True, taps_coarse, bands, 1)
    write_bands(True, taps_fine, bands, 0)
    span = grad.shape[3]
    half = span // 2
    coarse_grid[:, 6 * CH :, :] = jnp.zeros((6, 2 * CH, half), bf16)
    fine_grid[:, 6 * CH :, :] = jnp.zeros((6, 2 * CH, span), bf16)

    def place(yc, pair, value):
        for zc in range(2):
            at = (2 * pair + zc) * CH
            coarse_grid[yc, at : at + CH, :] = value[:, zc * half : (zc + 1) * half]

    finish(*loads[1:5])

    @pl.when(first("gy"))
    def low_end():
        beside[0] = jnp.zeros(beside.shape[1:], bf16)

    @pl.when(last("gy"))
    def high_end():
        beside[1] = jnp.zeros(beside.shape[1:], bf16)

    for yc in range(2):
        place(2 + yc, 0, kept[0, 4 + yc])
        place(2 + yc, 1, rounded[16 + yc])
        place(2 + yc, 2, kept[1, 4 + yc])
        for pair in range(3):
            place(yc, pair, beside[0, 6 + 3 * yc + pair])
            place(4 + yc, pair, beside[1, 6 + 3 * yc + pair])
    pooled = [
        0.125 * band_conv(bands[1], [coarse_grid[yc + a] for a in range(3)]) for yc in range(4)
    ]
    high, low = halves(jnp.concatenate(pooled, 0))
    up = up_matrix(span)
    lifted = dot(high, up) + dot(low, up)
    finish(*loads[5:7])
    for y in range(6):
        yc = (y + 1) // 2
        for z in range(6):
            at = (4 * yc + (z + 1) // 2) * CH
            if 1 <= y <= 4 and 1 <= z <= 4:
                value = grad[y - 1, z - 1]
            elif 1 <= y <= 4:
                value = kept[z // 5, y - 1].astype(f32)
            else:
                value = beside[y // 5, z].astype(f32)
            value = value + lifted[at : at + CH]
            mask = fine[y + 1, (z + 1) * CH : (z + 2) * CH, :].astype(f32) > 0
            fine_grid[y, z * CH : (z + 1) * CH, :] = jnp.where(mask, value, 0.0).astype(bf16)
    lin = block_diagonal(lin_ref[...].astype(f32).T.astype(bf16))
    for y in range(4):
        value = band_conv(bands[0], [fine_grid[y + a] for a in range(3)])
        value = value + dot(lin, rounded[4 * y : 4 * y + 4].reshape(4 * CH, span))
        base[y] = value.reshape(4, CH, span)
    finish(loads[8], *stores)


def swaps(blocks, axis):
    size_y, size_z = lax.axis_size("gy"), lax.axis_size("gz")
    results = []
    for start, block in enumerate(blocks):
        pairs = []
        for y in range(size_y):
            for z in range(size_z):
                step = 1 if ((y if axis == "gy" else z) - start) % 2 == 0 else -1
                to_y, to_z = y, z
                if axis == "gy":
                    to_y = (y + step) % size_y
                elif 0 <= z + step < size_z:
                    to_z = z + step
                else:
                    to_y = y ^ 1
                pairs.append((y * size_z + z, to_y * size_z + to_z))
        results.append(lax.ppermute(block, BOTH, pairs))
    return results


def exchange(block):
    return lax.all_to_all(block, BOTH, split_axis=0, concat_axis=0, tiled=True)


def shards(
    carbon_input_volume,
    cotangent,
    spec_weight,
    lin_weight,
    conv_fine,
    bias_fine,
    conv_coarse,
    bias_coarse,
):
    channels, rows_y, rows_z, span = carbon_input_volume.shape
    gy, gz = lax.axis_size("gy"), lax.axis_size("gz")
    devices = gy * gz
    cells = rows_y * rows_z
    local = MX // gy
    modes = (MY // gz) * MZ
    wide = local * CH
    scale = 1.0 / math.sqrt(span * cells * devices)
    there, back = mode_tables(gy, gz, rows_y, rows_z, scale)
    forward_x = jnp.asarray(x_tables(span, gy))
    inverse_table = jnp.asarray(x_back_table(span, gy, gz))

    limit = (14 << 20) + devices * (64 << 10)
    chunk = struct((devices, 2 * cells, wide), bf16)
    sent = pltpu.VMEM(chunk.shape, bf16)
    field = struct((rows_y, rows_z, CH, span))
    field_v = pltpu.VMEM(field.shape, f32)
    round_field = struct(field.shape, bf16)
    round_v = pltpu.VMEM(field.shape, bf16)
    raw = struct(carbon_input_volume.shape, bf16)
    raw_v = pltpu.VMEM(raw.shape, bf16)
    taps_v = pltpu.VMEM(conv_fine.shape, bf16)
    x_scratch = pltpu.VMEM((2 * gy * cells, wide), f32)
    wide_scratch = pltpu.VMEM((devices * 2 * cells, wide), f32)
    left_scratch = pltpu.VMEM((cells * CH, local * devices * 2), bf16)
    mode_field = struct((2 * modes, wide))
    mode_v = pltpu.VMEM(mode_field.shape, f32)
    rows = modes * CH
    packed = struct((modes // MZ, 2 * wide, MZ * CH), bf16)
    unpacked = struct((rows, 2 * wide), bf16)
    bands_v = pltpu.VMEM((2, 12 * CH, 24 * CH), bf16)
    side = struct((rows_y, 3, CH, span), bf16)
    message = struct((6, CH, span), bf16)
    y_side = struct((3, 10 * CH, span), bf16)
    y_message = struct((12, CH, span), bf16)

    with jax.named_scope("arrive"):
        u, one, two, my_x = run(
            arrive_kernel,
            [(IN_HBM, carbon_input_volume), (IN_HBM, forward_x)],
            [
                (IN_VMEM, round_field),
                (IN_VMEM, side),
                (IN_VMEM, side),
                (IN_VMEM, struct(forward_x.shape, bf16)),
            ],
            limit,
            [raw_v],
            copies=2,
        )
    one, two = swaps((one, two), "gz")

    def spread(values, table, exact, *others):
        with jax.named_scope("spread"):
            return run(
                lambda *refs: spread_kernel(exact, local, gy, gz, *refs),
                [(IN_VMEM, array) for array in (values, table) + others],
                [(IN_HBM, chunk)] + [(IN_HBM, struct(x.shape, x.dtype)) for x in others],
                limit,
                [x_scratch, sent],
                copies=2 + len(others),
                micros=1.2,
            )

    received = exchange(spread(u, my_x, True)[0])

    with jax.named_scope("y_message"):
        own_one, own_two = run(
            y_message_kernel,
            [(IN_VMEM, u), (IN_VMEM, one), (IN_VMEM, two)],
            [(IN_HBM, y_side), (IN_HBM, y_side)],
            limit,
            [pltpu.VMEM((rows_y, 10 * CH, span), bf16)],
            copies=2,
        )
    one, two = swaps((own_one, own_two), "gy")

    with jax.named_scope("setup"):
        w_high, w_low, my_there, my_back = run(
            lambda *refs: setup_kernel(local, *refs),
            [
                (IN_HBM, spec_weight.reshape(2, local, rows, CH)),
                (IN_HBM, there),
                (IN_HBM, back),
            ],
            [
                (IN_VMEM, packed),
                (IN_VMEM, packed),
                (IN_VMEM, struct(there.shape[1:], bf16)),
                (IN_VMEM, struct(back.shape[1:], bf16)),
            ],
            limit + (10 << 20),
            [pltpu.VMEM((2, local, rows, CH), f32)],
            copies=10,
            micros=4.5,
        )

    with jax.named_scope("mix"):
        v, w_kept, send = run(
            lambda *refs: mix_kernel(local, *refs),
            [
                (IN_VMEM, received),
                (IN_VMEM, my_there),
                (IN_VMEM, w_high),
                (IN_VMEM, w_low),
                (IN_VMEM, my_back),
            ],
            [(IN_HBM, mode_field), (IN_HBM, packed), (IN_HBM, chunk)],
            limit,
            [mode_v, sent],
            copies=6,
            micros=3,
        )
    received = exchange(send)

    with jax.named_scope("forward_convs"):
        base, fine, coarse, cot, my_inverse, my_x = run(
            forward_conv_kernel,
            [
                (IN_HBM, own_one),
                (IN_HBM, own_two),
                (IN_HBM, one),
                (IN_HBM, two),
                (IN_VMEM, lin_weight),
                (IN_HBM, conv_fine),
                (IN_HBM, conv_coarse),
                (IN_VMEM, bias_fine[None]),
                (IN_VMEM, bias_coarse[None]),
                (IN_HBM, cotangent),
                (IN_HBM, inverse_table),
                (IN_HBM, forward_x),
            ],
            [
                (IN_VMEM, field),
                (IN_HBM, struct((8, 8 * CH, span), bf16)),
                (IN_VMEM, struct((2, 2, CH, span // 2), bf16)),
                (IN_VMEM, round_field),
                (IN_VMEM, struct(inverse_table.shape, bf16)),
                (IN_VMEM, struct(forward_x.shape, bf16)),
            ],
            limit,
            [
                pltpu.VMEM((10, 12 * CH, span), bf16),
                taps_v,
                taps_v,
                raw_v,
                bands_v,
                pltpu.VMEM((4, 8 * CH, span // 2), bf16),
                pltpu.VMEM((8, 8 * CH, span), bf16),
            ],
            copies=10,
            micros=7,
        )

    with jax.named_scope("middle"):
        activated, grad, grad_round, one, two = run(
            lambda *refs: middle_kernel(local, *refs),
            [
                (IN_VMEM, received),
                (IN_VMEM, my_inverse),
                (IN_VMEM, base),
                (IN_VMEM, cot),
                (IN_VMEM, coarse),
            ],
            [
                (IN_VMEM, round_field),
                (IN_VMEM, field),
                (IN_VMEM, struct((cells + 2, CH, span), bf16)),
                (IN_VMEM, message),
                (IN_VMEM, message),
            ],
            limit,
            [wide_scratch, left_scratch],
            micros=2,
        )
    one, two = swaps((one, two), "gz")
    send, grad, activated, grad_round = spread(grad, my_x, False, grad, activated, grad_round)
    received = exchange(send)

    with jax.named_scope("y_gradient"):
        kept_z, one, two = run(
            y_gradient_kernel,
            [(IN_HBM, grad_round), (IN_VMEM, one), (IN_VMEM, two)],
            [
                (IN_HBM, struct((2,) + message.shape, bf16)),
                (IN_VMEM, y_message),
                (IN_VMEM, y_message),
            ],
            limit,
            [
                pltpu.VMEM((cells + 2, CH, span), bf16),
                pltpu.VMEM((2,) + message.shape, bf16),
            ],
            copies=2,
            micros=20,
        )
    one, two = swaps((one, two), "gy")
    with jax.named_scope("turn"):
        predicted, my_there, my_w, my_back, rep = run(
            turn_kernel,
            [
                (IN_HBM, activated),
                (IN_HBM, there),
                (IN_HBM, w_kept),
                (IN_HBM, back),
            ],
            [
                (IN_HBM, raw),
                (IN_VMEM, struct(there.shape[1:], bf16)),
                (IN_VMEM, unpacked),
                (IN_VMEM, struct(back.shape[1:], bf16)),
                (IN_VMEM, struct((wide, local * MZ * CH), bf16)),
            ],
            limit,
            [round_v, raw_v, pltpu.VMEM(packed.shape, bf16)],
            copies=5,
            micros=2,
        )

    with jax.named_scope("mix_adjoint"):
        d, send = run(
            lambda *refs: adjoint_kernel(local, *refs),
            [(IN_VMEM, array) for array in (received, my_there, my_w, my_back, rep)],
            [(IN_VMEM, mode_field), (IN_HBM, chunk)],
            limit,
            [sent],
            copies=4,
            micros=2,
        )
    received = exchange(send)

    with jax.named_scope("backward"):
        weight_grad, base, my_inverse = run(
            backward_kernel,
            [
                (IN_VMEM, d),
                (IN_VMEM, v),
                (IN_HBM, grad),
                (IN_HBM, grad_round),
                (IN_HBM, kept_z),
                (IN_HBM, one),
                (IN_HBM, two),
                (IN_HBM, fine),
                (IN_VMEM, lin_weight),
                (IN_HBM, conv_fine),
                (IN_HBM, conv_coarse),
                (IN_HBM, inverse_table),
            ],
            [
                (IN_HBM, struct((2, local, rows, CH))),
                (IN_VMEM, field),
                (IN_VMEM, struct(inverse_table.shape, bf16)),
            ],
            limit + (10 << 20),
            [
                pltpu.VMEM((2, local, rows, CH), f32),
                field_v,
                pltpu.VMEM((cells + 2, CH, span), bf16),
                pltpu.VMEM((2,) + message.shape, bf16),
                pltpu.VMEM((2,) + y_message.shape, bf16),
                pltpu.VMEM((8, 8 * CH, span), bf16),
                taps_v,
                taps_v,
                bands_v,
                pltpu.VMEM((6, 8 * CH, span // 2), bf16),
                pltpu.VMEM((6, 8 * CH, span), bf16),
            ],
            copies=9 + local,
            micros=6,
        )
    weight_grad = weight_grad.reshape(spec_weight.shape)

    with jax.named_scope("last"):
        (sensitivity,) = run(
            lambda *refs: last_kernel(local, *refs),
            [(IN_VMEM, received), (IN_VMEM, my_inverse), (IN_VMEM, base)],
            [(IN_HBM, raw)],
            limit,
            [raw_v, wide_scratch, left_scratch],
            copies=2,
            micros=2,
        )
    return (predicted, sensitivity, weight_grad)


def solution(mesh):
    field = P(None, "gy", "gz", None)
    modes = P(None, "gy", "gz", None, None, None)
    return jax.shard_map(
        shards,
        mesh=mesh,
        in_specs=(field, field, modes, P(), P(), P(), P(), P()),
        out_specs=(field, field, modes),
        check_vma=False,
    )
```

```python
import math

import jax
import jax.numpy as jnp
import ml_dtypes
import numpy as np
from jax import lax
from jax.experimental import pallas as pl
from jax.experimental.pallas import tpu as pltpu
from jax.sharding import PartitionSpec as P

MX = 32
MY = 32
MZ = 8
CH = 32
BOTH = ("gy", "gz")

f32 = jnp.float32
bf16 = jnp.bfloat16
root_coef = math.sqrt(2.0 / math.pi)
NN = (((1,), (0,)), ((), ()))
NT = (((1,), (1,)), ((), ()))
TN = (((0,), (0,)), ((), ()))


def dot(a, b, form=NN):
    return lax.dot_general(a, b, form, preferred_element_type=f32)


def halves(value):
    high = value.astype(bf16)
    return high, (value - high.astype(f32)).astype(bf16)


def iota(shape, dim):
    return lax.broadcasted_iota(jnp.int32, shape, dim)


IN_VMEM = pl.BlockSpec(memory_space=pltpu.VMEM)
IN_HBM = pl.BlockSpec(memory_space=pltpu.HBM)


def struct(shape, kind=f32):
    return jax.ShapeDtypeStruct(shape, kind)


def run(kernel, ins, outs, limit, scratch=(), micros=1.0, copies=0, **grid):
    scratch = list(scratch)
    if copies:
        scratch.append(pltpu.SemaphoreType.DMA((copies,)))
    held = {id(IN_HBM): pltpu.HBM, id(IN_VMEM): pltpu.VMEM}

    def placed(spec, array):
        if id(spec) in held:
            return pltpu.with_memory_space_constraint(array, held[id(spec)])
        return array

    def shaped(spec, shape):
        if id(spec) in held:
            return held[id(spec)](shape.shape, shape.dtype)
        return shape

    return pl.pallas_call(
        kernel,
        in_specs=[spec for spec, _ in ins],
        out_specs=[spec for spec, _ in outs],
        out_shape=[shaped(spec, shape) for spec, shape in outs],
        scratch_shapes=scratch,
        compiler_params=pltpu.CompilerParams(vmem_limit_bytes=limit),
        cost_estimate=pl.CostEstimate(
            flops=int(micros * 1.1e9), bytes_accessed=1 << 16, transcendentals=0
        ),
        **grid,
    )(*[placed(spec, array) for spec, array in ins])


def begin(sem, first, *pairs):
    copies = [
        pltpu.make_async_copy(source, target, sem.at[first + i])
        for i, (source, target) in enumerate(pairs)
    ]
    for copy in copies:
        copy.start()
    return copies


def finish(*copies):
    for copy in copies:
        copy.wait()


def kept(count, length):
    position = np.arange(count)
    return np.where(position < count // 2, position, length - count + position)


def split_np(table):
    high = table.astype(ml_dtypes.bfloat16)
    return high, (table - high.astype(np.float64)).astype(ml_dtypes.bfloat16)


def x_tables(cells_x, blocks):
    local = MX // blocks
    freqs = kept(MX, cells_x).reshape(blocks, local).T
    angles = 2.0 * np.pi * ((freqs[:, :, None] * np.arange(cells_x)) % cells_x) / cells_x
    table = np.stack([np.cos(angles), -np.sin(angles)], axis=2).reshape(2 * MX, cells_x)
    return np.concatenate(split_np(table), axis=0)


def x_back_table(cells_x, gy, gz):
    local = MX // gy
    freqs = kept(MX, cells_x).reshape(gy, local).T
    angles = 2.0 * np.pi * ((freqs[:, :, None] * np.arange(cells_x)) % cells_x) / cells_x
    table = np.stack([np.cos(angles), -np.sin(angles)], axis=2)
    table = np.broadcast_to(table[:, :, None], (local, gy, gz, 2, cells_x))
    return np.concatenate(split_np(table.reshape(-1, cells_x)), axis=0)


def yz_angles(xp, freqs_y, gy, gz, rows_y, rows_z):
    span_y, span_z = gy * rows_y, gz * rows_z
    phase_y = (freqs_y[:, None] * xp.arange(span_y)[None]) % span_y
    phase_z = (xp.arange(MZ)[:, None] * xp.arange(span_z)[None]) % span_z
    phase_y = phase_y.reshape(-1, 1, gy, 1, rows_y, 1)
    phase_z = phase_z.reshape(1, MZ, 1, gz, 1, rows_z)
    turn = (phase_y * span_z + phase_z * span_y) % (span_y * span_z)
    return turn.reshape(turn.shape[0] * MZ, gy * gz, rows_y * rows_z)


def yz_table(xp, freqs_y, gy, gz, rows_y, rows_z):
    cells = gy * gz * rows_y * rows_z
    turn = yz_angles(xp, freqs_y, gy, gz, rows_y, rows_z)
    angles = 2.0 * math.pi / cells * turn
    cosine, sine = xp.cos(angles), xp.sin(angles)
    table = xp.stack([xp.stack([cosine, sine], 2), xp.stack([-sine, cosine], 2)], 0)
    return table.reshape(2 * turn.shape[0], -1)


def mode_tables(gy, gz, rows_y, rows_z, scale):
    local = MY // gz
    cells = gy * gz * rows_y * rows_z
    freqs = kept(MY, gy * rows_y).reshape(gz, local)
    if gz * 2 * local * MZ * 2 * cells <= 1 << 20:
        there, back = [], []
        for block in range(gz):
            high, low = split_np(scale * yz_table(np, freqs[block], gy, gz, rows_y, rows_z))
            there.append(np.concatenate([high, low], 0))
            back.append(np.concatenate([high.T, low.T], 1))
        return jnp.asarray(np.stack(there)), jnp.asarray(np.stack(back))
    where = lax.axis_index("gz")
    mine = lax.dynamic_index_in_dim(jnp.asarray(freqs, jnp.int32), where, keepdims=False)
    high, low = halves(scale * yz_table(jnp, mine, gy, gz, rows_y, rows_z).astype(f32))
    return jnp.concatenate([high, low], 0)[None], jnp.concatenate([high.T, low.T], 1)[None]


def put_x_modes(product, local, blocks, copies, cells, scratch, sent, send_ref, sem, first):
    rows = 2 * blocks
    half = blocks // 2
    moves = []
    for start in (0, half):
        at = 2 * start * cells
        for cell in range(cells):
            piece = product[:, cell * CH : (cell + 1) * CH]
            parts = [piece[k * rows + 2 * start : k * rows + 2 * start + blocks] for k in range(local)]
            scratch[pl.ds(at + cell, blocks, stride=cells), :] = jnp.concatenate(parts, axis=1)
        for block in range(start, start + half):
            value = scratch[block * 2 * cells : (block + 1) * 2 * cells].astype(bf16)
            for copy in range(copies):
                sent[block * copies + copy] = value
        part = pl.ds(start * copies, half * copies)
        moves += begin(sem, first + len(moves), (sent.at[part], send_ref.at[part]))
    return moves


def odd(axis):
    return lax.axis_index(axis) & 1


def first(axis):
    return lax.axis_index(axis) == 0


def last(axis):
    return lax.axis_index(axis) == lax.axis_size(axis) - 1


def arrive_kernel(raw_ref, table_ref, u_ref, one_ref, two_ref, my_table_ref, raw, sem):
    loads = begin(sem, 0, (raw_ref, raw), (table_ref, my_table_ref))
    finish(*loads)
    u = jnp.transpose(raw[...], (1, 2, 0, 3))
    u_ref[...] = u
    side = odd("gz")
    one_ref[...] = u_ref[:, pl.ds(1 - side, 3)]
    two_ref[...] = u_ref[:, pl.ds(side, 3)]


def spread_kernel(
    exact, local, blocks, copies, u_ref, table, *refs
):
    *refs, scratch, sent, sem = refs
    count = len(refs) // 2
    stores = begin(sem, 2, *zip(refs[:count], refs[count + 1 :]))
    send_ref = refs[count]
    cells = u_ref.shape[0] * u_ref.shape[1]
    u = u_ref[...].reshape(cells * CH, -1)
    if exact:
        both = dot(table[...], u, NT)
        product = both[: 2 * MX] + both[2 * MX :]
    else:
        high, low = halves(u)
        both = dot(table[...], high, NT)
        product = both[: 2 * MX] + both[2 * MX :] + dot(table[: 2 * MX], low, NT)
    moves = put_x_modes(product, local, blocks, copies, cells, scratch, sent, send_ref, sem, 0)
    finish(*moves, *stores)


def pick(tables_ref):
    if tables_ref.shape[0] == 1:
        return tables_ref.at[0]
    return tables_ref.at[lax.axis_index("gz")]


def mode_values(rec_ref, there, rows):
    both = dot(there[...], rec_ref[...].reshape(-1, rec_ref.shape[2]))
    return both[:rows] + both[rows:]


def put_back(values, back_ref, sent, send_ref, sem, first):
    high, low = halves(values)
    parts = jnp.concatenate([high, high, low], 0)
    rows = values.shape[0]
    devices, depth, wide = sent.shape
    part = devices // 4
    moves = []
    for step in range(4):
        at = slice(step * part * depth, (step + 1) * part * depth)
        result = dot(jnp.concatenate([back_ref[at], back_ref[at, :rows]], 1), parts)
        sent[step * part : (step + 1) * part] = result.astype(bf16).reshape(part, depth, wide)
        span = pl.ds(step * part, part)
        moves += begin(sem, first + step, (sent.at[span], send_ref.at[span]))
    finish(*moves)


def kz_weight(shape):
    return jnp.where(iota(shape, 0) % MZ == 0, 1.0, 2.0).astype(f32)


def same_mode(rows, lanes):
    return (iota((rows, lanes), 0) % MZ) == ((iota((rows, lanes), 1) // CH) % MZ)


def mix_kernel(
    local,
    rec_ref,
    there_ref,
    high_ref,
    low_ref,
    back_ref,
    v_ref,
    kept_w_ref,
    send_ref,
    kept_v,
    sent,
    sem,
):
    store_w = begin(sem, 5, (high_ref, kept_w_ref))
    rows = there_ref.shape[0] // 2
    modes = rows // 2
    wide = local * CH
    v = mode_values(rec_ref, there_ref, rows)
    kept_v[...] = v
    store = begin(sem, 0, (kept_v, v_ref))
    real, imag = v[:modes], v[modes:]
    pair = (
        jnp.concatenate([real, -imag], 1),
        jnp.concatenate([imag, real], 1),
    )
    lane_k = (iota((MZ, 2 * wide), 1) // CH) % local
    size = MZ * CH
    diag = same_mode(2 * MZ * local, size)
    placed = [[[None] * (modes // MZ) for _ in range(local)] for _ in range(2)]
    for g in range(modes // MZ):
        pieces = []
        for k in range(local):
            for part in range(2):
                piece = pair[part][g * MZ : (g + 1) * MZ]
                pieces.append(jnp.where(lane_k == k, piece, 0.0))
        left_high, left_low = halves(jnp.concatenate(pieces, 0))
        w_high = high_ref[g]
        w_low = low_ref[g]
        count = left_high.shape[0]
        both = dot(jnp.concatenate([left_high, left_low], 0), w_high)
        value = both[:count] + both[count:] + dot(left_high, w_low)
        value = jnp.where(diag, value, 0.0)
        for k in range(local):
            for part in range(2):
                at = (2 * k + part) * MZ
                placed[part][k][g] = value[at : at + MZ]
    columns = [jnp.concatenate(placed[0][k] + placed[1][k], 0) for k in range(local)]
    all_values = jnp.concatenate(columns, 1)
    shape = (local * size, wide)
    fold = (iota(shape, 0) // size == iota(shape, 1) // CH) & (
        iota(shape, 0) % CH == iota(shape, 1) % CH
    )
    fold = fold.astype(bf16)
    high, low = halves(all_values)
    mixed = dot(high, fold) + dot(low, fold)
    put_back(mixed * kz_weight(mixed.shape), back_ref, sent, send_ref, sem, 1)
    finish(*store, *store_w)


def adjoint_kernel(
    local,
    rec_ref,
    there_ref,
    high_ref,
    back_ref,
    rep_ref,
    d_ref,
    send_ref,
    sent,
    sem,
):
    rows = there_ref.shape[0] // 2
    modes = rows // 2
    wide = local * CH
    size = MZ * CH
    d = mode_values(rec_ref, there_ref, rows)
    d = d * kz_weight(d.shape)
    d_ref[...] = d
    high, low = halves(d)
    spread = dot(high, rep_ref[...]) + dot(low, rep_ref[...])
    spread = jnp.where(same_mode(rows, local * size), spread, 0.0)
    lane_k = (iota((2 * MZ, 2 * wide), 1) // CH) % local
    parts = ([], [])
    for g in range(modes // MZ):
        pieces = []
        for k in range(local):
            for part in range(2):
                at = part * modes + g * MZ
                pieces.append(spread[at : at + MZ, k * size : (k + 1) * size])
        left_high, left_low = halves(jnp.concatenate(pieces, 0))
        count = left_high.shape[0]
        both = dot(
            jnp.concatenate([left_high, left_low], 0), high_ref[g * size : (g + 1) * size]
        )
        value = both[:count] + both[count:]
        total = None
        for k in range(local):
            piece = jnp.where(lane_k == k, value[2 * k * MZ : 2 * (k + 1) * MZ], 0.0)
            total = piece if total is None else total + piece
        parts[0].append(total[:MZ])
        parts[1].append(total[MZ:])
    real = jnp.concatenate(parts[0], 0)
    imag = jnp.concatenate(parts[1], 0)
    value = jnp.concatenate(
        [real[:, :wide] + imag[:, wide:], imag[:, :wide] - real[:, wide:]], 0
    )
    put_back(value, back_ref, sent, send_ref, sem, 0)


def setup_kernel(
    local,
    w_ref,
    there_ref,
    back_ref,
    high_ref,
    low_ref,
    my_there_ref,
    my_back_ref,
    w,
    sem,
):
    parts = high_ref.shape[0]
    rows = w.shape[2] // parts
    spans = [pl.ds(step * rows, rows) for step in range(parts)]
    loads = begin(sem, 0, *[(w_ref.at[:, :, span], w.at[:, :, span]) for span in spans])
    tables = begin(
        sem, parts, (pick(there_ref), my_there_ref), (pick(back_ref), my_back_ref)
    )
    for step in range(parts):
        at = slice(step * rows, (step + 1) * rows)
        finish(loads[step])
        pieces = [w[part, k, at] for part in range(2) for k in range(local)]
        high_ref[step], low_ref[step] = halves(jnp.concatenate(pieces, 1).T)
    finish(*tables)


def put_weight_grad(d_ref, v_ref, out, out_ref, sem, first):
    rows, wide = d_ref.shape
    modes = rows // 2
    size = MZ * CH
    keep = same_mode(rows, size)
    d_halves = halves(d_ref[...])
    v_halves = halves(v_ref[...])
    stores = []
    for k in range(wide // CH):
        shape = (wide, size)
        rep = (iota(shape, 0) == k * CH + iota(shape, 1) % CH).astype(bf16)
        d_high, d_low = [jnp.where(keep, dot(value, rep), 0.0) for value in d_halves]
        at = slice(k * CH, (k + 1) * CH)
        v_high, v_low = [value[:, at].astype(f32) for value in v_halves]
        for g in range(modes // MZ):
            real = slice(g * MZ, (g + 1) * MZ)
            imag = slice(modes + g * MZ, modes + (g + 1) * MZ)
            left = jnp.concatenate(
                [d_high[real], d_high[imag], d_low[real], d_low[imag], d_high[real], d_high[imag]],
                0,
            ).astype(bf16)
            for part in range(2):
                rights = []
                for v in (v_high, v_high, v_low):
                    rights += [v[real], v[imag]] if part == 0 else [-v[imag], v[real]]
                right = jnp.concatenate(rights, 0).astype(bf16)
                out[part, k, g * size : (g + 1) * size, :] = dot(left, right, TN)
        stores += begin(sem, first + k, (out.at[:, k], out_ref.at[:, k]))
    return stores


def widen(rec_ref, wide):
    wide[...] = rec_ref[...].reshape(-1, rec_ref.shape[2]).astype(f32)


def inverse_x(wide, table, local, cells, part, left):
    rows = wide.shape[0] // cells
    for cell in part:
        turned = wide[pl.ds(cell, rows, stride=cells), :].T.astype(bf16)
        for k in range(local):
            left[cell * CH : (cell + 1) * CH, k * rows : (k + 1) * rows] = turned[
                k * CH : (k + 1) * CH
            ]
    depth = local * rows
    value = left[part.start * CH : part.stop * CH]
    return dot(value, table[:depth]) + dot(value, table[depth:])


def gelu_pair(pre_act):
    cube_term = pre_act * pre_act * pre_act
    tanh_result = jnp.tanh(root_coef * (pre_act + 0.044715 * cube_term))
    activated_output = 0.5 * pre_act * (1.0 + tanh_result)
    gelu_slope = 0.5 * (1.0 + tanh_result) + 0.5 * pre_act * (
        1.0 - tanh_result * tanh_result
    ) * root_coef * (1.0 + 3.0 * 0.044715 * pre_act * pre_act)
    return (activated_output, gelu_slope)


def middle_kernel(
    local,
    rec_ref,
    back_ref,
    base_ref,
    cot_ref,
    coarse_ref,
    out_ref,
    grad_ref,
    rounded,
    one_ref,
    two_ref,
    wide,
    left,
):
    rows_y, rows_z, _, span = base_ref.shape
    cells = rows_y * rows_z
    widen(rec_ref, wide)
    pre_act = inverse_x(wide, back_ref, local, cells, range(cells), left)
    pre_act = pre_act + base_ref[...].reshape(pre_act.shape)
    activated, slope = gelu_pair(pre_act)
    out_ref[...] = activated.astype(bf16).reshape(out_ref.shape)
    value = cot_ref[...].astype(f32).reshape(pre_act.shape) * slope
    grad_ref[...] = value.reshape(grad_ref.shape)
    rounded[:cells] = value.astype(bf16).reshape(cells, CH, span)
    side = odd("gz")
    for y in range(rows_y):
        one_ref[y] = rounded[rows_z * y + (rows_z - 1) * (1 - side)]
        two_ref[y] = rounded[rows_z * y + (rows_z - 1) * side]
    pool = pool_matrix(span)
    for yc in range(2):
        sums = []
        for zc in range(2):
            y, z = 2 * yc, 2 * zc
            sums.append(
                grad_ref[y, z] + grad_ref[y, z + 1] + grad_ref[y + 1, z] + grad_ref[y + 1, z + 1]
            )
        total_high, total_low = halves(jnp.concatenate(sums, 0))
        total = dot(total_high, pool) + dot(total_low, pool)
        pieces = []
        for zc in range(2):
            piece = total[zc * CH : (zc + 1) * CH]
            pieces.append(jnp.where(coarse_ref[yc, zc].astype(f32) > 0, piece, 0.0))
        piece = jnp.concatenate(pieces, 1).astype(bf16)
        rounded[cells + yc] = piece
        one_ref[rows_y + yc] = piece
        two_ref[rows_y + yc] = piece


def last_kernel(local, rec_ref, back_ref, base_ref, out_ref, out, wide, left, sem):
    rows_y, rows_z, _, span = base_ref.shape
    cells = rows_y * rows_z
    widen(rec_ref, wide)
    moves = []
    for y in range(0, rows_y, 2):
        part = range(y * rows_z, (y + 2) * rows_z)
        value = inverse_x(wide, back_ref, local, cells, part, left)
        value = value.reshape(2, rows_z, CH, span) + base_ref[y : y + 2]
        out[:, y : y + 2] = jnp.transpose(value.astype(bf16), (2, 0, 1, 3))
        at = pl.ds(y, 2)
        moves += begin(sem, y // 2, (out.at[:, at], out_ref.at[:, at]))
    finish(*moves)


def turn_kernel(
    value_ref,
    there_ref,
    w_ref,
    back_ref,
    out_ref,
    my_there_ref,
    my_w_ref,
    my_back_ref,
    rep_ref,
    value,
    out,
    packed,
    sem,
):
    loads = begin(
        sem,
        0,
        (value_ref, value),
        (pick(there_ref), my_there_ref),
        (w_ref, packed),
        (pick(back_ref), my_back_ref),
    )
    shape = rep_ref.shape
    size = MZ * CH
    rep = (iota(shape, 1) // size == iota(shape, 0) // CH) & (
        iota(shape, 1) % CH == iota(shape, 0) % CH
    )
    rep_ref[...] = rep.astype(bf16)
    finish(loads[0])
    out[...] = jnp.transpose(value[...], (2, 0, 1, 3))
    store = begin(sem, 4, (out, out_ref))
    finish(*loads[1:])
    for g in range(packed.shape[0]):
        my_w_ref[g * size : (g + 1) * size] = packed[g].astype(f32).T.astype(bf16)
    finish(*store)


def write_bands(adjoint, k_ref, out, index):
    for a in range(3):
        for e in range(3):
            taps = []
            for b in range(3):
                if adjoint:
                    tap = k_ref[9 * (2 - a) + 3 * (2 - b) + 2 - e].astype(f32).T
                else:
                    tap = k_ref[9 * a + 3 * b + e].astype(f32)
                taps.append(tap)
            taps = jnp.concatenate(taps, 1)
            for z in range(4):
                pieces = [taps, jnp.zeros((CH, (5 - z) * CH), f32)]
                if z > 0:
                    pieces.insert(0, jnp.zeros((CH, z * CH), f32))
                row = jnp.concatenate(pieces, 1)
                at = (e * 4 + z) * CH
                out[index, at : at + CH, a * 8 * CH : (a + 1) * 8 * CH] = row.astype(bf16)


def x_sum(low, same, high):
    span = same.shape[1]
    lane = iota(same.shape, 1)
    before = jnp.where(lane == 0, 0.0, pltpu.roll(low, 1, axis=1))
    after = jnp.where(lane == span - 1, 0.0, pltpu.roll(high, span - 1, axis=1))
    return same + before + after


def band_conv(bands, planes):
    value = dot(bands, jnp.concatenate(planes, 0))
    size = 4 * CH
    return x_sum(value[:size], value[size : 2 * size], value[2 * size :])


def column(row_ref, copies):
    eye = iota((CH, CH), 0) == iota((CH, CH), 1)
    value = jnp.sum(jnp.where(eye, row_ref[...], 0.0), axis=1, keepdims=True)
    return jnp.concatenate([value] * copies, 0)


def block_diagonal(matrix):
    shape = (4 * CH, 4 * CH)
    wide = jnp.concatenate([matrix.astype(f32)] * 4, 1)
    tiled = jnp.concatenate([wide] * 4, 0)
    return jnp.where(iota(shape, 0) // CH == iota(shape, 1) // CH, tiled, 0.0).astype(bf16)


def pool_matrix(span):
    shape = (span, span // 2)
    return (iota(shape, 0) // 2 == iota(shape, 1)).astype(bf16)


def up_matrix(span):
    shape = (span // 2, span)
    return (iota(shape, 1) // 2 == iota(shape, 0)).astype(bf16)


def y_message_kernel(u_ref, z_one_ref, z_two_ref, one_ref, two_ref, rows, sem):
    side = odd("gz")
    for y in range(4):
        for z in range(3):
            at = pl.multiple_of((7 * (1 - side) + z) * CH, CH)
            rows[y, pl.ds(at, CH)] = z_one_ref[y, z]
            at = pl.multiple_of((7 * side + z) * CH, CH)
            rows[y, pl.ds(at, CH)] = z_two_ref[y, z]
        for z in range(4):
            rows[y, (z + 3) * CH : (z + 4) * CH] = u_ref[y, z]
    blank = jnp.zeros((4, 3 * CH, rows.shape[2]), bf16)

    @pl.when(first("gz"))
    def low_end():
        rows[:, : 3 * CH] = blank

    @pl.when(last("gz"))
    def high_end():
        rows[:, 7 * CH :] = blank

    side = odd("gy")
    finish(
        *begin(
            sem, 0, (rows.at[pl.ds(1 - side, 3)], one_ref), (rows.at[pl.ds(side, 3)], two_ref)
        )
    )


def forward_conv_kernel(
    own_one_ref,
    own_two_ref,
    y_one_ref,
    y_two_ref,
    lin_ref,
    taps_fine_ref,
    taps_coarse_ref,
    bias_fine_ref,
    bias_coarse_ref,
    cot_ref,
    table_ref,
    x_ref,
    base,
    fine_ref,
    coarse,
    my_cot_ref,
    my_table_ref,
    my_x_ref,
    grid,
    taps_fine,
    taps_coarse,
    raw,
    bands,
    pooled,
    fine,
    sem,
):
    span = grid.shape[2]
    inner = pl.ds(0, 10 * CH)
    side = odd("gy")
    loads = begin(
        sem,
        0,
        (taps_fine_ref, taps_fine),
        (own_one_ref, grid.at[pl.ds(4 - side, 3), inner]),
        (own_two_ref.at[pl.ds(2 * side, 1)], grid.at[pl.ds(3 + 3 * side, 1), inner]),
        (y_one_ref, grid.at[pl.ds(7 * (1 - side), 3), inner]),
        (y_two_ref, grid.at[pl.ds(7 * side, 3), inner]),
        (taps_coarse_ref, taps_coarse),
        (cot_ref, raw),
        (table_ref, my_table_ref),
        (x_ref, my_x_ref),
    )
    edges = [jnp.logical_not(end(axis)) for axis in ("gy", "gz") for end in (first, last)]
    grid[:, 10 * CH :, :] = jnp.zeros((10, 2 * CH, span), bf16)
    pooled[:, 4 * CH :, :] = jnp.zeros((4, 4 * CH, span // 2), bf16)
    bias = column(bias_fine_ref, 4)
    half = 4 * CH
    row_z = iota((half, span), 0) // CH
    finish(loads[0])
    write_bands(False, taps_fine, bands, 0)
    finish(*loads[1:3])
    for y in (3, 4, 2, 1, 0, 5, 6, 7):
        if y == 2:
            finish(loads[3], loads[4])

            @pl.when(first("gy"))
            def low_end():
                grid[:3] = jnp.zeros((3, 12 * CH, span), bf16)

            @pl.when(last("gy"))
            def high_end():
                grid[7:] = jnp.zeros((3, 12 * CH, span), bf16)

        y_in = None
        if y < 2:
            y_in = edges[0]
        elif y >= 6:
            y_in = edges[1]
        for h in range(2):
            at = h * half
            value = band_conv(bands[0], [grid[y + a, at : at + 8 * CH, :] for a in range(3)])
            value = jnp.maximum(value + bias, 0.0)
            inside = (row_z >= 2) | edges[2] if h == 0 else (row_z < 2) | edges[3]
            if y_in is not None:
                inside = inside & y_in
            fine[y, at : at + half, :] = jnp.where(inside, value, 0.0).astype(bf16)
    (store,) = begin(sem, 9, (fine, fine_ref))
    sums = []
    for yc in range(4):
        both = fine[2 * yc].astype(f32) + fine[2 * yc + 1].astype(f32)
        for zc in range(4):
            at = 2 * zc * CH
            sums.append(both[at : at + CH] + both[at + CH : at + 2 * CH])
    pool = pool_matrix(span)
    high, low = halves(jnp.concatenate(sums, 0))
    pools = (0.125 * (dot(high, pool) + dot(low, pool))).astype(bf16)
    pooled[:, : 4 * CH, :] = pools.reshape(4, 4 * CH, span // 2)
    bias = column(bias_coarse_ref, 4)
    finish(loads[5])
    write_bands(False, taps_coarse, bands, 1)
    planes = [jnp.concatenate([pooled[a], pooled[a + 1]], 1) for a in range(3)]
    value = dot(bands[1], jnp.concatenate(planes, 0))
    parts = [value[e * half : (e + 1) * half] for e in range(3)]
    for yc in range(2):
        at = slice(yc * span // 2, (yc + 1) * span // 2)
        value = x_sum(*[part[:, at] for part in parts])
        value = jnp.maximum(value + bias, 0.0).astype(bf16)
        coarse[yc] = value[: 2 * CH].reshape(2, CH, span // 2)
    lifted = dot(coarse[...].reshape(half, span // 2), up_matrix(span))
    lin = block_diagonal(lin_ref[...])
    for y in range(4):
        total = dot(lin, grid[y + 3, 3 * CH : 7 * CH, :])
        total = total + fine[y + 2, 2 * CH : 6 * CH, :].astype(f32)
        for z in range(4):
            at = (y // 2 * 2 + z // 2) * CH
            base[y, z] = total[z * CH : (z + 1) * CH] + lifted[at : at + CH]
    finish(loads[6])
    my_cot_ref[...] = jnp.transpose(raw[...], (1, 2, 0, 3))
    finish(store, *loads[7:])


def y_gradient_kernel(
    round_ref, z_one_ref, z_two_ref, kept_ref, one_ref, two_ref, own, halo, sem
):
    (load,) = begin(sem, 0, (round_ref, own))
    side = odd("gz")
    halo[1 - side] = z_one_ref[...]
    halo[side] = z_two_ref[...]

    @pl.when(first("gz"))
    def low_end():
        halo[0] = jnp.zeros(halo.shape[1:], bf16)

    @pl.when(last("gz"))
    def high_end():
        halo[1] = jnp.zeros(halo.shape[1:], bf16)

    (store,) = begin(sem, 1, (halo, kept_ref))
    finish(load)
    side = odd("gy")
    for out_ref, y in ((one_ref, 3 * (1 - side)), (two_ref, 3 * side)):
        out_ref[0] = halo[0, y]
        out_ref[1:5] = own[pl.ds(4 * y, 4)]
        out_ref[5] = halo[1, y]
        for yc in range(2):
            out_ref[6 + 3 * yc] = halo[0, 4 + yc]
            out_ref[7 + 3 * yc] = own[16 + yc]
            out_ref[8 + 3 * yc] = halo[1, 4 + yc]
    finish(store)


def backward_kernel(
    d_ref,
    v_ref,
    grad_ref,
    round_ref,
    kept_ref,
    y_one_ref,
    y_two_ref,
    fine_ref,
    lin_ref,
    taps_fine_ref,
    taps_coarse_ref,
    table_ref,
    weight_ref,
    base,
    my_table_ref,
    weights,
    grad,
    rounded,
    kept,
    beside,
    fine,
    taps_fine,
    taps_coarse,
    bands,
    coarse_grid,
    fine_grid,
    sem,
):
    side = odd("gy")
    loads = begin(
        sem,
        0,
        (taps_coarse_ref, taps_coarse),
        (round_ref, rounded),
        (kept_ref, kept),
        (y_one_ref, beside.at[1 - side]),
        (y_two_ref, beside.at[side]),
        (grad_ref, grad),
        (fine_ref, fine),
        (taps_fine_ref, taps_fine),
        (table_ref, my_table_ref),
    )
    stores = put_weight_grad(d_ref, v_ref, weights, weight_ref, sem, 9)
    finish(loads[0], loads[7])
    write_bands(True, taps_coarse, bands, 1)
    write_bands(True, taps_fine, bands, 0)
    span = grad.shape[3]
    half = span // 2
    coarse_grid[:, 6 * CH :, :] = jnp.zeros((6, 2 * CH, half), bf16)
    fine_grid[:, 6 * CH :, :] = jnp.zeros((6, 2 * CH, span), bf16)

    def place(yc, pair, value):
        for zc in range(2):
            at = (2 * pair + zc) * CH
            coarse_grid[yc, at : at + CH, :] = value[:, zc * half : (zc + 1) * half]

    finish(*loads[1:5])

    @pl.when(first("gy"))
    def low_end():
        beside[0] = jnp.zeros(beside.shape[1:], bf16)

    @pl.when(last("gy"))
    def high_end():
        beside[1] = jnp.zeros(beside.shape[1:], bf16)

    for yc in range(2):
        place(2 + yc, 0, kept[0, 4 + yc])
        place(2 + yc, 1, rounded[16 + yc])
        place(2 + yc, 2, kept[1, 4 + yc])
        for pair in range(3):
            place(yc, pair, beside[0, 6 + 3 * yc + pair])
            place(4 + yc, pair, beside[1, 6 + 3 * yc + pair])
    pooled = [
        0.125 * band_conv(bands[1], [coarse_grid[yc + a] for a in range(3)]) for yc in range(4)
    ]
    high, low = halves(jnp.concatenate(pooled, 0))
    up = up_matrix(span)
    lifted = dot(high, up) + dot(low, up)
    finish(*loads[5:7])
    for y in range(6):
        yc = (y + 1) // 2
        for z in range(6):
            at = (4 * yc + (z + 1) // 2) * CH
            if 1 <= y <= 4 and 1 <= z <= 4:
                value = grad[y - 1, z - 1]
            elif 1 <= y <= 4:
                value = kept[z // 5, y - 1].astype(f32)
            else:
                value = beside[y // 5, z].astype(f32)
            value = value + lifted[at : at + CH]
            mask = fine[y + 1, (z + 1) * CH : (z + 2) * CH, :].astype(f32) > 0
            fine_grid[y, z * CH : (z + 1) * CH, :] = jnp.where(mask, value, 0.0).astype(bf16)
    lin = block_diagonal(lin_ref[...].astype(f32).T.astype(bf16))
    for y in range(4):
        value = band_conv(bands[0], [fine_grid[y + a] for a in range(3)])
        value = value + dot(lin, rounded[4 * y : 4 * y + 4].reshape(4 * CH, span))
        base[y] = value.reshape(4, CH, span)
    finish(loads[8], *stores)


def swaps(blocks, axis):
    size_y, size_z = lax.axis_size("gy"), lax.axis_size("gz")
    results = []
    for start, block in enumerate(blocks):
        pairs = []
        for y in range(size_y):
            for z in range(size_z):
                step = 1 if ((y if axis == "gy" else z) - start) % 2 == 0 else -1
                to_y, to_z = y, z
                if axis == "gy":
                    to_y = (y + step) % size_y
                elif 0 <= z + step < size_z:
                    to_z = z + step
                else:
                    to_y = y ^ 1
                pairs.append((y * size_z + z, to_y * size_z + to_z))
        results.append(lax.ppermute(block, BOTH, pairs))
    return results


def exchange(block):
    return lax.all_to_all(block, BOTH, split_axis=0, concat_axis=0, tiled=True)


def shards(
    carbon_input_volume,
    cotangent,
    spec_weight,
    lin_weight,
    conv_fine,
    bias_fine,
    conv_coarse,
    bias_coarse,
):
    channels, rows_y, rows_z, span = carbon_input_volume.shape
    gy, gz = lax.axis_size("gy"), lax.axis_size("gz")
    devices = gy * gz
    cells = rows_y * rows_z
    local = MX // gy
    modes = (MY // gz) * MZ
    wide = local * CH
    scale = 1.0 / math.sqrt(span * cells * devices)
    there, back = mode_tables(gy, gz, rows_y, rows_z, scale)
    forward_x = jnp.asarray(x_tables(span, gy))
    inverse_table = jnp.asarray(x_back_table(span, gy, gz))

    limit = (14 << 20) + devices * (64 << 10)
    chunk = struct((devices, 2 * cells, wide), bf16)
    sent = pltpu.VMEM(chunk.shape, bf16)
    field = struct((rows_y, rows_z, CH, span))
    field_v = pltpu.VMEM(field.shape, f32)
    round_field = struct(field.shape, bf16)
    round_v = pltpu.VMEM(field.shape, bf16)
    raw = struct(carbon_input_volume.shape, bf16)
    raw_v = pltpu.VMEM(raw.shape, bf16)
    taps_v = pltpu.VMEM(conv_fine.shape, bf16)
    x_scratch = pltpu.VMEM((2 * gy * cells, wide), f32)
    wide_scratch = pltpu.VMEM((devices * 2 * cells, wide), f32)
    left_scratch = pltpu.VMEM((cells * CH, local * devices * 2), bf16)
    mode_field = struct((2 * modes, wide))
    mode_v = pltpu.VMEM(mode_field.shape, f32)
    rows = modes * CH
    packed = struct((modes // MZ, 2 * wide, MZ * CH), bf16)
    unpacked = struct((rows, 2 * wide), bf16)
    bands_v = pltpu.VMEM((2, 12 * CH, 24 * CH), bf16)
    side = struct((rows_y, 3, CH, span), bf16)
    message = struct((6, CH, span), bf16)
    y_side = struct((3, 10 * CH, span), bf16)
    y_message = struct((12, CH, span), bf16)

    with jax.named_scope("arrive"):
        u, one, two, my_x = run(
            arrive_kernel,
            [(IN_HBM, carbon_input_volume), (IN_HBM, forward_x)],
            [
                (IN_VMEM, round_field),
                (IN_VMEM, side),
                (IN_VMEM, side),
                (IN_VMEM, struct(forward_x.shape, bf16)),
            ],
            limit,
            [raw_v],
            copies=2,
        )
    one, two = swaps((one, two), "gz")

    def spread(values, table, exact, *others):
        with jax.named_scope("spread"):
            return run(
                lambda *refs: spread_kernel(exact, local, gy, gz, *refs),
                [(IN_VMEM, array) for array in (values, table) + others],
                [(IN_HBM, chunk)] + [(IN_HBM, struct(x.shape, x.dtype)) for x in others],
                limit,
                [x_scratch, sent],
                copies=2 + len(others),
                micros=1.2,
            )

    received = exchange(spread(u, my_x, True)[0])

    with jax.named_scope("y_message"):
        own_one, own_two = run(
            y_message_kernel,
            [(IN_VMEM, u), (IN_VMEM, one), (IN_VMEM, two)],
            [(IN_HBM, y_side), (IN_HBM, y_side)],
            limit,
            [pltpu.VMEM((rows_y, 10 * CH, span), bf16)],
            copies=2,
        )
    one, two = swaps((own_one, own_two), "gy")

    with jax.named_scope("setup"):
        w_high, w_low, my_there, my_back = run(
            lambda *refs: setup_kernel(local, *refs),
            [
                (IN_HBM, spec_weight.reshape(2, local, rows, CH)),
                (IN_HBM, there),
                (IN_HBM, back),
            ],
            [
                (IN_VMEM, packed),
                (IN_VMEM, packed),
                (IN_VMEM, struct(there.shape[1:], bf16)),
                (IN_VMEM, struct(back.shape[1:], bf16)),
            ],
            limit + (10 << 20),
            [pltpu.VMEM((2, local, rows, CH), f32)],
            copies=10,
            micros=4.5,
        )

    with jax.named_scope("mix"):
        v, w_kept, send = run(
            lambda *refs: mix_kernel(local, *refs),
            [
                (IN_VMEM, received),
                (IN_VMEM, my_there),
                (IN_VMEM, w_high),
                (IN_VMEM, w_low),
                (IN_VMEM, my_back),
            ],
            [(IN_HBM, mode_field), (IN_HBM, packed), (IN_HBM, chunk)],
            limit,
            [mode_v, sent],
            copies=6,
            micros=3,
        )
    received = exchange(send)

    with jax.named_scope("forward_convs"):
        base, fine, coarse, cot, my_inverse, my_x = run(
            forward_conv_kernel,
            [
                (IN_HBM, own_one),
                (IN_HBM, own_two),
                (IN_HBM, one),
                (IN_HBM, two),
                (IN_VMEM, lin_weight),
                (IN_HBM, conv_fine),
                (IN_HBM, conv_coarse),
                (IN_VMEM, bias_fine[None]),
                (IN_VMEM, bias_coarse[None]),
                (IN_HBM, cotangent),
                (IN_HBM, inverse_table),
                (IN_HBM, forward_x),
            ],
            [
                (IN_VMEM, field),
                (IN_HBM, struct((8, 8 * CH, span), bf16)),
                (IN_VMEM, struct((2, 2, CH, span // 2), bf16)),
                (IN_VMEM, round_field),
                (IN_VMEM, struct(inverse_table.shape, bf16)),
                (IN_VMEM, struct(forward_x.shape, bf16)),
            ],
            limit,
            [
                pltpu.VMEM((10, 12 * CH, span), bf16),
                taps_v,
                taps_v,
                raw_v,
                bands_v,
                pltpu.VMEM((4, 8 * CH, span // 2), bf16),
                pltpu.VMEM((8, 8 * CH, span), bf16),
            ],
            copies=10,
            micros=7,
        )

    with jax.named_scope("middle"):
        activated, grad, grad_round, one, two = run(
            lambda *refs: middle_kernel(local, *refs),
            [
                (IN_VMEM, received),
                (IN_VMEM, my_inverse),
                (IN_VMEM, base),
                (IN_VMEM, cot),
                (IN_VMEM, coarse),
            ],
            [
                (IN_VMEM, round_field),
                (IN_VMEM, field),
                (IN_VMEM, struct((cells + 2, CH, span), bf16)),
                (IN_VMEM, message),
                (IN_VMEM, message),
            ],
            limit,
            [wide_scratch, left_scratch],
            micros=2,
        )
    one, two = swaps((one, two), "gz")
    send, grad, activated, grad_round = spread(grad, my_x, False, grad, activated, grad_round)
    received = exchange(send)

    with jax.named_scope("y_gradient"):
        kept_z, one, two = run(
            y_gradient_kernel,
            [(IN_HBM, grad_round), (IN_VMEM, one), (IN_VMEM, two)],
            [
                (IN_HBM, struct((2,) + message.shape, bf16)),
                (IN_VMEM, y_message),
                (IN_VMEM, y_message),
            ],
            limit,
            [
                pltpu.VMEM((cells + 2, CH, span), bf16),
                pltpu.VMEM((2,) + message.shape, bf16),
            ],
            copies=2,
            micros=20,
        )
    one, two = swaps((one, two), "gy")
    with jax.named_scope("turn"):
        predicted, my_there, my_w, my_back, rep = run(
            turn_kernel,
            [
                (IN_HBM, activated),
                (IN_HBM, there),
                (IN_HBM, w_kept),
                (IN_HBM, back),
            ],
            [
                (IN_HBM, raw),
                (IN_VMEM, struct(there.shape[1:], bf16)),
                (IN_VMEM, unpacked),
                (IN_VMEM, struct(back.shape[1:], bf16)),
                (IN_VMEM, struct((wide, local * MZ * CH), bf16)),
            ],
            limit,
            [round_v, raw_v, pltpu.VMEM(packed.shape, bf16)],
            copies=5,
            micros=2,
        )

    with jax.named_scope("mix_adjoint"):
        d, send = run(
            lambda *refs: adjoint_kernel(local, *refs),
            [(IN_VMEM, array) for array in (received, my_there, my_w, my_back, rep)],
            [(IN_VMEM, mode_field), (IN_HBM, chunk)],
            limit,
            [sent],
            copies=4,
            micros=2,
        )
    received = exchange(send)

    with jax.named_scope("backward"):
        weight_grad, base, my_inverse = run(
            backward_kernel,
            [
                (IN_VMEM, d),
                (IN_VMEM, v),
                (IN_HBM, grad),
                (IN_HBM, grad_round),
                (IN_HBM, kept_z),
                (IN_HBM, one),
                (IN_HBM, two),
                (IN_HBM, fine),
                (IN_VMEM, lin_weight),
                (IN_HBM, conv_fine),
                (IN_HBM, conv_coarse),
                (IN_HBM, inverse_table),
            ],
            [
                (IN_HBM, struct((2, local, rows, CH))),
                (IN_VMEM, field),
                (IN_VMEM, struct(inverse_table.shape, bf16)),
            ],
            limit + (10 << 20),
            [
                pltpu.VMEM((2, local, rows, CH), f32),
                field_v,
                pltpu.VMEM((cells + 2, CH, span), bf16),
                pltpu.VMEM((2,) + message.shape, bf16),
                pltpu.VMEM((2,) + y_message.shape, bf16),
                pltpu.VMEM((8, 8 * CH, span), bf16),
                taps_v,
                taps_v,
                bands_v,
                pltpu.VMEM((6, 8 * CH, span // 2), bf16),
                pltpu.VMEM((6, 8 * CH, span), bf16),
            ],
            copies=9 + local,
            micros=6,
        )
    weight_grad = weight_grad.reshape(spec_weight.shape)

    with jax.named_scope("last"):
        (sensitivity,) = run(
            lambda *refs: last_kernel(local, *refs),
            [(IN_VMEM, received), (IN_VMEM, my_inverse), (IN_VMEM, base)],
            [(IN_HBM, raw)],
            limit,
            [raw_v, wide_scratch, left_scratch],
            copies=2,
            micros=2,
        )
    return (predicted, sensitivity, weight_grad)


def solution(mesh):
    field = P(None, "gy", "gz", None)
    modes = P(None, "gy", "gz", None, None, None)
    return jax.shard_map(
        shards,
        mesh=mesh,
        in_specs=(field, field, modes, P(), P(), P(), P(), P()),
        out_specs=(field, field, modes),
        check_vma=False,
    )
```

```python
import math

import jax
import jax.numpy as jnp
import ml_dtypes
import numpy as np
from jax import lax
from jax.experimental import pallas as pl
from jax.experimental.pallas import tpu as pltpu
from jax.sharding import PartitionSpec as P

MX = 32
MY = 32
MZ = 8
CH = 32
BOTH = ("gy", "gz")

f32 = jnp.float32
bf16 = jnp.bfloat16
root_coef = math.sqrt(2.0 / math.pi)
NN = (((1,), (0,)), ((), ()))
NT = (((1,), (1,)), ((), ()))
TN = (((0,), (0,)), ((), ()))


def dot(a, b, form=NN):
    return lax.dot_general(a, b, form, preferred_element_type=f32)


def halves(value):
    high = value.astype(bf16)
    return high, (value - high.astype(f32)).astype(bf16)


def iota(shape, dim):
    return lax.broadcasted_iota(jnp.int32, shape, dim)


IN_VMEM = pl.BlockSpec(memory_space=pltpu.VMEM)
IN_HBM = pl.BlockSpec(memory_space=pltpu.HBM)


def struct(shape, kind=f32):
    return jax.ShapeDtypeStruct(shape, kind)


def run(kernel, ins, outs, limit, scratch=(), micros=1.0, copies=0, **grid):
    scratch = list(scratch)
    if copies:
        scratch.append(pltpu.SemaphoreType.DMA((copies,)))
    held = {id(IN_HBM): pltpu.HBM, id(IN_VMEM): pltpu.VMEM}

    def placed(spec, array):
        if id(spec) in held:
            return pltpu.with_memory_space_constraint(array, held[id(spec)])
        return array

    def shaped(spec, shape):
        if id(spec) in held:
            return held[id(spec)](shape.shape, shape.dtype)
        return shape

    return pl.pallas_call(
        kernel,
        in_specs=[spec for spec, _ in ins],
        out_specs=[spec for spec, _ in outs],
        out_shape=[shaped(spec, shape) for spec, shape in outs],
        scratch_shapes=scratch,
        compiler_params=pltpu.CompilerParams(vmem_limit_bytes=limit),
        cost_estimate=pl.CostEstimate(
            flops=int(micros * 1.1e9), bytes_accessed=1 << 16, transcendentals=0
        ),
        **grid,
    )(*[placed(spec, array) for spec, array in ins])


def begin(sem, first, *pairs):
    copies = [
        pltpu.make_async_copy(source, target, sem.at[first + i])
        for i, (source, target) in enumerate(pairs)
    ]
    for copy in copies:
        copy.start()
    return copies


def finish(*copies):
    for copy in copies:
        copy.wait()


def kept(count, length):
    position = np.arange(count)
    return np.where(position < count // 2, position, length - count + position)


def split_np(table):
    high = table.astype(ml_dtypes.bfloat16)
    return high, (table - high.astype(np.float64)).astype(ml_dtypes.bfloat16)


def x_tables(cells_x, blocks):
    local = MX // blocks
    freqs = kept(MX, cells_x).reshape(blocks, local).T
    angles = 2.0 * np.pi * ((freqs[:, :, None] * np.arange(cells_x)) % cells_x) / cells_x
    table = np.stack([np.cos(angles), -np.sin(angles)], axis=2).reshape(2 * MX, cells_x)
    return np.concatenate(split_np(table), axis=0)


def x_back_table(cells_x, gy, gz):
    local = MX // gy
    freqs = kept(MX, cells_x).reshape(gy, local).T
    angles = 2.0 * np.pi * ((freqs[:, :, None] * np.arange(cells_x)) % cells_x) / cells_x
    table = np.stack([np.cos(angles), -np.sin(angles)], axis=2)
    table = np.broadcast_to(table[:, :, None], (local, gy, gz, 2, cells_x))
    return np.concatenate(split_np(table.reshape(-1, cells_x)), axis=0)


def yz_angles(xp, freqs_y, gy, gz, rows_y, rows_z):
    span_y, span_z = gy * rows_y, gz * rows_z
    phase_y = (freqs_y[:, None] * xp.arange(span_y)[None]) % span_y
    phase_z = (xp.arange(MZ)[:, None] * xp.arange(span_z)[None]) % span_z
    phase_y = phase_y.reshape(-1, 1, gy, 1, rows_y, 1)
    phase_z = phase_z.reshape(1, MZ, 1, gz, 1, rows_z)
    turn = (phase_y * span_z + phase_z * span_y) % (span_y * span_z)
    return turn.reshape(turn.shape[0] * MZ, gy * gz, rows_y * rows_z)


def yz_table(xp, freqs_y, gy, gz, rows_y, rows_z):
    cells = gy * gz * rows_y * rows_z
    turn = yz_angles(xp, freqs_y, gy, gz, rows_y, rows_z)
    angles = 2.0 * math.pi / cells * turn
    cosine, sine = xp.cos(angles), xp.sin(angles)
    table = xp.stack([xp.stack([cosine, sine], 2), xp.stack([-sine, cosine], 2)], 0)
    return table.reshape(2 * turn.shape[0], -1)


def mode_tables(gy, gz, rows_y, rows_z, scale):
    local = MY // gz
    cells = gy * gz * rows_y * rows_z
    freqs = kept(MY, gy * rows_y).reshape(gz, local)
    if gz * 2 * local * MZ * 2 * cells <= 1 << 20:
        there, back = [], []
        for block in range(gz):
            high, low = split_np(scale * yz_table(np, freqs[block], gy, gz, rows_y, rows_z))
            there.append(np.concatenate([high, low], 0))
            back.append(np.concatenate([high.T, low.T], 1))
        return jnp.asarray(np.stack(there)), jnp.asarray(np.stack(back))
    where = lax.axis_index("gz")
    mine = lax.dynamic_index_in_dim(jnp.asarray(freqs, jnp.int32), where, keepdims=False)
    high, low = halves(scale * yz_table(jnp, mine, gy, gz, rows_y, rows_z).astype(f32))
    return jnp.concatenate([high, low], 0)[None], jnp.concatenate([high.T, low.T], 1)[None]


def put_x_modes(product, local, blocks, copies, cells, scratch, sent, send_ref, sem, first):
    rows = 2 * blocks
    half = blocks // 2
    moves = []
    for start in (0, half):
        at = 2 * start * cells
        for cell in range(cells):
            piece = product[:, cell * CH : (cell + 1) * CH]
            parts = [piece[k * rows + 2 * start : k * rows + 2 * start + blocks] for k in range(local)]
            scratch[pl.ds(at + cell, blocks, stride=cells), :] = jnp.concatenate(parts, axis=1)
        for block in range(start, start + half):
            value = scratch[block * 2 * cells : (block + 1) * 2 * cells].astype(bf16)
            for copy in range(copies):
                sent[block * copies + copy] = value
        part = pl.ds(start * copies, half * copies)
        moves += begin(sem, first + len(moves), (sent.at[part], send_ref.at[part]))
    return moves


def odd(axis):
    return lax.axis_index(axis) & 1


def first(axis):
    return lax.axis_index(axis) == 0


def last(axis):
    return lax.axis_index(axis) == lax.axis_size(axis) - 1


def arrive_kernel(raw_ref, table_ref, u_ref, one_ref, two_ref, my_table_ref, raw, sem):
    loads = begin(sem, 0, (raw_ref, raw), (table_ref, my_table_ref))
    finish(*loads)
    u = jnp.transpose(raw[...], (1, 2, 0, 3))
    u_ref[...] = u
    side = odd("gz")
    one_ref[...] = u_ref[:, pl.ds(1 - side, 3)]
    two_ref[...] = u_ref[:, pl.ds(side, 3)]


def spread_kernel(
    exact, local, blocks, copies, u_ref, table, *refs
):
    *refs, scratch, sent, sem = refs
    count = len(refs) // 2
    stores = begin(sem, 2, *zip(refs[:count], refs[count + 1 :]))
    send_ref = refs[count]
    cells = u_ref.shape[0] * u_ref.shape[1]
    u = u_ref[...].reshape(cells * CH, -1)
    if exact:
        both = dot(table[...], u, NT)
        product = both[: 2 * MX] + both[2 * MX :]
    else:
        high, low = halves(u)
        both = dot(table[...], high, NT)
        product = both[: 2 * MX] + both[2 * MX :] + dot(table[: 2 * MX], low, NT)
    moves = put_x_modes(product, local, blocks, copies, cells, scratch, sent, send_ref, sem, 0)
    finish(*moves, *stores)


def pick(tables_ref):
    if tables_ref.shape[0] == 1:
        return tables_ref.at[0]
    return tables_ref.at[lax.axis_index("gz")]


def mode_values(rec_ref, there, rows):
    both = dot(there[...], rec_ref[...].reshape(-1, rec_ref.shape[2]))
    return both[:rows] + both[rows:]


def put_back(values, back_ref, sent, send_ref, sem, first):
    high, low = halves(values)
    twice = jnp.concatenate([high, high], 0)
    rows = values.shape[0]
    devices, depth, wide = sent.shape
    part = devices // 8
    moves = []
    for step in range(8):
        at = slice(step * part * depth, (step + 1) * part * depth)
        result = dot(back_ref[at], twice) + dot(back_ref[at, :rows], low)
        sent[step * part : (step + 1) * part] = result.astype(bf16).reshape(part, depth, wide)
        span = pl.ds(step * part, part)
        moves += begin(sem, first + step, (sent.at[span], send_ref.at[span]))
    finish(*moves)


def kz_weight(shape):
    return jnp.where(iota(shape, 0) % MZ == 0, 1.0, 2.0).astype(f32)


def same_mode(rows, lanes):
    return (iota((rows, lanes), 0) % MZ) == ((iota((rows, lanes), 1) // CH) % MZ)


def mix_kernel(
    local,
    rec_ref,
    there_ref,
    high_ref,
    low_ref,
    back_ref,
    v_ref,
    kept_w_ref,
    send_ref,
    kept_v,
    sent,
    sem,
):
    store_w = begin(sem, 9, (high_ref, kept_w_ref))
    rows = there_ref.shape[0] // 2
    modes = rows // 2
    wide = local * CH
    v = mode_values(rec_ref, there_ref, rows)
    kept_v[...] = v
    store = begin(sem, 0, (kept_v, v_ref))
    real, imag = v[:modes], v[modes:]
    pair = (
        jnp.concatenate([real, -imag], 1),
        jnp.concatenate([imag, real], 1),
    )
    lane_k = (iota((MZ, 2 * wide), 1) // CH) % local
    size = MZ * CH
    diag = same_mode(2 * MZ * local, size)
    placed = [[[None] * (modes // MZ) for _ in range(local)] for _ in range(2)]
    for g in range(modes // MZ):
        pieces = []
        for k in range(local):
            for part in range(2):
                piece = pair[part][g * MZ : (g + 1) * MZ]
                pieces.append(jnp.where(lane_k == k, piece, 0.0))
        left_high, left_low = halves(jnp.concatenate(pieces, 0))
        w_high = high_ref[g]
        w_low = low_ref[g]
        count = left_high.shape[0]
        both = dot(jnp.concatenate([left_high, left_low], 0), w_high)
        value = both[:count] + both[count:] + dot(left_high, w_low)
        value = jnp.where(diag, value, 0.0)
        for k in range(local):
            for part in range(2):
                at = (2 * k + part) * MZ
                placed[part][k][g] = value[at : at + MZ]
    columns = [jnp.concatenate(placed[0][k] + placed[1][k], 0) for k in range(local)]
    all_values = jnp.concatenate(columns, 1)
    shape = (local * size, wide)
    fold = (iota(shape, 0) // size == iota(shape, 1) // CH) & (
        iota(shape, 0) % CH == iota(shape, 1) % CH
    )
    fold = fold.astype(bf16)
    high, low = halves(all_values)
    mixed = dot(high, fold) + dot(low, fold)
    put_back(mixed * kz_weight(mixed.shape), back_ref, sent, send_ref, sem, 1)
    finish(*store, *store_w)


def adjoint_kernel(
    local,
    rec_ref,
    there_ref,
    high_ref,
    back_ref,
    rep_ref,
    d_ref,
    send_ref,
    sent,
    sem,
):
    rows = there_ref.shape[0] // 2
    modes = rows // 2
    wide = local * CH
    size = MZ * CH
    d = mode_values(rec_ref, there_ref, rows)
    d = d * kz_weight(d.shape)
    d_ref[...] = d
    high, low = halves(d)
    spread = dot(high, rep_ref[...]) + dot(low, rep_ref[...])
    spread = jnp.where(same_mode(rows, local * size), spread, 0.0)
    lane_k = (iota((2 * MZ, 2 * wide), 1) // CH) % local
    parts = ([], [])
    for g in range(modes // MZ):
        pieces = []
        for k in range(local):
            for part in range(2):
                at = part * modes + g * MZ
                pieces.append(spread[at : at + MZ, k * size : (k + 1) * size])
        left_high, left_low = halves(jnp.concatenate(pieces, 0))
        count = left_high.shape[0]
        both = dot(
            jnp.concatenate([left_high, left_low], 0), high_ref[g * size : (g + 1) * size]
        )
        value = both[:count] + both[count:]
        total = None
        for k in range(local):
            piece = jnp.where(lane_k == k, value[2 * k * MZ : 2 * (k + 1) * MZ], 0.0)
            total = piece if total is None else total + piece
        parts[0].append(total[:MZ])
        parts[1].append(total[MZ:])
    real = jnp.concatenate(parts[0], 0)
    imag = jnp.concatenate(parts[1], 0)
    value = jnp.concatenate(
        [real[:, :wide] + imag[:, wide:], imag[:, :wide] - real[:, wide:]], 0
    )
    put_back(value, back_ref, sent, send_ref, sem, 0)


def setup_kernel(
    local,
    w_ref,
    there_ref,
    back_ref,
    high_ref,
    low_ref,
    my_there_ref,
    my_back_ref,
    w,
    sem,
):
    parts = high_ref.shape[0]
    rows = w.shape[2] // parts
    spans = [pl.ds(step * rows, rows) for step in range(parts)]
    loads = begin(sem, 0, *[(w_ref.at[:, :, span], w.at[:, :, span]) for span in spans])
    tables = begin(
        sem, parts, (pick(there_ref), my_there_ref), (pick(back_ref), my_back_ref)
    )
    for step in range(parts):
        at = slice(step * rows, (step + 1) * rows)
        finish(loads[step])
        pieces = [w[part, k, at] for part in range(2) for k in range(local)]
        high_ref[step], low_ref[step] = halves(jnp.concatenate(pieces, 1).T)
    finish(*tables)


def put_weight_grad(d_ref, v_ref, out, out_ref, sem, first):
    rows, wide = d_ref.shape
    modes = rows // 2
    size = MZ * CH
    keep = same_mode(rows, size)
    d_halves = halves(d_ref[...])
    v_halves = halves(v_ref[...])
    stores = []
    for k in range(wide // CH):
        shape = (wide, size)
        rep = (iota(shape, 0) == k * CH + iota(shape, 1) % CH).astype(bf16)
        d_high, d_low = [jnp.where(keep, dot(value, rep), 0.0) for value in d_halves]
        at = slice(k * CH, (k + 1) * CH)
        v_high, v_low = [value[:, at].astype(f32) for value in v_halves]
        for g in range(modes // MZ):
            real = slice(g * MZ, (g + 1) * MZ)
            imag = slice(modes + g * MZ, modes + (g + 1) * MZ)
            left = jnp.concatenate(
                [d_high[real], d_high[imag], d_low[real], d_low[imag], d_high[real], d_high[imag]],
                0,
            ).astype(bf16)
            for part in range(2):
                rights = []
                for v in (v_high, v_high, v_low):
                    rights += [v[real], v[imag]] if part == 0 else [-v[imag], v[real]]
                right = jnp.concatenate(rights, 0).astype(bf16)
                out[part, k, g * size : (g + 1) * size, :] = dot(left, right, TN)
        stores += begin(sem, first + k, (out.at[:, k], out_ref.at[:, k]))
    return stores


def widen(rec_ref, wide):
    wide[...] = rec_ref[...].reshape(-1, rec_ref.shape[2]).astype(f32)


def inverse_x(wide, table, local, cells, part, left):
    rows = wide.shape[0] // cells
    for cell in part:
        turned = wide[pl.ds(cell, rows, stride=cells), :].T.astype(bf16)
        for k in range(local):
            left[cell * CH : (cell + 1) * CH, k * rows : (k + 1) * rows] = turned[
                k * CH : (k + 1) * CH
            ]
    depth = local * rows
    value = left[part.start * CH : part.stop * CH]
    return dot(value, table[:depth]) + dot(value, table[depth:])


def gelu_pair(pre_act):
    cube_term = pre_act * pre_act * pre_act
    tanh_result = jnp.tanh(root_coef * (pre_act + 0.044715 * cube_term))
    activated_output = 0.5 * pre_act * (1.0 + tanh_result)
    gelu_slope = 0.5 * (1.0 + tanh_result) + 0.5 * pre_act * (
        1.0 - tanh_result * tanh_result
    ) * root_coef * (1.0 + 3.0 * 0.044715 * pre_act * pre_act)
    return (activated_output, gelu_slope)


def middle_kernel(
    local,
    rec_ref,
    back_ref,
    base_ref,
    cot_ref,
    coarse_ref,
    out_ref,
    grad_ref,
    rounded,
    one_ref,
    two_ref,
    wide,
    left,
):
    rows_y, rows_z, _, span = base_ref.shape
    cells = rows_y * rows_z
    widen(rec_ref, wide)
    pre_act = inverse_x(wide, back_ref, local, cells, range(cells), left)
    pre_act = pre_act + base_ref[...].reshape(pre_act.shape)
    activated, slope = gelu_pair(pre_act)
    out_ref[...] = activated.astype(bf16).reshape(out_ref.shape)
    value = cot_ref[...].astype(f32).reshape(pre_act.shape) * slope
    grad_ref[...] = value.reshape(grad_ref.shape)
    rounded[:cells] = value.astype(bf16).reshape(cells, CH, span)
    side = odd("gz")
    for y in range(rows_y):
        one_ref[y] = rounded[rows_z * y + (rows_z - 1) * (1 - side)]
        two_ref[y] = rounded[rows_z * y + (rows_z - 1) * side]
    pool = pool_matrix(span)
    for yc in range(2):
        sums = []
        for zc in range(2):
            y, z = 2 * yc, 2 * zc
            sums.append(
                grad_ref[y, z] + grad_ref[y, z + 1] + grad_ref[y + 1, z] + grad_ref[y + 1, z + 1]
            )
        total_high, total_low = halves(jnp.concatenate(sums, 0))
        total = dot(total_high, pool) + dot(total_low, pool)
        pieces = []
        for zc in range(2):
            piece = total[zc * CH : (zc + 1) * CH]
            pieces.append(jnp.where(coarse_ref[yc, zc].astype(f32) > 0, piece, 0.0))
        piece = jnp.concatenate(pieces, 1).astype(bf16)
        rounded[cells + yc] = piece
        one_ref[rows_y + yc] = piece
        two_ref[rows_y + yc] = piece


def last_kernel(local, rec_ref, back_ref, base_ref, out_ref, out, wide, left, sem):
    rows_y, rows_z, _, span = base_ref.shape
    cells = rows_y * rows_z
    widen(rec_ref, wide)
    moves = []
    for y in range(0, rows_y, 2):
        part = range(y * rows_z, (y + 2) * rows_z)
        value = inverse_x(wide, back_ref, local, cells, part, left)
        value = value.reshape(2, rows_z, CH, span) + base_ref[y : y + 2]
        out[:, y : y + 2] = jnp.transpose(value.astype(bf16), (2, 0, 1, 3))
        at = pl.ds(y, 2)
        moves += begin(sem, y // 2, (out.at[:, at], out_ref.at[:, at]))
    finish(*moves)


def turn_kernel(
    value_ref,
    there_ref,
    w_ref,
    back_ref,
    out_ref,
    my_there_ref,
    my_w_ref,
    my_back_ref,
    rep_ref,
    value,
    out,
    packed,
    sem,
):
    loads = begin(
        sem,
        0,
        (value_ref, value),
        (pick(there_ref), my_there_ref),
        (w_ref, packed),
        (pick(back_ref), my_back_ref),
    )
    shape = rep_ref.shape
    size = MZ * CH
    rep = (iota(shape, 1) // size == iota(shape, 0) // CH) & (
        iota(shape, 1) % CH == iota(shape, 0) % CH
    )
    rep_ref[...] = rep.astype(bf16)
    finish(loads[0])
    out[...] = jnp.transpose(value[...], (2, 0, 1, 3))
    store = begin(sem, 4, (out, out_ref))
    finish(*loads[1:])
    for g in range(packed.shape[0]):
        my_w_ref[g * size : (g + 1) * size] = packed[g].astype(f32).T.astype(bf16)
    finish(*store)


def write_bands(adjoint, k_ref, out, index):
    for a in range(3):
        for e in range(3):
            taps = []
            for b in range(3):
                if adjoint:
                    tap = k_ref[9 * (2 - a) + 3 * (2 - b) + 2 - e].astype(f32).T
                else:
                    tap = k_ref[9 * a + 3 * b + e].astype(f32)
                taps.append(tap)
            taps = jnp.concatenate(taps, 1)
            for z in range(4):
                pieces = [taps, jnp.zeros((CH, (5 - z) * CH), f32)]
                if z > 0:
                    pieces.insert(0, jnp.zeros((CH, z * CH), f32))
                row = jnp.concatenate(pieces, 1)
                at = (e * 4 + z) * CH
                out[index, at : at + CH, a * 8 * CH : (a + 1) * 8 * CH] = row.astype(bf16)


def x_sum(low, same, high):
    span = same.shape[1]
    lane = iota(same.shape, 1)
    before = jnp.where(lane == 0, 0.0, pltpu.roll(low, 1, axis=1))
    after = jnp.where(lane == span - 1, 0.0, pltpu.roll(high, span - 1, axis=1))
    return same + before + after


def band_conv(bands, planes):
    value = dot(bands, jnp.concatenate(planes, 0))
    size = 4 * CH
    return x_sum(value[:size], value[size : 2 * size], value[2 * size :])


def column(row_ref, copies):
    eye = iota((CH, CH), 0) == iota((CH, CH), 1)
    value = jnp.sum(jnp.where(eye, row_ref[...], 0.0), axis=1, keepdims=True)
    return jnp.concatenate([value] * copies, 0)


def block_diagonal(matrix):
    shape = (4 * CH, 4 * CH)
    wide = jnp.concatenate([matrix.astype(f32)] * 4, 1)
    tiled = jnp.concatenate([wide] * 4, 0)
    return jnp.where(iota(shape, 0) // CH == iota(shape, 1) // CH, tiled, 0.0).astype(bf16)


def pool_matrix(span):
    shape = (span, span // 2)
    return (iota(shape, 0) // 2 == iota(shape, 1)).astype(bf16)


def up_matrix(span):
    shape = (span // 2, span)
    return (iota(shape, 1) // 2 == iota(shape, 0)).astype(bf16)


def y_message_kernel(u_ref, z_one_ref, z_two_ref, one_ref, two_ref, rows, sem):
    side = odd("gz")
    for y in range(4):
        for z in range(3):
            at = pl.multiple_of((7 * (1 - side) + z) * CH, CH)
            rows[y, pl.ds(at, CH)] = z_one_ref[y, z]
            at = pl.multiple_of((7 * side + z) * CH, CH)
            rows[y, pl.ds(at, CH)] = z_two_ref[y, z]
        for z in range(4):
            rows[y, (z + 3) * CH : (z + 4) * CH] = u_ref[y, z]
    blank = jnp.zeros((4, 3 * CH, rows.shape[2]), bf16)

    @pl.when(first("gz"))
    def low_end():
        rows[:, : 3 * CH] = blank

    @pl.when(last("gz"))
    def high_end():
        rows[:, 7 * CH :] = blank

    side = odd("gy")
    finish(
        *begin(
            sem, 0, (rows.at[pl.ds(1 - side, 3)], one_ref), (rows.at[pl.ds(side, 3)], two_ref)
        )
    )


def forward_conv_kernel(
    own_one_ref,
    own_two_ref,
    y_one_ref,
    y_two_ref,
    lin_ref,
    taps_fine_ref,
    taps_coarse_ref,
    bias_fine_ref,
    bias_coarse_ref,
    cot_ref,
    table_ref,
    x_ref,
    base,
    fine_ref,
    coarse,
    my_cot_ref,
    my_table_ref,
    my_x_ref,
    grid,
    taps_fine,
    taps_coarse,
    raw,
    bands,
    pooled,
    fine,
    sem,
):
    span = grid.shape[2]
    inner = pl.ds(0, 10 * CH)
    side = odd("gy")
    loads = begin(
        sem,
        0,
        (taps_fine_ref, taps_fine),
        (own_one_ref, grid.at[pl.ds(4 - side, 3), inner]),
        (own_two_ref.at[pl.ds(2 * side, 1)], grid.at[pl.ds(3 + 3 * side, 1), inner]),
        (y_one_ref, grid.at[pl.ds(7 * (1 - side), 3), inner]),
        (y_two_ref, grid.at[pl.ds(7 * side, 3), inner]),
        (taps_coarse_ref, taps_coarse),
        (cot_ref, raw),
        (table_ref, my_table_ref),
        (x_ref, my_x_ref),
    )
    edges = [jnp.logical_not(end(axis)) for axis in ("gy", "gz") for end in (first, last)]
    grid[:, 10 * CH :, :] = jnp.zeros((10, 2 * CH, span), bf16)
    pooled[:, 4 * CH :, :] = jnp.zeros((4, 4 * CH, span // 2), bf16)
    bias = column(bias_fine_ref, 4)
    half = 4 * CH
    row_z = iota((half, span), 0) // CH
    finish(loads[0])
    write_bands(False, taps_fine, bands, 0)
    finish(*loads[1:3])
    for y in (3, 4, 2, 1, 0, 5, 6, 7):
        if y == 2:
            finish(loads[3], loads[4])

            @pl.when(first("gy"))
            def low_end():
                grid[:3] = jnp.zeros((3, 12 * CH, span), bf16)

            @pl.when(last("gy"))
            def high_end():
                grid[7:] = jnp.zeros((3, 12 * CH, span), bf16)

        y_in = None
        if y < 2:
            y_in = edges[0]
        elif y >= 6:
            y_in = edges[1]
        for h in range(2):
            at = h * half
            value = band_conv(bands[0], [grid[y + a, at : at + 8 * CH, :] for a in range(3)])
            value = jnp.maximum(value + bias, 0.0)
            inside = (row_z >= 2) | edges[2] if h == 0 else (row_z < 2) | edges[3]
            if y_in is not None:
                inside = inside & y_in
            fine[y, at : at + half, :] = jnp.where(inside, value, 0.0).astype(bf16)
    (store,) = begin(sem, 9, (fine, fine_ref))
    sums = []
    for yc in range(4):
        both = fine[2 * yc].astype(f32) + fine[2 * yc + 1].astype(f32)
        for zc in range(4):
            at = 2 * zc * CH
            sums.append(both[at : at + CH] + both[at + CH : at + 2 * CH])
    pool = pool_matrix(span)
    high, low = halves(jnp.concatenate(sums, 0))
    pools = (0.125 * (dot(high, pool) + dot(low, pool))).astype(bf16)
    pooled[:, : 4 * CH, :] = pools.reshape(4, 4 * CH, span // 2)
    bias = column(bias_coarse_ref, 4)
    finish(loads[5])
    write_bands(False, taps_coarse, bands, 1)
    planes = [jnp.concatenate([pooled[a], pooled[a + 1]], 1) for a in range(3)]
    value = dot(bands[1], jnp.concatenate(planes, 0))
    parts = [value[e * half : (e + 1) * half] for e in range(3)]
    for yc in range(2):
        at = slice(yc * span // 2, (yc + 1) * span // 2)
        value = x_sum(*[part[:, at] for part in parts])
        value = jnp.maximum(value + bias, 0.0).astype(bf16)
        coarse[yc] = value[: 2 * CH].reshape(2, CH, span // 2)
    lifted = dot(coarse[...].reshape(half, span // 2), up_matrix(span))
    lin = block_diagonal(lin_ref[...])
    for y in range(4):
        total = dot(lin, grid[y + 3, 3 * CH : 7 * CH, :])
        total = total + fine[y + 2, 2 * CH : 6 * CH, :].astype(f32)
        for z in range(4):
            at = (y // 2 * 2 + z // 2) * CH
            base[y, z] = total[z * CH : (z + 1) * CH] + lifted[at : at + CH]
    finish(loads[6])
    my_cot_ref[...] = jnp.transpose(raw[...], (1, 2, 0, 3))
    finish(store, *loads[7:])


def y_gradient_kernel(
    round_ref, z_one_ref, z_two_ref, kept_ref, one_ref, two_ref, own, halo, sem
):
    (load,) = begin(sem, 0, (round_ref, own))
    side = odd("gz")
    halo[1 - side] = z_one_ref[...]
    halo[side] = z_two_ref[...]

    @pl.when(first("gz"))
    def low_end():
        halo[0] = jnp.zeros(halo.shape[1:], bf16)

    @pl.when(last("gz"))
    def high_end():
        halo[1] = jnp.zeros(halo.shape[1:], bf16)

    (store,) = begin(sem, 1, (halo, kept_ref))
    finish(load)
    side = odd("gy")
    for out_ref, y in ((one_ref, 3 * (1 - side)), (two_ref, 3 * side)):
        out_ref[0] = halo[0, y]
        out_ref[1:5] = own[pl.ds(4 * y, 4)]
        out_ref[5] = halo[1, y]
        for yc in range(2):
            out_ref[6 + 3 * yc] = halo[0, 4 + yc]
            out_ref[7 + 3 * yc] = own[16 + yc]
            out_ref[8 + 3 * yc] = halo[1, 4 + yc]
    finish(store)


def backward_kernel(
    d_ref,
    v_ref,
    grad_ref,
    round_ref,
    kept_ref,
    y_one_ref,
    y_two_ref,
    fine_ref,
    lin_ref,
    taps_fine_ref,
    taps_coarse_ref,
    table_ref,
    weight_ref,
    base,
    my_table_ref,
    weights,
    grad,
    rounded,
    kept,
    beside,
    fine,
    taps_fine,
    taps_coarse,
    bands,
    coarse_grid,
    fine_grid,
    sem,
):
    side = odd("gy")
    loads = begin(
        sem,
        0,
        (taps_coarse_ref, taps_coarse),
        (round_ref, rounded),
        (kept_ref, kept),
        (y_one_ref, beside.at[1 - side]),
        (y_two_ref, beside.at[side]),
        (grad_ref, grad),
        (fine_ref, fine),
        (taps_fine_ref, taps_fine),
        (table_ref, my_table_ref),
    )
    stores = put_weight_grad(d_ref, v_ref, weights, weight_ref, sem, 9)
    finish(loads[0], loads[7])
    write_bands(True, taps_coarse, bands, 1)
    write_bands(True, taps_fine, bands, 0)
    span = grad.shape[3]
    half = span // 2
    coarse_grid[:, 6 * CH :, :] = jnp.zeros((6, 2 * CH, half), bf16)
    fine_grid[:, 6 * CH :, :] = jnp.zeros((6, 2 * CH, span), bf16)

    def place(yc, pair, value):
        for zc in range(2):
            at = (2 * pair + zc) * CH
            coarse_grid[yc, at : at + CH, :] = value[:, zc * half : (zc + 1) * half]

    finish(*loads[1:5])

    @pl.when(first("gy"))
    def low_end():
        beside[0] = jnp.zeros(beside.shape[1:], bf16)

    @pl.when(last("gy"))
    def high_end():
        beside[1] = jnp.zeros(beside.shape[1:], bf16)

    for yc in range(2):
        place(2 + yc, 0, kept[0, 4 + yc])
        place(2 + yc, 1, rounded[16 + yc])
        place(2 + yc, 2, kept[1, 4 + yc])
        for pair in range(3):
            place(yc, pair, beside[0, 6 + 3 * yc + pair])
            place(4 + yc, pair, beside[1, 6 + 3 * yc + pair])
    pooled = [
        0.125 * band_conv(bands[1], [coarse_grid[yc + a] for a in range(3)]) for yc in range(4)
    ]
    high, low = halves(jnp.concatenate(pooled, 0))
    up = up_matrix(span)
    lifted = dot(high, up) + dot(low, up)
    finish(*loads[5:7])
    for y in range(6):
        yc = (y + 1) // 2
        for z in range(6):
            at = (4 * yc + (z + 1) // 2) * CH
            if 1 <= y <= 4 and 1 <= z <= 4:
                value = grad[y - 1, z - 1]
            elif 1 <= y <= 4:
                value = kept[z // 5, y - 1].astype(f32)
            else:
                value = beside[y // 5, z].astype(f32)
            value = value + lifted[at : at + CH]
            mask = fine[y + 1, (z + 1) * CH : (z + 2) * CH, :].astype(f32) > 0
            fine_grid[y, z * CH : (z + 1) * CH, :] = jnp.where(mask, value, 0.0).astype(bf16)
    lin = block_diagonal(lin_ref[...].astype(f32).T.astype(bf16))
    for y in range(4):
        value = band_conv(bands[0], [fine_grid[y + a] for a in range(3)])
        value = value + dot(lin, rounded[4 * y : 4 * y + 4].reshape(4 * CH, span))
        base[y] = value.reshape(4, CH, span)
    finish(loads[8], *stores)


def swaps(blocks, axis):
    size_y, size_z = lax.axis_size("gy"), lax.axis_size("gz")
    results = []
    for start, block in enumerate(blocks):
        pairs = []
        for y in range(size_y):
            for z in range(size_z):
                step = 1 if ((y if axis == "gy" else z) - start) % 2 == 0 else -1
                to_y, to_z = y, z
                if axis == "gy":
                    to_y = (y + step) % size_y
                elif 0 <= z + step < size_z:
                    to_z = z + step
                else:
                    to_y = y ^ 1
                pairs.append((y * size_z + z, to_y * size_z + to_z))
        results.append(lax.ppermute(block, BOTH, pairs))
    return results


def exchange(block):
    return lax.all_to_all(block, BOTH, split_axis=0, concat_axis=0, tiled=True)


def shards(
    carbon_input_volume,
    cotangent,
    spec_weight,
    lin_weight,
    conv_fine,
    bias_fine,
    conv_coarse,
    bias_coarse,
):
    channels, rows_y, rows_z, span = carbon_input_volume.shape
    gy, gz = lax.axis_size("gy"), lax.axis_size("gz")
    devices = gy * gz
    cells = rows_y * rows_z
    local = MX // gy
    modes = (MY // gz) * MZ
    wide = local * CH
    scale = 1.0 / math.sqrt(span * cells * devices)
    there, back = mode_tables(gy, gz, rows_y, rows_z, scale)
    forward_x = jnp.asarray(x_tables(span, gy))
    inverse_table = jnp.asarray(x_back_table(span, gy, gz))

    limit = (14 << 20) + devices * (64 << 10)
    chunk = struct((devices, 2 * cells, wide), bf16)
    sent = pltpu.VMEM(chunk.shape, bf16)
    field = struct((rows_y, rows_z, CH, span))
    field_v = pltpu.VMEM(field.shape, f32)
    round_field = struct(field.shape, bf16)
    round_v = pltpu.VMEM(field.shape, bf16)
    raw = struct(carbon_input_volume.shape, bf16)
    raw_v = pltpu.VMEM(raw.shape, bf16)
    taps_v = pltpu.VMEM(conv_fine.shape, bf16)
    x_scratch = pltpu.VMEM((2 * gy * cells, wide), f32)
    wide_scratch = pltpu.VMEM((devices * 2 * cells, wide), f32)
    left_scratch = pltpu.VMEM((cells * CH, local * devices * 2), bf16)
    mode_field = struct((2 * modes, wide))
    mode_v = pltpu.VMEM(mode_field.shape, f32)
    rows = modes * CH
    packed = struct((modes // MZ, 2 * wide, MZ * CH), bf16)
    unpacked = struct((rows, 2 * wide), bf16)
    bands_v = pltpu.VMEM((2, 12 * CH, 24 * CH), bf16)
    side = struct((rows_y, 3, CH, span), bf16)
    message = struct((6, CH, span), bf16)
    y_side = struct((3, 10 * CH, span), bf16)
    y_message = struct((12, CH, span), bf16)

    with jax.named_scope("arrive"):
        u, one, two, my_x = run(
            arrive_kernel,
            [(IN_HBM, carbon_input_volume), (IN_HBM, forward_x)],
            [
                (IN_VMEM, round_field),
                (IN_VMEM, side),
                (IN_VMEM, side),
                (IN_VMEM, struct(forward_x.shape, bf16)),
            ],
            limit,
            [raw_v],
            copies=2,
        )
    one, two = swaps((one, two), "gz")

    def spread(values, table, exact, *others):
        with jax.named_scope("spread"):
            return run(
                lambda *refs: spread_kernel(exact, local, gy, gz, *refs),
                [(IN_VMEM, array) for array in (values, table) + others],
                [(IN_HBM, chunk)] + [(IN_HBM, struct(x.shape, x.dtype)) for x in others],
                limit,
                [x_scratch, sent],
                copies=2 + len(others),
                micros=1.2,
            )

    received = exchange(spread(u, my_x, True)[0])

    with jax.named_scope("y_message"):
        own_one, own_two = run(
            y_message_kernel,
            [(IN_VMEM, u), (IN_VMEM, one), (IN_VMEM, two)],
            [(IN_HBM, y_side), (IN_HBM, y_side)],
            limit,
            [pltpu.VMEM((rows_y, 10 * CH, span), bf16)],
            copies=2,
        )
    one, two = swaps((own_one, own_two), "gy")

    with jax.named_scope("setup"):
        w_high, w_low, my_there, my_back = run(
            lambda *refs: setup_kernel(local, *refs),
            [
                (IN_HBM, spec_weight.reshape(2, local, rows, CH)),
                (IN_HBM, there),
                (IN_HBM, back),
            ],
            [
                (IN_VMEM, packed),
                (IN_VMEM, packed),
                (IN_VMEM, struct(there.shape[1:], bf16)),
                (IN_VMEM, struct(back.shape[1:], bf16)),
            ],
            limit + (10 << 20),
            [pltpu.VMEM((2, local, rows, CH), f32)],
            copies=10,
            micros=4.5,
        )

    with jax.named_scope("mix"):
        v, w_kept, send = run(
            lambda *refs: mix_kernel(local, *refs),
            [
                (IN_VMEM, received),
                (IN_VMEM, my_there),
                (IN_VMEM, w_high),
                (IN_VMEM, w_low),
                (IN_VMEM, my_back),
            ],
            [(IN_HBM, mode_field), (IN_HBM, packed), (IN_HBM, chunk)],
            limit,
            [mode_v, sent],
            copies=10,
            micros=3,
        )
    received = exchange(send)

    with jax.named_scope("forward_convs"):
        base, fine, coarse, cot, my_inverse, my_x = run(
            forward_conv_kernel,
            [
                (IN_HBM, own_one),
                (IN_HBM, own_two),
                (IN_HBM, one),
                (IN_HBM, two),
                (IN_VMEM, lin_weight),
                (IN_HBM, conv_fine),
                (IN_HBM, conv_coarse),
                (IN_VMEM, bias_fine[None]),
                (IN_VMEM, bias_coarse[None]),
                (IN_HBM, cotangent),
                (IN_HBM, inverse_table),
                (IN_HBM, forward_x),
            ],
            [
                (IN_VMEM, field),
                (IN_HBM, struct((8, 8 * CH, span), bf16)),
                (IN_VMEM, struct((2, 2, CH, span // 2), bf16)),
                (IN_VMEM, round_field),
                (IN_VMEM, struct(inverse_table.shape, bf16)),
                (IN_VMEM, struct(forward_x.shape, bf16)),
            ],
            limit,
            [
                pltpu.VMEM((10, 12 * CH, span), bf16),
                taps_v,
                taps_v,
                raw_v,
                bands_v,
                pltpu.VMEM((4, 8 * CH, span // 2), bf16),
                pltpu.VMEM((8, 8 * CH, span), bf16),
            ],
            copies=10,
            micros=7,
        )

    with jax.named_scope("middle"):
        activated, grad, grad_round, one, two = run(
            lambda *refs: middle_kernel(local, *refs),
            [
                (IN_VMEM, received),
                (IN_VMEM, my_inverse),
                (IN_VMEM, base),
                (IN_VMEM, cot),
                (IN_VMEM, coarse),
            ],
            [
                (IN_VMEM, round_field),
                (IN_VMEM, field),
                (IN_VMEM, struct((cells + 2, CH, span), bf16)),
                (IN_VMEM, message),
                (IN_VMEM, message),
            ],
            limit,
            [wide_scratch, left_scratch],
            micros=2,
        )
    one, two = swaps((one, two), "gz")
    send, grad, activated, grad_round = spread(grad, my_x, False, grad, activated, grad_round)
    received = exchange(send)

    with jax.named_scope("y_gradient"):
        kept_z, one, two = run(
            y_gradient_kernel,
            [(IN_HBM, grad_round), (IN_VMEM, one), (IN_VMEM, two)],
            [
                (IN_HBM, struct((2,) + message.shape, bf16)),
                (IN_VMEM, y_message),
                (IN_VMEM, y_message),
            ],
            limit,
            [
                pltpu.VMEM((cells + 2, CH, span), bf16),
                pltpu.VMEM((2,) + message.shape, bf16),
            ],
            copies=2,
            micros=20,
        )
    one, two = swaps((one, two), "gy")
    with jax.named_scope("turn"):
        predicted, my_there, my_w, my_back, rep = run(
            turn_kernel,
            [
                (IN_HBM, activated),
                (IN_HBM, there),
                (IN_HBM, w_kept),
                (IN_HBM, back),
            ],
            [
                (IN_HBM, raw),
                (IN_VMEM, struct(there.shape[1:], bf16)),
                (IN_VMEM, unpacked),
                (IN_VMEM, struct(back.shape[1:], bf16)),
                (IN_VMEM, struct((wide, local * MZ * CH), bf16)),
            ],
            limit,
            [round_v, raw_v, pltpu.VMEM(packed.shape, bf16)],
            copies=5,
            micros=2,
        )

    with jax.named_scope("mix_adjoint"):
        d, send = run(
            lambda *refs: adjoint_kernel(local, *refs),
            [(IN_VMEM, array) for array in (received, my_there, my_w, my_back, rep)],
            [(IN_VMEM, mode_field), (IN_HBM, chunk)],
            limit,
            [sent],
            copies=8,
            micros=2,
        )
    received = exchange(send)

    with jax.named_scope("backward"):
        weight_grad, base, my_inverse = run(
            backward_kernel,
            [
                (IN_VMEM, d),
                (IN_VMEM, v),
                (IN_HBM, grad),
                (IN_HBM, grad_round),
                (IN_HBM, kept_z),
                (IN_HBM, one),
                (IN_HBM, two),
                (IN_HBM, fine),
                (IN_VMEM, lin_weight),
                (IN_HBM, conv_fine),
                (IN_HBM, conv_coarse),
                (IN_HBM, inverse_table),
            ],
            [
                (IN_HBM, struct((2, local, rows, CH))),
                (IN_VMEM, field),
                (IN_VMEM, struct(inverse_table.shape, bf16)),
            ],
            limit + (10 << 20),
            [
                pltpu.VMEM((2, local, rows, CH), f32),
                field_v,
                pltpu.VMEM((cells + 2, CH, span), bf16),
                pltpu.VMEM((2,) + message.shape, bf16),
                pltpu.VMEM((2,) + y_message.shape, bf16),
                pltpu.VMEM((8, 8 * CH, span), bf16),
                taps_v,
                taps_v,
                bands_v,
                pltpu.VMEM((6, 8 * CH, span // 2), bf16),
                pltpu.VMEM((6, 8 * CH, span), bf16),
            ],
            copies=9 + local,
            micros=6,
        )
    weight_grad = weight_grad.reshape(spec_weight.shape)

    with jax.named_scope("last"):
        (sensitivity,) = run(
            lambda *refs: last_kernel(local, *refs),
            [(IN_VMEM, received), (IN_VMEM, my_inverse), (IN_VMEM, base)],
            [(IN_HBM, raw)],
            limit,
            [raw_v, wide_scratch, left_scratch],
            copies=2,
            micros=2,
        )
    return (predicted, sensitivity, weight_grad)


def solution(mesh):
    field = P(None, "gy", "gz", None)
    modes = P(None, "gy", "gz", None, None, None)
    return jax.shard_map(
        shards,
        mesh=mesh,
        in_specs=(field, field, modes, P(), P(), P(), P(), P()),
        out_specs=(field, field, modes),
        check_vma=False,
    )
```
